128 devices in a mesh: rep: 16 (over y, z_lo, core), shard: 8 (over x, z_hi).
Axes of the slice: x: 4, y: 4, z: 4 (z_hi: 2, z_lo: 2; z = z_hi * 2 + z_lo), core: 2. Of those that a mesh axis runs over, the one named last changes fastest.
Arguments:
- features: bfloat16 [128, 28, 28, 704], P(('rep', 'shard')), may hold values from -6 to 6
- cotangent: bfloat16 [128, 28, 28, 704], P(('rep', 'shard')), may hold values from -6 to 6
- dw_kernel: float32 [49, 704], replicated, may hold values from -0.875 to 0.875
- norm_gain: float32 [704], replicated, may hold values from 0.1 to 1.9
- w_expand: bfloat16 [2816, 704], P('shard'), may hold values from -1 to 1
- grn_gamma: float32 [2816], replicated, may hold values from -3 to 3
- grn_beta: float32 [2816], replicated, may hold values from -3 to 3
- w_reduce: bfloat16 [2816, 704], P('shard'), may hold values from -0.109375 to 0.109375
Outputs:
- block_out: bfloat16 [128, 28, 28, 704], P(('rep', 'shard'))
- grad_features: bfloat16 [128, 28, 28, 704], P(('rep', 'shard'))
- grad_kernel: float32 [49, 704], replicated
- grad_gain: float32 [704], replicated
- grad_expand: float32 [2816, 704], P('shard')
- grad_gamma: float32 [2816], replicated
- grad_beta: float32 [2816], replicated
- grad_reduce: float32 [2816, 704], P('shard')
The draws below stay inside these ranges and needn't reach their ends.
All inputs are finite; a program needn't handle non-finite values.
Results may differ from the reference program's by a relative error of at most 0.02.
Values may be sent and summed in bfloat16 or wider, within the bound.
No kernel may reach another device: no remote copies, remote signals or barrier semaphores. Data moves between devices by JAX's collectives and lax.ppermute only.
A program may use at most 320 MiB of HBM per device.

```python
import math
import jax
import jax.numpy as jnp
from jax import lax

C = 704
H = 2816
SIDE = 28
IMG_DEV = 1
IMAGES = 128
N_REP = 16
N_SHARD = 8


def draw_w_expand(key, part):
    first_key, second_key = jax.random.split(jax.random.fold_in(key, 11))
    row_scale = jnp.exp(jax.random.uniform(second_key, (H, 1), jnp.float32, math.log(0.3), math.log(3.0)))
    base = jax.random.normal(first_key, (H, C), jnp.float32)
    scaled = jnp.clip(base * row_scale * C ** (-0.5), -1.0, 1.0)
    return scaled.astype(jnp.bfloat16)


def block_levels(key, dims, cuts, low, high):
    def one(axis_at, shards_of):
        heights = jax.random.uniform(jax.random.fold_in(jax.random.fold_in(key, 6), axis_at), (shards_of,), jnp.float32, low / len(cuts), high / len(cuts))
        return jnp.repeat(jnp.exp(heights), dims[axis_at] // shards_of).reshape((-1,) + (1,) * (len(dims) - axis_at - 1))

    gain = one(*cuts[0])
    for cut in cuts[1:]:
        gain = gain * one(*cut)
    return gain


def normal_values(own_key, dims, scale, limit, cuts=(), held_as=jnp.bfloat16):
    entries = scale * jax.random.normal(own_key, dims, jnp.float32)
    if cuts:
        entries = entries * block_levels(own_key, dims, cuts, -0.22, 0.18)
    return jnp.clip(entries, -limit, limit).astype(held_as)


def setup_inputs(seed: int = 0) -> dict:
    key_list = jax.random.split(jax.random.key(seed), 9)
    features = normal_values(key_list[0], (IMAGES, SIDE, SIDE, C), 1.0, 6.0, ((0, 128),))
    cotangent = normal_values(key_list[1], (IMAGES, SIDE, SIDE, C), 1.0, 6.0, ((0, 128),))
    dw_kernel = normal_values(key_list[2], (49, C), 49 ** -0.5, 0.875, (), jnp.float32)
    norm_gain = jnp.clip(1.0 + 0.18 * jax.random.normal(key_list[3], (C,), jnp.float32), 0.1, 1.9)
    w_expand = draw_w_expand(jax.random.fold_in(key_list[8], 71), 0)
    grn_gamma = normal_values(key_list[5], (H,), 0.5, 3.0, (), jnp.float32)
    grn_beta = normal_values(key_list[6], (H,), 0.5, 3.0, (), jnp.float32)
    w_reduce = normal_values(key_list[7], (H, C), H ** -0.5, 0.109375, ((0, 8),))
    return dict(features=features, cotangent=cotangent, dw_kernel=dw_kernel, norm_gain=norm_gain, w_expand=w_expand, grn_gamma=grn_gamma, grn_beta=grn_beta, w_reduce=w_reduce)


def stem_norm(images, dw_kernel, norm_gain):
    height = images.shape[1]
    breadth = images.shape[2]
    padded = jnp.pad(images, ((0, 0), (3, 3), (3, 3), (0, 0)))
    filtered = jnp.zeros_like(images)
    for offset_row in range(7):
        for offset_col in range(7):
            filtered = filtered + dw_kernel[offset_row * 7 + offset_col] * padded[:, offset_row:offset_row + height, offset_col:offset_col + breadth, :]
    centre = lax.optimization_barrier(jnp.mean(filtered, axis=-1, keepdims=True))
    shifted = filtered - centre
    spread = lax.optimization_barrier(jnp.mean(shifted * shifted, axis=-1, keepdims=True))
    return shifted * lax.rsqrt(spread + 1e-06) * norm_gain

def hidden_map(preact, grn_gamma, grn_beta):
    active = jax.nn.gelu(preact, approximate=False)
    energy = jnp.sqrt(lax.optimization_barrier(jnp.sum(active * active, axis=(1, 2), keepdims=True)) + 1e-06)
    ratio_map = energy / (lax.optimization_barrier(jnp.mean(energy, axis=-1, keepdims=True)) + 1e-06)
    return grn_gamma * (active * ratio_map) + grn_beta + active

def contract_rows(left_cols, right_cols):
    return lax.dot_general(left_cols, right_cols, (((0,), (0,)), ((), ())), preferred_element_type=jnp.float32)

def device_pass(features, cotangent, dw_kernel, norm_gain, w_expand, grn_gamma, grn_beta, w_reduce):
    images = features.astype(jnp.float32)
    normed, stem_back = jax.vjp(stem_norm, images, dw_kernel, norm_gain)
    normed_b = normed.astype(jnp.bfloat16)
    tokens = images.shape[0] * images.shape[1] * images.shape[2]
    rows_in = normed_b.reshape(tokens, -1)
    preact = lax.dot_general(rows_in, w_expand, (((1,), (1,)), ((), ())), preferred_element_type=jnp.float32)
    hidden_shape = images.shape[:3] + (w_expand.shape[0],)
    mapped, map_back = jax.vjp(hidden_map, preact.reshape(hidden_shape), grn_gamma, grn_beta)
    mapped_b = mapped.astype(jnp.bfloat16).reshape(tokens, -1)
    branch = jnp.dot(mapped_b, w_reduce, preferred_element_type=jnp.float32)
    block_out = (images + branch.reshape(images.shape)).astype(jnp.bfloat16)
    upstream = cotangent.reshape(tokens, -1)
    back_mapped = lax.dot_general(upstream, w_reduce, (((1,), (1,)), ((), ())), preferred_element_type=jnp.float32)
    back_preact, back_gamma, back_beta = map_back(back_mapped.reshape(hidden_shape))
    back_preact_b = back_preact.astype(jnp.bfloat16).reshape(tokens, -1)
    back_normed = jnp.dot(back_preact_b, w_expand, preferred_element_type=jnp.float32)
    back_images, back_kernel, back_gain = stem_back(back_normed.reshape(images.shape))
    grad_features = (cotangent.astype(jnp.float32) + back_images).astype(jnp.bfloat16)
    term_block = jnp.concatenate([contract_rows(back_preact_b, rows_in), contract_rows(mapped_b, upstream)], axis=1)
    term_block = lax.optimization_barrier(term_block.astype(jnp.bfloat16)).astype(jnp.float32)
    return (block_out, grad_features, term_block, back_kernel, back_gain, back_gamma, back_beta)

def reference(features, cotangent, dw_kernel, norm_gain, w_expand, grn_gamma, grn_beta, w_reduce):
    devices = N_REP * N_SHARD
    stacked_shape = (devices, IMG_DEV) + features.shape[1:]
    stacked = (features.reshape(stacked_shape), cotangent.reshape(stacked_shape))

    def one_device(carry, pair):
        results = device_pass(pair[0], pair[1], dw_kernel, norm_gain, w_expand, grn_gamma, grn_beta, w_reduce)
        updated = tuple((carry[slot] + results[slot + 2] for slot in range(5)))
        return (updated, (results[0], results[1]))
    initial = (jnp.zeros((H, 2 * C), jnp.float32), jnp.zeros((49, C), jnp.float32), jnp.zeros((C,), jnp.float32), jnp.zeros((H,), jnp.float32), jnp.zeros((H,), jnp.float32))
    sums, (outputs, grads) = lax.scan(one_device, initial, stacked)
    inverse = 1.0 / IMAGES
    block_out = outputs.reshape(features.shape)
    grad_features = grads.reshape(features.shape)
    grad_expand = sums[0][:, :C] * inverse
    grad_reduce = sums[0][:, C:] * inverse
    return (block_out, grad_features, sums[1] * inverse, sums[2] * inverse, grad_expand, sums[3] * inverse, sums[4] * inverse, grad_reduce)
```

```python
import jax
import jax.numpy as jnp
from jax import lax
from jax.sharding import PartitionSpec as P
from jax.experimental import pallas as pl
from jax.experimental.pallas import tpu as pltpu

S, W, C = 28, 32, 704
T = S * W
CB = 128
NCB = 6
HEAD = 8
F32, BF16 = jnp.float32, jnp.bfloat16


def params(mib=48, n=1):
    return pltpu.CompilerParams(vmem_limit_bytes=mib * 1024 * 1024, dimension_semantics=("arbitrary",) * n)


def cost(flops, nbytes):
    return pl.CostEstimate(flops=int(flops), bytes_accessed=int(nbytes), transcendentals=0)


def conv_taps(src, k_ref, dst, flip):
    def cols(jv, carry):
        base = jv * 8
        acc = [None] * S
        for b in range(7):
            taps = []
            for a in range(7):
                at = (6 - a) * 7 + (6 - b) if flip else a * 7 + b
                taps.append(jnp.broadcast_to(k_ref[pl.ds(at, 1), :], (8, CB)))
            for r in range(S):
                v = src[pl.ds(r * W + HEAD + b - 3 + base, 8), :]
                for a in range(7):
                    i = r + 3 - a
                    if 0 <= i < S:
                        t = taps[a] * v
                        acc[i] = t if acc[i] is None else acc[i] + t
        for i in range(S):
            dst[pl.ds(i * W + base, 8), :] = acc[i]
        return carry

    lax.fori_loop(0, W // 8, cols, 0)


def stem_kernel(x_ref, k_ref, gain_ref, normed_ref, xhat_ref, rstd_ref, pad, filt):
    cb = pl.program_id(0)

    @pl.when(cb == 0)
    def _():
        pad[...] = jnp.zeros_like(pad)

    for i in range(S):
        pad[pl.ds(HEAD + i * W, S), :] = x_ref[i].astype(F32)
    conv_taps(pad, k_ref, filt.at[cb], False)

    @pl.when(cb == NCB - 1)
    def _():
        lane = lax.broadcasted_iota(jnp.int32, (W, CB), 1)
        row = lax.broadcasted_iota(jnp.int32, (W, CB), 0)
        last = lane < C - (NCB - 1) * CB
        inside = row < S

        def rows(i, carry):
            at = pl.ds(pl.multiple_of(i * W, W), W)
            v = [filt[c, at, :] for c in range(NCB)]
            v[-1] = jnp.where(last, v[-1], 0.0)
            total = v[0]
            for c in range(1, NCB):
                total = total + v[c]
            mean = jnp.sum(total, axis=1, keepdims=True) * (1.0 / C)
            d = [u - mean for u in v]
            d[-1] = jnp.where(last, d[-1], 0.0)
            total = d[0] * d[0]
            for c in range(1, NCB):
                total = total + d[c] * d[c]
            spread = jnp.sum(total, axis=1, keepdims=True) * (1.0 / C)
            rstd = jnp.broadcast_to(lax.rsqrt(spread + 1e-06), (W, CB))
            rstd_ref[at, :] = rstd
            for c in range(NCB):
                n = min(CB, C - c * CB)
                xh = jnp.where(inside, d[c] * rstd, 0.0)
                xhat_ref[at, c * CB : c * CB + n] = xh[:, :n]
                g = jnp.broadcast_to(gain_ref[0:1, c * CB : c * CB + n], (W, n))
                normed_ref[at, c * CB : c * CB + n] = (xh[:, :n] * g).astype(BF16)
            return carry

        lax.fori_loop(0, S, rows, 0)


def stem(x, k, gain):
    return pl.pallas_call(
        stem_kernel,
        name="stem",
        grid=(NCB,),
        in_specs=[
            pl.BlockSpec((S, S, CB), lambda c: (0, 0, c)),
            pl.BlockSpec((49, CB), lambda c: (0, c)),
            pl.BlockSpec((1, C), lambda c: (0, 0)),
        ],
        out_specs=[
            pl.BlockSpec((T, C), lambda c: (0, 0)),
            pl.BlockSpec((T, C), lambda c: (0, 0)),
            pl.BlockSpec((T, CB), lambda c: (0, 0)),
        ],
        out_shape=[
            jax.ShapeDtypeStruct((T, C), BF16),
            jax.ShapeDtypeStruct((T, C), F32),
            jax.ShapeDtypeStruct((T, CB), F32),
        ],
        scratch_shapes=[pltpu.VMEM((T + 2 * HEAD, CB), F32), pltpu.VMEM((NCB, T, CB), F32)],
        compiler_params=params(),
        cost_estimate=cost(2 * 49 * T * C, 8 * T * C),
    )(x, k, gain.reshape(1, C))


def widen_kernel(x_ref, y_ref):
    zero = jnp.zeros((W - S, C), F32)
    for i in range(S):
        y_ref[pl.ds(i * W, W), :] = jnp.concatenate([x_ref[i].astype(F32), zero], axis=0).astype(BF16)


def widen(x):
    return pl.pallas_call(
        widen_kernel,
        name="widen",
        out_shape=jax.ShapeDtypeStruct((T, C), BF16),
        compiler_params=pltpu.CompilerParams(vmem_limit_bytes=16 * 1024 * 1024),
        cost_estimate=cost(T * C, 4 * T * C),
    )(x)


def gelu_pair(x):
    mag = jnp.abs(x)
    e = jnp.exp(-0.5 * (x * x))
    t = 1.0 / (1.0 + (0.3275911 * 0.7071067811865476) * mag)
    poly = (((1.061405429 * t - 1.453152027) * t + 1.421413741) * t - 0.284496736) * t + 0.254829592
    tail = (0.5 * poly) * (t * e)
    cdf = jnp.where(x < 0.0, tail, 1.0 - tail)
    return x * cdf, cdf + (0.3989422804014327 * x) * e


HB = 256
ROWS = 448


def hidden_kernel(n_ref, c_ref, we_ref, wr_ref, act_ref, slope_ref, back_ref, stat_ref):
    nt = (((1,), (1,)), ((), ()))
    e2 = s1 = s0 = None
    we = we_ref[...]
    wr = wr_ref[...]
    for r in range(T // ROWS):
        at = slice(r * ROWS, (r + 1) * ROWS)
        pre = lax.dot_general(n_ref[at, :], we, nt, preferred_element_type=F32)
        dm = lax.dot_general(c_ref[at, :], wr, nt, preferred_element_type=F32)
        act, slope = gelu_pair(pre)
        act_ref[at, :] = act.astype(BF16)
        slope_ref[at, :] = slope.astype(BF16)
        back_ref[at, :] = dm.astype(BF16)
        a2 = jnp.sum((act * act).reshape(ROWS // 8, 8, HB), axis=0)
        d1 = jnp.sum((dm * act).reshape(ROWS // 8, 8, HB), axis=0)
        d0 = jnp.sum(dm.reshape(ROWS // 8, 8, HB), axis=0)
        e2 = a2 if e2 is None else e2 + a2
        s1 = d1 if s1 is None else s1 + d1
        s0 = d0 if s0 is None else s0 + d0
    stat_ref[0:1, :] = jnp.sum(e2, axis=0, keepdims=True)
    stat_ref[1:2, :] = jnp.sum(s1, axis=0, keepdims=True)
    stat_ref[2:3, :] = jnp.sum(s0, axis=0, keepdims=True)


def hidden(normed, cot, we, wr):
    n = we.shape[0]
    steps = pl.cdiv(n, HB)
    wide = pl.BlockSpec((T, HB), lambda h: (0, h))
    rows = pl.BlockSpec((HB, C), lambda h: (h, 0))
    full = pl.BlockSpec((T, C), lambda h: (0, 0))
    return pl.pallas_call(
        hidden_kernel,
        name="hidden",
        grid=(steps,),
        in_specs=[full, full, rows, rows],
        out_specs=[wide, wide, wide, pl.BlockSpec((8, HB), lambda h: (0, h))],
        out_shape=[jax.ShapeDtypeStruct((T, n), BF16)] * 3 + [jax.ShapeDtypeStruct((8, n), F32)],
        compiler_params=params(),
        cost_estimate=cost(4 * T * C * n, 6 * T * n),
    )(normed, cot, we, wr)


def mix_kernel(act0, act1, slope0, slope1, back0, back1, n0, n1, c0, c1, we_ref, wr_ref, v_ref,
               te_ref, tr_ref, br0, br1, bn0, bn1, acc_br, acc_bn):
    h = pl.program_id(0)
    steps = pl.num_programs(0)
    tn = (((0,), (0,)), ((), ()))
    we = we_ref[...]
    wr = wr_ref[...]
    te = tr = None
    for im, (act, slope, back, nn, cc) in enumerate(((act0, slope0, back0, n0, c0), (act1, slope1, back1, n1, c1))):
        p = v_ref[3 * im : 3 * im + 1, :]
        q = v_ref[3 * im + 1 : 3 * im + 2, :]
        beta = v_ref[3 * im + 2 : 3 * im + 3, :]
        a = act[...].astype(F32)
        mapped = (a * p + beta).astype(BF16)
        bp = ((back[...].astype(F32) * p + a * q) * slope[...].astype(F32)).astype(BF16)
        br = lax.dot(mapped, wr, preferred_element_type=F32)
        bn = lax.dot(bp, we, preferred_element_type=F32)

        @pl.when(h == 0)
        def _():
            acc_br[im] = br
            acc_bn[im] = bn

        @pl.when(h > 0)
        def _():
            acc_br[im] += br
            acc_bn[im] += bn

        r1 = lax.dot_general(mapped, cc[...], tn, preferred_element_type=F32)
        e1 = lax.dot_general(bp, nn[...], tn, preferred_element_type=F32)
        tr = r1 if tr is None else tr + r1
        te = e1 if te is None else te + e1
    te_ref[...] = te.astype(BF16)
    tr_ref[...] = tr.astype(BF16)

    @pl.when(h == steps - 1)
    def _():
        br0[...] = acc_br[0].astype(BF16)
        br1[...] = acc_br[1].astype(BF16)
        bn0[...] = acc_bn[0].astype(bn0.dtype)
        bn1[...] = acc_bn[1].astype(BF16)


MB = 256


def mix(a0, a1, we, wr, vecs, n0, n1, c0, c1):
    n = we.shape[0]
    steps = n // MB
    wide = pl.BlockSpec((T, MB), lambda h: (0, h))
    rows = pl.BlockSpec((MB, C), lambda h: (h, 0))
    full = pl.BlockSpec((T, C), lambda h: (0, 0))
    return pl.pallas_call(
        mix_kernel,
        name="mix",
        grid=(steps,),
        in_specs=[wide] * 6 + [full] * 4 + [rows, rows, pl.BlockSpec((8, MB), lambda h: (0, h))],
        out_specs=[rows, rows, full, full, full, full],
        out_shape=[jax.ShapeDtypeStruct((n, C), BF16)] * 2
        + [jax.ShapeDtypeStruct((T, C), d) for d in (BF16, BF16, F32, BF16)],
        scratch_shapes=[pltpu.VMEM((2, T, C), F32), pltpu.VMEM((2, T, C), F32)],
        compiler_params=params(60),
        cost_estimate=cost(16 * T * C * n, 12 * T * n),
    )(a0[0], a1[0], a0[1], a1[1], a0[2], a1[2], n0, n1, c0, c1, we, wr, vecs)


def unnorm_kernel(b0, b1, xhat, rstd, gain, d_ref, gg_ref, *, step):
    @pl.when(pl.program_id(0) == 0)
    def _():
        gg_ref[...] = jnp.zeros_like(gg_ref)

    def rows(i, carry):
        at = pl.ds(pl.multiple_of(i * W, W), W)
        bn = b0[at, :].astype(F32) + b1[at, :].astype(F32)
        xh = xhat[at, :]
        g = bn * gain[0:1, :]
        m1 = jnp.sum(g, axis=1, keepdims=True) * (1.0 / C)
        m2 = jnp.sum(g * xh, axis=1, keepdims=True) * (1.0 / C)
        r = rstd[at, 0:1]
        d_ref[at, :] = r * (g - m1 - xh * m2)
        gg_ref[...] += jnp.sum((bn * xh).reshape(W // 8, 8, C), axis=0)
        return carry

    lax.fori_loop(0, step // W, rows, 0)


def unnorm(b0, b1, xhat, rstd, gain):
    step = T // 4
    full = pl.BlockSpec((step, C), lambda r: (r, 0))
    return pl.pallas_call(
        lambda *refs: unnorm_kernel(*refs, step=step),
        name="unnorm",
        grid=(T // step,),
        in_specs=[full, full, full, pl.BlockSpec((step, CB), lambda r: (r, 0)), pl.BlockSpec((1, C), lambda r: (0, 0))],
        out_specs=[full, pl.BlockSpec((8, C), lambda r: (0, 0))],
        out_shape=[jax.ShapeDtypeStruct((T, C), F32), jax.ShapeDtypeStruct((8, C), F32)],
        compiler_params=params(),
        cost_estimate=cost(10 * T * C, 14 * T * C),
    )(b0, b1, xhat, rstd, gain.reshape(1, C))


def taps_kernel(x_ref, d_ref, g_ref, pad):
    @pl.when(pl.program_id(0) == 0)
    def _():
        pad[...] = jnp.zeros_like(pad)

    for i in range(S):
        pad[pl.ds(HEAD + i * W, S), :] = x_ref[i].astype(F32)

    for b in range(7):
        def cols(jv, acc):
            base = jv * 8
            acc = list(acc)
            d = {}
            for r in range(S):
                if r == 0:
                    for i in range(4):
                        d[i] = d_ref[pl.ds(i * W + base, 8), :]
                elif r + 3 < S:
                    d[r + 3] = d_ref[pl.ds((r + 3) * W + base, 8), :]
                v = pad[pl.ds(r * W + HEAD + b - 3 + base, 8), :]
                for a in range(7):
                    i = r + 3 - a
                    if 0 <= i < S:
                        acc[a] = acc[a] + d[i] * v
            return tuple(acc)

        acc = lax.fori_loop(0, W // 8, cols, (jnp.zeros((8, CB), F32),) * 7)
        for a in range(7):
            g_ref[pl.ds(a * 7 + b, 1), :] = jnp.sum(acc[a], axis=0, keepdims=True)


def taps(x, d):
    return pl.pallas_call(
        taps_kernel,
        name="taps",
        grid=(NCB,),
        in_specs=[pl.BlockSpec((S, S, CB), lambda c: (0, 0, c)), pl.BlockSpec((T, CB), lambda c: (0, c))],
        out_specs=pl.BlockSpec((49, CB), lambda c: (0, c)),
        out_shape=jax.ShapeDtypeStruct((49, C), F32),
        scratch_shapes=[pltpu.VMEM((T + 2 * HEAD, CB), F32)],
        compiler_params=params(),
        cost_estimate=cost(2 * 49 * T * C, 6 * T * C),
    )(x, d)


def unstem_kernel(d_ref, k_ref, c_ref, o_ref, pad, res):
    @pl.when(pl.program_id(0) == 0)
    def _():
        pad[...] = jnp.zeros_like(pad)

    pad[pl.ds(HEAD, T), :] = d_ref[...]
    conv_taps(pad, k_ref, res, True)
    for i in range(S):
        o_ref[i] = (c_ref[i].astype(F32) + res[pl.ds(i * W, S), :]).astype(BF16)


def unstem(d, k, cot):
    return pl.pallas_call(
        unstem_kernel,
        name="unstem",
        grid=(NCB,),
        in_specs=[
            pl.BlockSpec((T, CB), lambda c: (0, c)),
            pl.BlockSpec((49, CB), lambda c: (0, c)),
            pl.BlockSpec((S, S, CB), lambda c: (0, 0, c)),
        ],
        out_specs=pl.BlockSpec((S, S, CB), lambda c: (0, 0, c)),
        out_shape=jax.ShapeDtypeStruct((S, S, C), BF16),
        scratch_shapes=[pltpu.VMEM((T + 2 * HEAD, CB), F32), pltpu.VMEM((T, CB), F32)],
        compiler_params=params(),
        cost_estimate=cost(2 * 49 * T * C, 8 * T * C),
    )(d, k, cot)


def finish_kernel(x_ref, b0, b1, o_ref):
    for i in range(S):
        at = pl.ds(i * W, W)
        t = b0[at, :].astype(F32) + b1[at, :].astype(F32)
        o_ref[i] = (x_ref[i].astype(F32) + t[:S]).astype(BF16)


def finish(x, b0, b1):
    return pl.pallas_call(
        finish_kernel,
        name="finish",
        out_shape=jax.ShapeDtypeStruct((S, S, C), BF16),
        compiler_params=pltpu.CompilerParams(vmem_limit_bytes=24 * 1024 * 1024),
        cost_estimate=cost(2 * T * C, 8 * T * C),
    )(x, b0, b1)


SHIFTS = (0, -1, 1, 2)
AXES = ("rep", "shard")


def place(x, y, z, c):
    return ((y * 2 + z % 2) * 2 + c) * 8 + x * 2 + z // 2


def moves(fn):
    pairs = []
    for x in range(4):
        for y in range(4):
            for z in range(4):
                for c in range(2):
                    nx, ny, nz, nc = fn(x, y, z, c)
                    pairs.append((place(x, y, z, c), place(nx % 4, ny % 4, nz % 4, nc)))
    return pairs


def along_x(d):
    return lambda x, y, z, c: (x + d, y, z, c)


def along_y(d):
    return lambda x, y, z, c: (x, y + d, z, c)


def minor(d):
    return lambda x, y, z, c: (x, y, z + d, c) if c == 0 else (x + d, y, z, c)


def major(d):
    return lambda x, y, z, c: (x + d, y, z, c) if c == 0 else (x, y, z + d, c)


def swap_core(x, y, z, c):
    return (x, y, z, 1 - c)


def swap_zlo(x, y, z, c):
    return (x, y, z + 1 - 2 * (z % 2), c)


def send(v, fn):
    return lax.ppermute(v, AXES, moves(fn))


def spread(v, axis_fn):
    return [v] + [send(v, axis_fn(-d)) for d in SHIFTS[1:]]


def gather_sum(parts, axis_fn):
    got = [parts[0]] + [send(parts[j], axis_fn(SHIFTS[j])) for j in (1, 2, 3)]
    total = got[0].astype(F32)
    for g in got[1:]:
        total = total + g.astype(F32)
    return total


def turn(v, start):
    size = v.shape[0]
    return lax.dynamic_slice_in_dim(jnp.concatenate([v, v], axis=0), start, size, axis=0)


ORDER = (0, 3, 1, 2)
BACK = (0, 2, 3, 1)


def shards(features, cotangent, dw_kernel, norm_gain, w_expand, grn_gamma, grn_beta, w_reduce):
    rep = lax.axis_index("rep")
    shard = lax.axis_index("shard")
    c = rep % 2
    zl = (rep // 2) % 2
    x = shard // 2
    z = (shard % 2) * 2 + zl
    hid = grn_gamma.shape[0]
    piece = hid // 32
    wide = 96
    n = 16 * wide
    img = features[0]
    cot = cotangent[0]

    first = c * (2 * piece) + zl * piece
    own = jnp.stack([lax.dynamic_slice_in_dim(w, first, piece, axis=0) for w in (w_expand, w_reduce)])
    own = jnp.pad(own, ((0, 0), (0, wide - piece), (0, 0)))
    row = jnp.concatenate(spread(own, minor), axis=1)
    weights = jnp.concatenate(spread(row, major), axis=1)
    we, wr = weights[0], weights[1]

    def to_own(v):
        v = lax.dynamic_index_in_dim(v.reshape(4, 2, 2, 2, piece), c, axis=2, keepdims=False).reshape(4, 4, piece)
        v = turn(v, x).transpose(1, 0, 2)
        v = turn(v, z)
        v = jnp.where(c == 0, v.transpose(1, 0, 2), v)
        v = jnp.stack([v[k] for k in ORDER])
        v = jnp.stack([v[:, k] for k in ORDER], axis=1)
        return jnp.pad(v, ((0, 0), (0, 0), (0, wide - piece))).reshape(1, n)

    def to_all(v):
        v = v.reshape(4, 4, wide)[:, :, :piece]
        v = jnp.stack([v[k] for k in BACK])
        v = jnp.stack([v[:, k] for k in BACK], axis=1)
        v = jnp.where(c == 0, v, v.transpose(1, 0, 2))
        v = turn(v, (4 - x) % 4).transpose(1, 0, 2)
        v = turn(v, (4 - z) % 4).transpose(1, 0, 2).reshape(4, 2, 1, 2, piece)
        zero = jnp.zeros_like(v)
        both = jnp.where(c == 0, jnp.concatenate([v, zero], axis=2), jnp.concatenate([zero, v], axis=2))
        return both.reshape(4, hid // 4)

    gamma = to_own(grn_gamma)
    beta = to_own(grn_beta)
    valid = (jnp.arange(n) % wide < piece).astype(F32)[None]

    cot0 = widen(cot)
    cot1 = send(cot0, swap_core)
    norm0, xhat, rstd = stem(img, dw_kernel, norm_gain)
    norm1 = send(norm0, swap_core)
    h0 = hidden(norm0, cot0, we, wr)
    h1 = hidden(norm1, cot1, we, wr)
    stats = jnp.stack([h0[3], h1[3]])
    energy = jnp.sqrt(stats[:, 0] + 1e-06)
    back_ratio = gamma * stats[:, 1]
    sums = jnp.stack([jnp.sum(energy * valid, axis=1), jnp.sum(back_ratio * energy, axis=1)], axis=1)
    sums = sums + send(sums, swap_core)[::-1]
    den = sums[:, 0:1] * (1.0 / hid) + 1e-06
    ratio = energy / den
    scale = 1.0 + gamma * ratio
    back_energy = back_ratio / den - sums[:, 1:2] * (1.0 / hid) / (den * den)
    pull = back_energy / energy
    vecs = jnp.stack([scale[0], pull[0], beta[0], scale[1], pull[1], beta[0], beta[0], beta[0]])
    back_gamma = to_all(jnp.sum(ratio * stats[:, 1], axis=0))
    back_beta = to_all(jnp.sum(stats[:, 2], axis=0))

    te, tr, br0, br1, bn0, bn1 = mix(h0, h1, we, wr, vecs, norm0, norm1, cot0, cot1)
    bn1 = send(bn1, swap_core)
    br1 = send(br1, swap_core)
    d, gain_rows = unnorm(bn0, bn1, xhat, rstd, norm_gain)
    grad_taps = taps(img, d)
    small = jnp.concatenate([grad_taps, jnp.sum(gain_rows, axis=0, keepdims=True), back_gamma, back_beta], axis=0)
    small = lax.psum(small, AXES)
    grad_features = unstem(d, dw_kernel, cot)
    block_out = finish(img, br0, br1)

    terms = jnp.concatenate([te.reshape(4, 4, wide, C), tr.reshape(4, 4, wide, C)], axis=2)
    part = gather_sum([terms[k] for k in range(4)], major).astype(BF16)
    part = gather_sum([part[k] for k in range(4)], minor).astype(BF16)
    total = part.astype(F32)
    for d_y in (1, -1, 2):
        total = total + send(part, along_y(d_y)).astype(F32)
    inverse = 1.0 / (features.shape[0] * lax.axis_size("rep") * lax.axis_size("shard"))
    total = total.astype(BF16).reshape(2, 1, wide, C)[:, :, :piece]
    other = send(total, swap_zlo)
    total = jnp.where(zl == 0, jnp.concatenate([total, other], axis=1), jnp.concatenate([other, total], axis=1))
    total = total.reshape(2, 1, 2 * piece, C)
    other = send(total, swap_core)
    total = jnp.where(c == 0, jnp.concatenate([total, other], axis=1), jnp.concatenate([other, total], axis=1))
    total = total.reshape(2, 4 * piece, C).astype(F32) * inverse
    small = small * inverse
    return (
        block_out[None],
        grad_features[None],
        small[:49],
        small[49],
        total[0],
        small[50:54].reshape(hid),
        small[54:58].reshape(hid),
        total[1],
    )


def solution(mesh):
    data = P(AXES, None, None, None)
    rows = P("shard", None)
    return jax.shard_map(
        shards,
        mesh=mesh,
        in_specs=(data, data, P(), P(), rows, P(), P(), rows),
        out_specs=(data, data, P(), P(), rows, P(), P(), rows),
        check_vma=False,
    )
```

```python
import jax
import jax.numpy as jnp
from jax import lax
from jax.sharding import PartitionSpec as P
from jax.experimental import pallas as pl
from jax.experimental.pallas import tpu as pltpu

S, W, C = 28, 32, 704
T = S * W
CB = 128
NCB = 6
HEAD = 8
CP = NCB * CB
HALF = NCB // 2
SLOT = 384
F32, BF16 = jnp.float32, jnp.bfloat16


def params(mib=48, n=1):
    return pltpu.CompilerParams(vmem_limit_bytes=mib * 1024 * 1024, dimension_semantics=("arbitrary",) * n)


def cost(flops, nbytes):
    return pl.CostEstimate(flops=int(flops), bytes_accessed=int(nbytes), transcendentals=0)


def conv_taps(src, k_ref, dst, flip):
    def cols(jv, carry):
        base = jv * 8
        acc = [None] * S
        for b in range(7):
            taps = []
            for a in range(7):
                at = (6 - a) * 7 + (6 - b) if flip else a * 7 + b
                taps.append(jnp.broadcast_to(k_ref[pl.ds(at, 1), :], (8, CB)))
            for r in range(S):
                v = src[pl.ds(r * W + HEAD + b - 3 + base, 8), :]
                for a in range(7):
                    i = r + 3 - a
                    if 0 <= i < S:
                        t = taps[a] * v
                        acc[i] = t if acc[i] is None else acc[i] + t
        for i in range(S):
            dst[pl.ds(i * W + base, 8), :] = acc[i]
        return carry

    lax.fori_loop(0, W // 8, cols, 0)


def load_map(x_ref, pad):
    for i in range(S):
        pad[pl.ds(HEAD + i * W, S), :] = x_ref[i].astype(F32)


def stem_first_kernel(x_ref, k_ref, filt_ref, pad):
    @pl.when(pl.program_id(0) == 0)
    def _():
        pad[...] = jnp.zeros_like(pad)

    load_map(x_ref, pad)
    conv_taps(pad, k_ref, filt_ref.at[0], False)


def stem_first(x, k):
    return pl.pallas_call(
        stem_first_kernel,
        name="stem_first",
        grid=(HALF,),
        in_specs=[pl.BlockSpec((S, S, CB), lambda c: (0, 0, c)), pl.BlockSpec((49, CB), lambda c: (0, c))],
        out_specs=pl.BlockSpec((1, T, CB), lambda c: (c, 0, 0)),
        out_shape=jax.ShapeDtypeStruct((HALF, T, CB), F32),
        scratch_shapes=[pltpu.VMEM((T + 2 * HEAD, CB), F32)],
        compiler_params=params(24),
        cost_estimate=cost(49 * T * C * 8, 6 * T * C),
    )(x, k)


def stem_kernel(x_ref, k_ref, gain_ref, first_ref, normed_ref, xhat_ref, rstd_ref, pad, filt):
    cb = pl.program_id(0)

    @pl.when(cb == 0)
    def _():
        pad[...] = jnp.zeros_like(pad)

    load_map(x_ref, pad)
    conv_taps(pad, k_ref, filt.at[cb], False)

    @pl.when(cb == HALF - 1)
    def _():
        lane = lax.broadcasted_iota(jnp.int32, (W, CB), 1)
        row = lax.broadcasted_iota(jnp.int32, (W, CB), 0)
        last = lane < C - (NCB - 1) * CB
        inside = row < S

        def rows(i, carry):
            at = pl.ds(pl.multiple_of(i * W, W), W)
            v = [first_ref[c, at, :] for c in range(HALF)] + [filt[c, at, :] for c in range(NCB - HALF)]
            v[-1] = jnp.where(last, v[-1], 0.0)
            total = v[0]
            for c in range(1, NCB):
                total = total + v[c]
            mean = jnp.sum(total, axis=1, keepdims=True) * (1.0 / C)
            d = [u - mean for u in v]
            d[-1] = jnp.where(last, d[-1], 0.0)
            total = d[0] * d[0]
            for c in range(1, NCB):
                total = total + d[c] * d[c]
            spread = jnp.sum(total, axis=1, keepdims=True) * (1.0 / C)
            rstd = jnp.broadcast_to(lax.rsqrt(spread + 1e-06), (W, CB))
            rstd_ref[at, :] = rstd
            for c in range(NCB):
                n = min(CB, C - c * CB)
                xh = jnp.where(inside, d[c] * rstd, 0.0)
                xhat_ref[at, c * CB : c * CB + n] = xh[:, :n]
                g = jnp.broadcast_to(gain_ref[0:1, c * CB : (c + 1) * CB], (W, CB))
                normed_ref[at, c * CB : (c + 1) * CB] = (xh * g).astype(BF16)
            return carry

        lax.fori_loop(0, S, rows, 0)


def stem(x, k, gain, first):
    return pl.pallas_call(
        stem_kernel,
        name="stem",
        grid=(NCB - HALF,),
        in_specs=[
            pl.BlockSpec((S, S, CB), lambda c: (0, 0, c + HALF)),
            pl.BlockSpec((49, CB), lambda c: (0, c + HALF)),
            pl.BlockSpec((1, CP), lambda c: (0, 0)),
            pl.BlockSpec((HALF, T, CB), lambda c: (0, 0, 0)),
        ],
        out_specs=[
            pl.BlockSpec((T, CP), lambda c: (0, 0)),
            pl.BlockSpec((T, C), lambda c: (0, 0)),
            pl.BlockSpec((T, CB), lambda c: (0, 0)),
        ],
        out_shape=[
            jax.ShapeDtypeStruct((T, CP), BF16),
            jax.ShapeDtypeStruct((T, C), F32),
            jax.ShapeDtypeStruct((T, CB), F32),
        ],
        scratch_shapes=[pltpu.VMEM((T + 2 * HEAD, CB), F32), pltpu.VMEM((NCB - HALF, T, CB), F32)],
        compiler_params=params(36),
        cost_estimate=cost(49 * T * C * 8, 8 * T * C),
    )(x, k, jnp.pad(gain, (0, CP - C)).reshape(1, CP), first)


def widen_kernel(x_ref, y_ref):
    zero = jnp.zeros((W - S, C), F32)
    y_ref[:, C:] = jnp.zeros((T, CP - C), BF16)
    for i in range(S):
        y_ref[pl.ds(i * W, W), :C] = jnp.concatenate([x_ref[i].astype(F32), zero], axis=0).astype(BF16)


def widen(x):
    return pl.pallas_call(
        widen_kernel,
        name="widen",
        out_shape=jax.ShapeDtypeStruct((T, CP), BF16),
        compiler_params=pltpu.CompilerParams(vmem_limit_bytes=16 * 1024 * 1024),
        cost_estimate=cost(T * C, 4 * T * C),
    )(x)


def gelu_pair(x):
    mag = jnp.abs(x)
    e = jnp.exp(-0.5 * (x * x))
    t = 1.0 / (1.0 + (0.3275911 * 0.7071067811865476) * mag)
    poly = (((1.061405429 * t - 1.453152027) * t + 1.421413741) * t - 0.284496736) * t + 0.254829592
    tail = (0.5 * poly) * (t * e)
    cdf = jnp.where(x < 0.0, tail, 1.0 - tail)
    return x * cdf, cdf + (0.3989422804014327 * x) * e


def split_rows(w):
    zero = jnp.zeros((SLOT - w.shape[0], C), BF16)
    return jnp.concatenate([w[:, :C], zero], axis=0), jnp.concatenate([w[:, C:], zero], axis=0)


ROWS = 448
STEPS = T // ROWS


def hidden_kernel(n0, n1, c0, c1, w_ref, act_ref, slope_ref, back_ref, stat_ref):
    g = pl.program_id(0)
    nt = (((1,), (1,)), ((), ()))

    def body(n_ref, c_ref):
        we, wr = split_rows(w_ref[...])
        pre = lax.dot_general(n_ref[:, :C], we, nt, preferred_element_type=F32)
        dm = lax.dot_general(c_ref[:, :C], wr, nt, preferred_element_type=F32)
        act, slope = gelu_pair(pre)
        act_ref[...] = act.astype(BF16)
        slope_ref[...] = slope.astype(BF16)
        back_ref[...] = dm.astype(BF16)
        e2 = jnp.sum(act * act, axis=0, keepdims=True)
        s1 = jnp.sum(dm * act, axis=0, keepdims=True)
        s0 = jnp.sum(dm, axis=0, keepdims=True)
        stat_ref[0] += jnp.concatenate([e2, s1, s0, jnp.zeros((5, SLOT), F32)], axis=0)

    @pl.when(g % STEPS == 0)
    def _():
        stat_ref[...] = jnp.zeros_like(stat_ref)

    @pl.when(g < STEPS)
    def _():
        body(n0, c0)

    @pl.when(g >= STEPS)
    def _():
        body(n1, c1)


def hidden(n0, n1, c0, c1, w):
    wide = pl.BlockSpec((ROWS, SLOT), lambda g: (g, 0))
    one = pl.BlockSpec((ROWS, CP), lambda g: (jnp.minimum(g, STEPS - 1), 0))
    two = pl.BlockSpec((ROWS, CP), lambda g: (jnp.maximum(g - STEPS, 0), 0))
    return pl.pallas_call(
        hidden_kernel,
        name="hidden",
        grid=(2 * STEPS,),
        in_specs=[one, two, one, two, pl.BlockSpec(w.shape, lambda g: (0, 0))],
        out_specs=[wide, wide, wide, pl.BlockSpec((1, 8, SLOT), lambda g: (g // STEPS, 0, 0))],
        out_shape=[jax.ShapeDtypeStruct((2 * T, SLOT), BF16)] * 3 + [jax.ShapeDtypeStruct((2, 8, SLOT), F32)],
        compiler_params=params(32),
        cost_estimate=cost(24 * T * C * SLOT, 12 * T * SLOT),
    )(n0, n1, c0, c1, w)


def mix_kernel(act, slope, back, n0, n1, c0, c1, v_ref, mapped_ref, bp_ref, t_ref, te, tr):
    im = pl.program_id(0)
    tn = (((0,), (0,)), ((), ()))
    v = v_ref[0, 0]
    p, q, beta = v[0:1], v[1:2], v[2:3]
    a = act[...].astype(F32)
    mapped = (a * p + beta).astype(BF16)
    bp = ((back[...].astype(F32) * p + a * q) * slope[...].astype(F32)).astype(BF16)
    mapped_ref[...] = mapped
    bp_ref[...] = bp

    def terms(n_ref, c_ref):
        e = lax.dot_general(bp, n_ref[:, :C], tn, preferred_element_type=F32)
        r = lax.dot_general(mapped, c_ref[:, :C], tn, preferred_element_type=F32)
        return e, r

    @pl.when(im == 0)
    def _():
        te[...], tr[...] = terms(n0, c0)

    @pl.when(im == 1)
    def _():
        e, r = terms(n1, c1)
        n = t_ref.shape[0]
        t_ref[:, :C] = (te[...] + e)[:n].astype(BF16)
        t_ref[:, C:] = (tr[...] + r)[:n].astype(BF16)


def mix(h, n0, n1, c0, c1, vecs, slot, n):
    wide = pl.BlockSpec((T, SLOT), lambda g: (g, 0))
    full = pl.BlockSpec((T, CP), lambda g: (0, 0))
    return pl.pallas_call(
        mix_kernel,
        name="mix",
        grid=(2,),
        in_specs=[wide] * 3 + [full] * 4 + [pl.BlockSpec((1, 1, 8, SLOT), lambda g: (slot, g, 0, 0))],
        out_specs=[wide, wide, pl.BlockSpec((n, 2 * C), lambda g: (0, 0))],
        out_shape=[jax.ShapeDtypeStruct((2 * T, SLOT), BF16)] * 2 + [jax.ShapeDtypeStruct((n, 2 * C), BF16)],
        scratch_shapes=[pltpu.VMEM((SLOT, C), F32), pltpu.VMEM((SLOT, C), F32)],
        compiler_params=params(44),
        cost_estimate=cost(16 * T * C * SLOT, 16 * T * SLOT),
    )(h[0], h[1], h[2], n0, n1, c0, c1, vecs)


def project_kernel(m0, m1, m2, m3, w0, w1, w2, w3, o_ref, *, part):
    w = jnp.concatenate([split_rows(r[...])[part] for r in (w0, w1, w2, w3)], axis=0)
    m = jnp.concatenate([r[...] for r in (m0, m1, m2, m3)], axis=1)
    out = lax.dot(m, w, preferred_element_type=F32)
    o_ref[:, :C] = out.astype(o_ref.dtype)
    o_ref[:, C:] = jnp.zeros((ROWS, CP - C), o_ref.dtype)


def project(ms, ws, part, im, dtype):
    wide = pl.BlockSpec((ROWS, SLOT), lambda g: (g + im * STEPS, 0))
    return pl.pallas_call(
        lambda *refs: project_kernel(*refs, part=part),
        name="project",
        grid=(STEPS,),
        in_specs=[wide] * 4 + [pl.BlockSpec(ws[0].shape, lambda g: (0, 0))] * 4,
        out_specs=pl.BlockSpec((ROWS, CP), lambda g: (g, 0)),
        out_shape=jax.ShapeDtypeStruct((T, CP), dtype),
        compiler_params=params(36),
        cost_estimate=cost(8 * T * C * SLOT, 16 * T * SLOT),
    )(*ms, *ws)


def unnorm_kernel(b0, b1, xhat, rstd, gain, d_ref, gg_ref, *, step):
    @pl.when(pl.program_id(0) == 0)
    def _():
        gg_ref[...] = jnp.zeros_like(gg_ref)

    def rows(i, carry):
        at = pl.ds(pl.multiple_of(i * W, W), W)
        bn = b0[at, :C].astype(F32) + b1[at, :C].astype(F32)
        xh = xhat[at, :]
        g = bn * gain[0:1, :]
        m1 = jnp.sum(g, axis=1, keepdims=True) * (1.0 / C)
        m2 = jnp.sum(g * xh, axis=1, keepdims=True) * (1.0 / C)
        r = rstd[at, 0:1]
        d_ref[at, :] = r * (g - m1 - xh * m2)
        gg_ref[...] += jnp.sum((bn * xh).reshape(W // 8, 8, C), axis=0)
        return carry

    lax.fori_loop(0, step // W, rows, 0)


def unnorm(b0, b1, xhat, rstd, gain):
    step = T // 4
    full = pl.BlockSpec((step, C), lambda r: (r, 0))
    wide = pl.BlockSpec((step, CP), lambda r: (r, 0))
    return pl.pallas_call(
        lambda *refs: unnorm_kernel(*refs, step=step),
        name="unnorm",
        grid=(T // step,),
        in_specs=[wide, wide, full, pl.BlockSpec((step, CB), lambda r: (r, 0)), pl.BlockSpec((1, C), lambda r: (0, 0))],
        out_specs=[full, pl.BlockSpec((8, C), lambda r: (0, 0))],
        out_shape=[jax.ShapeDtypeStruct((T, C), F32), jax.ShapeDtypeStruct((8, C), F32)],
        compiler_params=params(),
        cost_estimate=cost(10 * T * C, 14 * T * C),
    )(b0, b1, xhat, rstd, gain.reshape(1, C))


def taps_kernel(x_ref, d_ref, g_ref, pad):
    @pl.when(pl.program_id(0) == 0)
    def _():
        pad[...] = jnp.zeros_like(pad)

    for i in range(S):
        pad[pl.ds(HEAD + i * W, S), :] = x_ref[i].astype(F32)

    for b in range(7):
        def cols(jv, acc):
            base = jv * 8
            acc = list(acc)
            d = {}
            for r in range(S):
                if r == 0:
                    for i in range(4):
                        d[i] = d_ref[pl.ds(i * W + base, 8), :]
                elif r + 3 < S:
                    d[r + 3] = d_ref[pl.ds((r + 3) * W + base, 8), :]
                v = pad[pl.ds(r * W + HEAD + b - 3 + base, 8), :]
                for a in range(7):
                    i = r + 3 - a
                    if 0 <= i < S:
                        acc[a] = acc[a] + d[i] * v
            return tuple(acc)

        acc = lax.fori_loop(0, W // 8, cols, (jnp.zeros((8, CB), F32),) * 7)
        for a in range(7):
            g_ref[pl.ds(a * 7 + b, 1), :] = jnp.sum(acc[a], axis=0, keepdims=True)


def taps(x, d):
    return pl.pallas_call(
        taps_kernel,
        name="taps",
        grid=(NCB,),
        in_specs=[pl.BlockSpec((S, S, CB), lambda c: (0, 0, c)), pl.BlockSpec((T, CB), lambda c: (0, c))],
        out_specs=pl.BlockSpec((49, CB), lambda c: (0, c)),
        out_shape=jax.ShapeDtypeStruct((49, C), F32),
        scratch_shapes=[pltpu.VMEM((T + 2 * HEAD, CB), F32)],
        compiler_params=params(),
        cost_estimate=cost(2 * 49 * T * C, 6 * T * C),
    )(x, d)


def unstem_kernel(d_ref, k_ref, c_ref, old_ref, o_ref, pad, res):
    @pl.when(pl.program_id(0) == 0)
    def _():
        pad[...] = jnp.zeros_like(pad)

    pad[pl.ds(HEAD, T), :] = d_ref[...]
    conv_taps(pad, k_ref, res, True)
    for i in range(S):
        o_ref[i] = (c_ref[i].astype(F32) + res[pl.ds(i * W, S), :]).astype(BF16)


def unstem(d, k, cot, old, at):
    return pl.pallas_call(
        unstem_kernel if old is not None else (lambda d, k, c, *r: unstem_kernel(d, k, c, None, *r)),
        name="unstem",
        grid=(HALF,),
        in_specs=[
            pl.BlockSpec((T, CB), lambda c: (0, c + at)),
            pl.BlockSpec((49, CB), lambda c: (0, c + at)),
            pl.BlockSpec((S, S, CB), lambda c: (0, 0, c + at)),
        ]
        + ([pl.BlockSpec(memory_space=pl.ANY)] if old is not None else []),
        out_specs=pl.BlockSpec((S, S, CB), lambda c: (0, 0, c + at)),
        out_shape=jax.ShapeDtypeStruct((S, S, C), BF16),
        scratch_shapes=[pltpu.VMEM((T + 2 * HEAD, CB), F32), pltpu.VMEM((T, CB), F32)],
        input_output_aliases={3: 0} if old is not None else {},
        compiler_params=params(24),
        cost_estimate=cost(49 * T * C * 8, 8 * T * C),
    )(d, k, cot, *([old] if old is not None else []))


def finish_kernel(x_ref, b0, b1, o_ref):
    for i in range(S):
        at = pl.ds(i * W, W)
        t = b0[at, :].astype(F32) + b1[at, :].astype(F32)
        o_ref[i] = (x_ref[i].astype(F32) + t[:S, :C]).astype(BF16)


def finish(x, b0, b1):
    return pl.pallas_call(
        finish_kernel,
        name="finish",
        out_shape=jax.ShapeDtypeStruct((S, S, C), BF16),
        compiler_params=pltpu.CompilerParams(vmem_limit_bytes=24 * 1024 * 1024),
        cost_estimate=cost(2 * T * C, 8 * T * C),
    )(x, b0, b1)


SHIFTS = (0, -1, 1, 2)
AXES = ("rep", "shard")


def place(x, y, z, c):
    return ((y * 2 + z % 2) * 2 + c) * 8 + x * 2 + z // 2


def moves(fn):
    pairs = []
    for x in range(4):
        for y in range(4):
            for z in range(4):
                for c in range(2):
                    nx, ny, nz, nc = fn(x, y, z, c)
                    pairs.append((place(x, y, z, c), place(nx % 4, ny % 4, nz % 4, nc)))
    return pairs


def along_x(d):
    return lambda x, y, z, c: (x + d, y, z, c)


def along_y(d):
    return lambda x, y, z, c: (x, y + d, z, c)


def minor(d):
    return lambda x, y, z, c: (x, y, z + d, c) if c == 0 else (x + d, y, z, c)


def major(d):
    return lambda x, y, z, c: (x + d, y, z, c) if c == 0 else (x, y, z + d, c)


def swap_core(x, y, z, c):
    return (x, y, z, 1 - c)


def swap_zlo(x, y, z, c):
    return (x, y, z + 1 - 2 * (z % 2), c)


def send(v, fn):
    return lax.ppermute(v, AXES, moves(fn))


def spread(v, axis_fn):
    return [v] + [send(v, axis_fn(-d)) for d in SHIFTS[1:]]


def turn(v, start):
    size = v.shape[0]
    return lax.dynamic_slice_in_dim(jnp.concatenate([v, v], axis=0), start, size, axis=0)


ORDER = (0, 3, 1, 2)
BACK = (0, 2, 3, 1)


def add_up(parts):
    total = parts[0].astype(F32)
    for g in parts[1:]:
        total = total + g.astype(F32)
    return total


def after(v, *done):
    return lax.optimization_barrier((v,) + done)[0]


def shards(features, cotangent, dw_kernel, norm_gain, w_expand, grn_gamma, grn_beta, w_reduce):
    rep = lax.axis_index("rep")
    shard = lax.axis_index("shard")
    c = rep % 2
    zl = (rep // 2) % 2
    x = shard // 2
    z = (shard % 2) * 2 + zl
    hid = grn_gamma.shape[0]
    piece = hid // 32
    n = 4 * piece
    img = features[0]
    cot = cotangent[0]

    first = c * (2 * piece) + zl * piece
    own = jnp.concatenate([lax.dynamic_slice_in_dim(w, first, piece, axis=0) for w in (w_expand, w_reduce)], axis=1)
    filt = stem_first(img, dw_kernel)
    row = jnp.concatenate(spread(own, minor), axis=0)
    ws = spread(row, major)

    def to_own(v):
        v = lax.dynamic_index_in_dim(v.reshape(4, 2, 2, 2, piece), c, axis=2, keepdims=False).reshape(4, 4, piece)
        v = turn(v, x).transpose(1, 0, 2)
        v = turn(v, z)
        v = jnp.where(c == 0, v.transpose(1, 0, 2), v)
        v = jnp.stack([v[k] for k in ORDER])
        v = jnp.stack([v[:, k] for k in ORDER], axis=1)
        return jnp.pad(v.reshape(1, 4, n), ((0, 0), (0, 0), (0, SLOT - n)))

    def to_all(v):
        v = v[:, :n].reshape(4, 4, piece)
        v = jnp.stack([v[k] for k in BACK])
        v = jnp.stack([v[:, k] for k in BACK], axis=1)
        v = jnp.where(c == 0, v, v.transpose(1, 0, 2))
        v = turn(v, (4 - x) % 4).transpose(1, 0, 2)
        v = turn(v, (4 - z) % 4).transpose(1, 0, 2).reshape(4, 2, 1, 2, piece)
        zero = jnp.zeros_like(v)
        both = jnp.where(c == 0, jnp.concatenate([v, zero], axis=2), jnp.concatenate([zero, v], axis=2))
        return both.reshape(4, hid // 4)

    gamma = to_own(grn_gamma)
    beta = to_own(grn_beta)
    valid = (jnp.arange(SLOT) < n).astype(F32)[None, None]

    c0 = widen(cot)
    c1 = send(c0, swap_core)
    n0, xhat, rstd = stem(after(img, row), dw_kernel, norm_gain, filt)
    n1 = send(n0, swap_core)
    hs = [hidden(n0, n1, c0, c1, w) for w in ws]
    stats = jnp.stack([h[3][:, :3] for h in hs], axis=2)
    energy = jnp.sqrt(stats[:, 0] + 1e-06)
    back_ratio = gamma * stats[:, 1]
    sums = jnp.stack([jnp.sum(energy * valid, axis=(1, 2)), jnp.sum(back_ratio * energy, axis=(1, 2))], axis=1)
    sums = sums + send(sums, swap_core)[::-1]
    sums = sums.reshape(2, 2, 1, 1)
    den = sums[:, 0] * (1.0 / hid) + 1e-06
    ratio = energy / den
    scale = 1.0 + gamma * ratio
    back_energy = back_ratio / den - sums[:, 1] * (1.0 / hid) / (den * den)
    pull = back_energy / energy
    vecs = jnp.stack([scale, pull, jnp.broadcast_to(beta, scale.shape)] + [jnp.zeros_like(scale)] * 5)
    vecs = vecs.transpose(2, 1, 0, 3)
    back_gamma = to_all(jnp.sum(ratio * stats[:, 1], axis=0))
    back_beta = to_all(jnp.sum(stats[:, 2], axis=0))

    mapped, bps, terms, sent = [None] * 4, [None] * 4, [None] * 4, [None] * 4
    prev = vecs
    for j in (3, 1, 2, 0):
        mapped[j], bps[j], terms[j] = mix(hs[j], n0, n1, c0, c1, after(vecs, prev), j, n)
        prev = bps[j]
        sent[j] = send(terms[j], major(SHIFTS[j])) if j else terms[j]
    bn1 = project(bps, ws, 0, 1, BF16)
    bn1_in = send(bn1, swap_core)
    bn0 = project([after(b, bn1) for b in bps], ws, 0, 0, F32)
    br1 = project([after(b, bn0) for b in mapped], ws, 1, 1, BF16)
    br1_in = send(br1, swap_core)
    d, gain_rows = unnorm(bn0, bn1_in, xhat, rstd, norm_gain)
    grad_taps = taps(img, d)
    br0 = project([after(b, grad_taps) for b in mapped], ws, 1, 0, BF16)

    small = jnp.concatenate([grad_taps, jnp.sum(gain_rows, axis=0, keepdims=True), back_gamma, back_beta], axis=0)
    small = jnp.pad(small, ((0, 6), (0, 0))).astype(BF16)
    small = jnp.concatenate([small[:32], small[32:]], axis=1)
    half = lax.dynamic_slice_in_dim(small, c * 16, 16, axis=0)
    give = lax.dynamic_slice_in_dim(small, 16 - c * 16, 16, axis=0)
    small = add_up([half, send(give, swap_core)]).astype(BF16)
    grad_features = unstem(after(d, br0), dw_kernel, cot, None, 0)
    part = add_up([sent[0]] + [after(s, grad_taps) for s in sent[1:]]).astype(BF16)
    part = [part[k * piece : (k + 1) * piece] for k in range(4)]
    part = [part[0]] + [send(part[k], minor(SHIFTS[k])) for k in (1, 2, 3)]
    small = add_up([small] + [send(small, major(s)) for s in SHIFTS[1:]]).astype(BF16)
    small = [small] + [send(small, minor(s)) for s in SHIFTS[1:]]
    part = add_up([part[0]] + [after(s, grad_features) for s in part[1:]])
    grad_features = unstem(d, dw_kernel, cot, grad_features, HALF)
    block_out = finish(img, br0, br1_in)
    small = add_up([small[0]] + [after(s, grad_features) for s in small[1:]])
    merged = jnp.concatenate([part, small], axis=0).astype(BF16)
    total = add_up([merged] + [send(merged, along_y(s)) for s in SHIFTS[1:]])
    inverse = 1.0 / (features.shape[0] * lax.axis_size("rep") * lax.axis_size("shard"))
    total = (total * inverse).astype(BF16)
    small = total[piece:]
    total = total[:piece]
    other = send(total, swap_zlo)
    total = jnp.where(zl == 0, jnp.concatenate([total, other], axis=0), jnp.concatenate([other, total], axis=0))
    total = jnp.concatenate([total, small], axis=0)
    other = send(total, swap_core)
    lo = jnp.where(c == 0, total, other)
    hi = jnp.where(c == 0, other, total)
    rows = 2 * piece
    total = jnp.concatenate([lo[:rows], hi[:rows]], axis=0).astype(F32)
    small = jnp.concatenate([lo[rows:], hi[rows:]], axis=0).astype(F32)
    small = jnp.concatenate([small[:, :C], small[:, C:]], axis=0)
    return (
        block_out[None],
        grad_features[None],
        small[:49],
        small[49],
        total[:, :C],
        small[50:54].reshape(hid),
        small[54:58].reshape(hid),
        total[:, C:],
    )


def solution(mesh):
    data = P(AXES, None, None, None)
    rows = P("shard", None)
    return jax.shard_map(
        shards,
        mesh=mesh,
        in_specs=(data, data, P(), P(), rows, P(), P(), rows),
        out_specs=(data, data, P(), P(), rows, P(), P(), rows),
        check_vma=False,
    )
```

```python
import jax
import jax.numpy as jnp
from jax import lax
from jax.sharding import PartitionSpec as P
from jax.experimental import pallas as pl
from jax.experimental.pallas import tpu as pltpu

S, W, C = 28, 32, 704
T = S * W
CB = 128
NCB = 6
HEAD = 8
CP = NCB * CB
HALF = NCB // 2
SLOT = 384
F32, BF16 = jnp.float32, jnp.bfloat16


def params(mib=48, n=1):
    return pltpu.CompilerParams(vmem_limit_bytes=mib * 1024 * 1024, dimension_semantics=("arbitrary",) * n)


def cost(flops, nbytes):
    return pl.CostEstimate(flops=int(flops), bytes_accessed=int(nbytes), transcendentals=0)


def conv_taps(src, k_ref, dst, flip):
    def cols(jv, carry):
        base = jv * 8
        acc = [None] * S
        for b in range(7):
            taps = []
            for a in range(7):
                at = (6 - a) * 7 + (6 - b) if flip else a * 7 + b
                taps.append(jnp.broadcast_to(k_ref[pl.ds(at, 1), :], (8, CB)))
            for r in range(S):
                v = src[pl.ds(r * W + HEAD + b - 3 + base, 8), :]
                for a in range(7):
                    i = r + 3 - a
                    if 0 <= i < S:
                        t = taps[a] * v
                        acc[i] = t if acc[i] is None else acc[i] + t
        for i in range(S):
            dst[pl.ds(i * W + base, 8), :] = acc[i]
        return carry

    lax.fori_loop(0, W // 8, cols, 0)


def load_map(x_ref, pad):
    for i in range(S):
        pad[pl.ds(HEAD + i * W, S), :] = x_ref[i].astype(F32)


def stem_first_kernel(x_ref, k_ref, filt_ref, pad):
    @pl.when(pl.program_id(0) == 0)
    def _():
        pad[...] = jnp.zeros_like(pad)

    load_map(x_ref, pad)
    conv_taps(pad, k_ref, filt_ref.at[0], False)


def stem_first(x, k):
    return pl.pallas_call(
        stem_first_kernel,
        name="stem_first",
        grid=(HALF,),
        in_specs=[pl.BlockSpec((S, S, CB), lambda c: (0, 0, c)), pl.BlockSpec((49, CB), lambda c: (0, c))],
        out_specs=pl.BlockSpec((1, T, CB), lambda c: (c, 0, 0)),
        out_shape=jax.ShapeDtypeStruct((HALF, T, CB), F32),
        scratch_shapes=[pltpu.VMEM((T + 2 * HEAD, CB), F32)],
        compiler_params=params(60),
        cost_estimate=cost(T * C, T * C),
    )(x, k)


def stem_kernel(x_ref, k_ref, gain_ref, first_ref, normed_ref, xhat_ref, rstd_ref, pad, filt):
    cb = pl.program_id(0)

    @pl.when(cb == 0)
    def _():
        pad[...] = jnp.zeros_like(pad)

    load_map(x_ref, pad)
    conv_taps(pad, k_ref, filt.at[cb], False)

    @pl.when(cb == HALF - 1)
    def _():
        lane = lax.broadcasted_iota(jnp.int32, (W, CB), 1)
        row = lax.broadcasted_iota(jnp.int32, (W, CB), 0)
        last = lane < C - (NCB - 1) * CB
        inside = row < S

        def rows(i, carry):
            at = pl.ds(pl.multiple_of(i * W, W), W)
            v = [first_ref[c, at, :] for c in range(HALF)] + [filt[c, at, :] for c in range(NCB - HALF)]
            v[-1] = jnp.where(last, v[-1], 0.0)
            total = v[0]
            for c in range(1, NCB):
                total = total + v[c]
            mean = jnp.sum(total, axis=1, keepdims=True) * (1.0 / C)
            d = [u - mean for u in v]
            d[-1] = jnp.where(last, d[-1], 0.0)
            total = d[0] * d[0]
            for c in range(1, NCB):
                total = total + d[c] * d[c]
            spread = jnp.sum(total, axis=1, keepdims=True) * (1.0 / C)
            rstd = jnp.broadcast_to(lax.rsqrt(spread + 1e-06), (W, CB))
            rstd_ref[at, :] = rstd
            for c in range(NCB):
                n = min(CB, C - c * CB)
                xh = jnp.where(inside, d[c] * rstd, 0.0)
                xhat_ref[at, c * CB : c * CB + n] = xh[:, :n]
                g = jnp.broadcast_to(gain_ref[0:1, c * CB : (c + 1) * CB], (W, CB))
                normed_ref[at, c * CB : (c + 1) * CB] = (xh * g).astype(BF16)
            return carry

        lax.fori_loop(0, S // 4, lambda i, carry: [rows(4 * i + j, carry) for j in range(4)][-1], 0)


def stem(x, k, gain, first):
    return pl.pallas_call(
        stem_kernel,
        name="stem",
        grid=(NCB - HALF,),
        in_specs=[
            pl.BlockSpec((S, S, CB), lambda c: (0, 0, c + HALF)),
            pl.BlockSpec((49, CB), lambda c: (0, c + HALF)),
            pl.BlockSpec((1, CP), lambda c: (0, 0)),
            pl.BlockSpec((HALF, T, CB), lambda c: (0, 0, 0)),
        ],
        out_specs=[
            pl.BlockSpec((T, CP), lambda c: (0, 0)),
            pl.BlockSpec((T, C), lambda c: (0, 0)),
            pl.BlockSpec((T, CB), lambda c: (0, 0)),
        ],
        out_shape=[
            jax.ShapeDtypeStruct((T, CP), BF16),
            jax.ShapeDtypeStruct((T, C), F32),
            jax.ShapeDtypeStruct((T, CB), F32),
        ],
        scratch_shapes=[pltpu.VMEM((T + 2 * HEAD, CB), F32), pltpu.VMEM((NCB - HALF, T, CB), F32)],
        compiler_params=params(60),
        cost_estimate=cost(T * C, T * C),
    )(x, k, jnp.pad(gain, (0, CP - C)).reshape(1, CP), first)


def widen_kernel(x_ref, y_ref):
    zero = jnp.zeros((W - S, C), F32)
    y_ref[:, C:] = jnp.zeros((T, CP - C), BF16)
    for i in range(S):
        y_ref[pl.ds(i * W, W), :C] = jnp.concatenate([x_ref[i].astype(F32), zero], axis=0).astype(BF16)


def widen(x):
    return pl.pallas_call(
        widen_kernel,
        name="widen",
        out_shape=jax.ShapeDtypeStruct((T, CP), BF16),
        compiler_params=pltpu.CompilerParams(vmem_limit_bytes=60 * 1024 * 1024),
        cost_estimate=cost(T * C, T * C),
    )(x)


def gelu_pair(x):
    mag = jnp.abs(x)
    e = jnp.exp(-0.5 * (x * x))
    t = 1.0 / (1.0 + (0.3275911 * 0.7071067811865476) * mag)
    poly = (((1.061405429 * t - 1.453152027) * t + 1.421413741) * t - 0.284496736) * t + 0.254829592
    tail = (0.5 * poly) * (t * e)
    cdf = jnp.where(x < 0.0, tail, 1.0 - tail)
    return x * cdf, cdf + (0.3989422804014327 * x) * e


def split_rows(w):
    zero = jnp.zeros((SLOT - w.shape[0], C), BF16)
    return jnp.concatenate([w[:, :C], zero], axis=0), jnp.concatenate([w[:, C:], zero], axis=0)


ROWS = 448
STEPS = T // ROWS


def hidden_kernel(n0, n1, c0, c1, w_ref, *refs):
    act_ref, slope_ref, back_ref, stat_ref = refs[-4:]
    g = pl.program_id(0)
    nt = (((1,), (1,)), ((), ()))

    def body(n_ref, c_ref):
        we, wr = split_rows(w_ref[...])
        pre = lax.dot_general(n_ref[:, :C], we, nt, preferred_element_type=F32)
        dm = lax.dot_general(c_ref[:, :C], wr, nt, preferred_element_type=F32)
        act, slope = gelu_pair(pre)
        act_ref[0] = act.astype(BF16)
        slope_ref[0] = slope.astype(BF16)
        back_ref[0] = dm.astype(BF16)
        e2 = jnp.sum(act * act, axis=0, keepdims=True)
        s1 = jnp.sum(dm * act, axis=0, keepdims=True)
        s0 = jnp.sum(dm, axis=0, keepdims=True)
        stat_ref[0, 0] += jnp.concatenate([e2, s1, s0, jnp.zeros((5, SLOT), F32)], axis=0)

    @pl.when(g % STEPS == 0)
    def _():
        stat_ref[...] = jnp.zeros_like(stat_ref)

    @pl.when(g < STEPS)
    def _():
        body(n0, c0)

    @pl.when(g >= STEPS)
    def _():
        body(n1, c1)


def hidden(n0, n1, c0, c1, w, slot, old):
    wide = pl.BlockSpec((1, ROWS, SLOT), lambda g: (slot, g, 0))
    one = pl.BlockSpec((ROWS, CP), lambda g: (jnp.minimum(g, STEPS - 1), 0))
    two = pl.BlockSpec((ROWS, CP), lambda g: (jnp.maximum(g - STEPS, 0), 0))
    return pl.pallas_call(
        hidden_kernel,
        name="hidden",
        grid=(2 * STEPS,),
        in_specs=[one, two, one, two, pl.BlockSpec(w.shape, lambda g: (0, 0))]
        + [pl.BlockSpec(memory_space=pl.ANY)] * len(old),
        out_specs=[wide, wide, wide, pl.BlockSpec((1, 1, 8, SLOT), lambda g: (slot, g // STEPS, 0, 0))],
        out_shape=[jax.ShapeDtypeStruct((4, 2 * T, SLOT), BF16)] * 3 + [jax.ShapeDtypeStruct((4, 2, 8, SLOT), F32)],
        input_output_aliases={5 + i: i for i in range(len(old))},
        compiler_params=params(60),
        cost_estimate=cost(T * C, T * C),
    )(n0, n1, c0, c1, w, *old)


def full_sum(v):
    return jnp.sum(jnp.sum(jnp.sum(v, axis=0), axis=0, keepdims=True), axis=1, keepdims=True)


def tally_kernel(stat_ref, gamma_ref, valid_ref, o_ref):
    rows = []
    for im in range(2):
        energy = jnp.sqrt(stat_ref[:, im, 0:1, :] + 1e-06)
        rows.append(jnp.broadcast_to(full_sum(energy * valid_ref[...]), (1, CB)))
        rows.append(jnp.broadcast_to(full_sum(gamma_ref[...] * stat_ref[:, im, 1:2, :] * energy), (1, CB)))
    o_ref[...] = jnp.concatenate(rows + [jnp.zeros((4, CB), F32)], axis=0)


def tally(stat, gamma, valid):
    return pl.pallas_call(
        tally_kernel,
        name="tally",
        out_shape=jax.ShapeDtypeStruct((8, CB), F32),
        compiler_params=pltpu.CompilerParams(vmem_limit_bytes=60 * 1024 * 1024),
        cost_estimate=cost(T * C, T * C),
    )(stat, gamma, valid)


def vectors_kernel(stat_ref, gamma_ref, beta_ref, mine, theirs, v_ref, g_ref, *, hid):
    gamma = gamma_ref[...]
    back_gamma = back_beta = 0.0
    for im in range(2):
        far = 2 * (1 - im)
        e_all = (mine[2 * im : 2 * im + 1, 0:1] + theirs[far : far + 1, 0:1]).reshape(1, 1, 1)
        d_all = (mine[2 * im + 1 : 2 * im + 2, 0:1] + theirs[far + 1 : far + 2, 0:1]).reshape(1, 1, 1)
        energy = jnp.sqrt(stat_ref[:, im, 0:1, :] + 1e-06)
        s1 = stat_ref[:, im, 1:2, :]
        inv = 1.0 / (e_all * (1.0 / hid) + 1e-06)
        ratio = energy * inv
        pull = (gamma * s1 * inv - d_all * (1.0 / hid) * inv * inv) / energy
        v_ref[:, im, 0:1, :] = 1.0 + gamma * ratio
        v_ref[:, im, 1:2, :] = pull
        v_ref[:, im, 2:3, :] = beta_ref[...]
        v_ref[:, im, 3:8, :] = jnp.zeros((4, 5, SLOT), F32)
        back_gamma = back_gamma + ratio * s1
        back_beta = back_beta + stat_ref[:, im, 2:3, :]
    g_ref[:, 0:1, :] = back_gamma
    g_ref[:, 1:2, :] = back_beta
    g_ref[:, 2:8, :] = jnp.zeros((4, 6, SLOT), F32)


def vectors(stat, gamma, beta, mine, theirs, hid):
    return pl.pallas_call(
        lambda *refs: vectors_kernel(*refs, hid=hid),
        name="vectors",
        out_shape=[jax.ShapeDtypeStruct((4, 2, 8, SLOT), F32), jax.ShapeDtypeStruct((4, 8, SLOT), F32)],
        compiler_params=pltpu.CompilerParams(vmem_limit_bytes=60 * 1024 * 1024),
        cost_estimate=cost(T * C, T * C),
    )(stat, gamma, beta, mine, theirs)


def mix_kernel(act, slope, back, n0, n1, c0, c1, wa, wb, v_ref, *refs):
    ta, tb, br0, br1, bn0, bn1, te, tr, we, wr, acc_br, acc_bn = refs[-12:]
    old = refs[:-12]
    s = pl.program_id(0)
    im = pl.program_id(1)
    tn = (((0,), (0,)), ((), ()))

    for k, w in enumerate((wa, wb)):

        @pl.when((s == k) & (im == 0))
        def _():
            we[...], wr[...] = split_rows(w[...])

    @pl.when(s == 0)
    def _():
        if old:
            acc_br[im] = old[0][0].astype(F32)
            acc_bn[im] = old[1][0].astype(F32)
        else:
            acc_br[im] = jnp.zeros((T, C), F32)
            acc_bn[im] = jnp.zeros((T, C), F32)

    v = v_ref[0, 0]
    p, q, beta = v[0:1], v[1:2], v[2:3]

    def body(n_ref, c_ref):
        a = act[0].astype(F32)
        mapped = (a * p + beta).astype(BF16)
        bp = ((back[0].astype(F32) * p + a * q) * slope[0].astype(F32)).astype(BF16)
        acc_br[im] += lax.dot(mapped, wr[...], preferred_element_type=F32)
        acc_bn[im] += lax.dot(bp, we[...], preferred_element_type=F32)
        e = lax.dot_general(bp, n_ref[:, :C], tn, preferred_element_type=F32)
        r = lax.dot_general(mapped, c_ref[:, :C], tn, preferred_element_type=F32)
        return e, r

    @pl.when(im == 0)
    def _():
        te[...], tr[...] = body(n0, c0)

    @pl.when(im == 1)
    def _():
        e, r = body(n1, c1)
        n = ta.shape[0]
        te[...] += e
        tr[...] += r
        for k, t in enumerate((ta, tb)):

            @pl.when(s == k)
            def _():
                t[:, :C] = te[:n, :].astype(BF16)
                t[:, C:] = tr[:n, :].astype(BF16)

    for k, (br, bn) in enumerate(((br0, bn0), (br1, bn1))):

        @pl.when((s == 1) & (im == k))
        def _():
            for o, acc in ((br, acc_br), (bn, acc_bn)):
                if len(o.shape) == 3:
                    o[k] = acc[k].astype(BF16)
                else:
                    o[:, :C] = acc[k].astype(BF16)
                    o[:, C:] = jnp.zeros((T, CP - C), BF16)


def mix_first_kernel(*refs):
    ins, (ta, tb, br, bn), scratch = refs[:10], refs[10:14], refs[14:]
    mix_kernel(*ins, ta, tb, br, br, bn, bn, *scratch)


def mix(h, n0, n1, c0, c1, wa, wb, vecs, first, n, old):
    slot = lambda s: first - 2 * s
    once = pl.Buffered(1)
    wide = pl.BlockSpec((1, T, SLOT), lambda s, g: (slot(s), g, 0))
    full = pl.BlockSpec((T, CP), lambda s, g: (0, 0), pipeline_mode=once)
    rows = pl.BlockSpec((n, 2 * C), lambda s, g: (0, 0), pipeline_mode=once)
    part = pl.BlockSpec((1, T, C), lambda s, g: (g, 0, 0))
    both = pl.BlockSpec((2, T, C), lambda s, g: (0, 0, 0))
    terms = jax.ShapeDtypeStruct((n, 2 * C), BF16)
    if old:
        outs, shapes = [full] * 4, [jax.ShapeDtypeStruct((T, CP), BF16)] * 4
    else:
        outs, shapes = [both] * 2, [jax.ShapeDtypeStruct((2, T, C), BF16)] * 2
    return pl.pallas_call(
        mix_kernel if old else mix_first_kernel,
        name="mix",
        grid=(2, 2),
        in_specs=[wide] * 3
        + [full] * 4
        + [rows, rows, pl.BlockSpec((1, 1, 8, SLOT), lambda s, g: (slot(s), g, 0, 0))]
        + [part] * len(old),
        out_specs=[rows, rows] + outs,
        out_shape=[terms, terms] + shapes,
        scratch_shapes=[pltpu.VMEM((SLOT, C), F32)] * 2
        + [pltpu.VMEM((SLOT, C), BF16)] * 2
        + [pltpu.VMEM((2, T, C), F32)] * 2,
        compiler_params=params(60, 2),
        cost_estimate=cost(T * C, T * C),
    )(h[0], h[1], h[2], n0, n1, c0, c1, wa, wb, vecs, *old)


def unnorm_kernel(b0, b1, xhat, rstd, gain, d_ref, gg_ref, *, step):
    @pl.when(pl.program_id(0) == 0)
    def _():
        gg_ref[...] = jnp.zeros_like(gg_ref)

    def rows(i, carry):
        at = pl.ds(pl.multiple_of(i * W, W), W)
        bn = b0[at, :C].astype(F32) + b1[at, :C].astype(F32)
        xh = xhat[at, :]
        g = bn * gain[0:1, :]
        m1 = jnp.sum(g, axis=1, keepdims=True) * (1.0 / C)
        m2 = jnp.sum(g * xh, axis=1, keepdims=True) * (1.0 / C)
        r = rstd[at, 0:1]
        d_ref[at, :] = r * (g - m1 - xh * m2)
        gg_ref[...] += jnp.sum((bn * xh).reshape(W // 8, 8, C), axis=0)
        return carry

    lax.fori_loop(0, step // W, rows, 0, unroll=True)


def unnorm(b0, b1, xhat, rstd, gain):
    step = T // 4
    full = pl.BlockSpec((step, C), lambda r: (r, 0))
    wide = pl.BlockSpec((step, CP), lambda r: (r, 0))
    return pl.pallas_call(
        lambda *refs: unnorm_kernel(*refs, step=step),
        name="unnorm",
        grid=(T // step,),
        in_specs=[wide, wide, full, pl.BlockSpec((step, CB), lambda r: (r, 0)), pl.BlockSpec((1, C), lambda r: (0, 0))],
        out_specs=[full, pl.BlockSpec((8, C), lambda r: (0, 0))],
        out_shape=[jax.ShapeDtypeStruct((T, C), F32), jax.ShapeDtypeStruct((8, C), F32)],
        compiler_params=params(60),
        cost_estimate=cost(T * C, T * C),
    )(b0, b1, xhat, rstd, gain.reshape(1, C))


def taps_kernel(x_ref, d_ref, g_ref, pad):
    @pl.when(pl.program_id(0) == 0)
    def _():
        pad[...] = jnp.zeros_like(pad)

    for i in range(S):
        pad[pl.ds(HEAD + i * W, S), :] = x_ref[i].astype(F32)

    for b in range(7):
        def cols(jv, acc):
            base = jv * 8
            acc = list(acc)
            d = {}
            for r in range(S):
                if r == 0:
                    for i in range(4):
                        d[i] = d_ref[pl.ds(i * W + base, 8), :]
                elif r + 3 < S:
                    d[r + 3] = d_ref[pl.ds((r + 3) * W + base, 8), :]
                v = pad[pl.ds(r * W + HEAD + b - 3 + base, 8), :]
                for a in range(7):
                    i = r + 3 - a
                    if 0 <= i < S:
                        acc[a] = acc[a] + d[i] * v
            return tuple(acc)

        acc = lax.fori_loop(0, W // 8, cols, (jnp.zeros((8, CB), F32),) * 7)
        for a in range(7):
            g_ref[pl.ds(a * 7 + b, 1), :] = jnp.sum(acc[a], axis=0, keepdims=True)


def taps(x, d):
    return pl.pallas_call(
        taps_kernel,
        name="taps",
        grid=(NCB,),
        in_specs=[pl.BlockSpec((S, S, CB), lambda c: (0, 0, c)), pl.BlockSpec((T, CB), lambda c: (0, c))],
        out_specs=pl.BlockSpec((49, CB), lambda c: (0, c)),
        out_shape=jax.ShapeDtypeStruct((49, C), F32),
        scratch_shapes=[pltpu.VMEM((T + 2 * HEAD, CB), F32)],
        compiler_params=params(60),
        cost_estimate=cost(T * C, T * C),
    )(x, d)


def unstem_kernel(d_ref, k_ref, c_ref, old_ref, o_ref, pad, res):
    @pl.when(pl.program_id(0) == 0)
    def _():
        pad[...] = jnp.zeros_like(pad)

    pad[pl.ds(HEAD, T), :] = d_ref[...]
    conv_taps(pad, k_ref, res, True)
    for i in range(S):
        o_ref[i] = (c_ref[i].astype(F32) + res[pl.ds(i * W, S), :]).astype(BF16)


def unstem(d, k, cot, old, at):
    return pl.pallas_call(
        unstem_kernel if old is not None else (lambda d, k, c, *r: unstem_kernel(d, k, c, None, *r)),
        name="unstem",
        grid=(HALF,),
        in_specs=[
            pl.BlockSpec((T, CB), lambda c: (0, c + at)),
            pl.BlockSpec((49, CB), lambda c: (0, c + at)),
            pl.BlockSpec((S, S, CB), lambda c: (0, 0, c + at)),
        ]
        + ([pl.BlockSpec(memory_space=pl.ANY)] if old is not None else []),
        out_specs=pl.BlockSpec((S, S, CB), lambda c: (0, 0, c + at)),
        out_shape=jax.ShapeDtypeStruct((S, S, C), BF16),
        scratch_shapes=[pltpu.VMEM((T + 2 * HEAD, CB), F32), pltpu.VMEM((T, CB), F32)],
        input_output_aliases={3: 0} if old is not None else {},
        compiler_params=params(60),
        cost_estimate=cost(T * C, T * C),
    )(d, k, cot, *([old] if old is not None else []))


def finish_kernel(x_ref, b0, b1, o_ref):
    for i in range(S):
        at = pl.ds(i * W, W)
        t = b0[at, :].astype(F32) + b1[at, :].astype(F32)
        o_ref[i] = (x_ref[i].astype(F32) + t[:S, :C]).astype(BF16)


def finish(x, b0, b1):
    return pl.pallas_call(
        finish_kernel,
        name="finish",
        out_shape=jax.ShapeDtypeStruct((S, S, C), BF16),
        compiler_params=pltpu.CompilerParams(vmem_limit_bytes=60 * 1024 * 1024),
        cost_estimate=cost(T * C, T * C),
    )(x, b0, b1)


SHIFTS = (0, -1, 1, 2)
AXES = ("rep", "shard")


def place(x, y, z, c):
    return ((y * 2 + z % 2) * 2 + c) * 8 + x * 2 + z // 2


def moves(fn):
    pairs = []
    for x in range(4):
        for y in range(4):
            for z in range(4):
                for c in range(2):
                    nx, ny, nz, nc = fn(x, y, z, c)
                    pairs.append((place(x, y, z, c), place(nx % 4, ny % 4, nz % 4, nc)))
    return pairs


def along_x(d):
    return lambda x, y, z, c: (x + d, y, z, c)


def along_y(d):
    return lambda x, y, z, c: (x, y + d, z, c)


def minor(d):
    return lambda x, y, z, c: (x, y, z + d, c) if c == 0 else (x + d, y, z, c)


def major(d):
    return lambda x, y, z, c: (x + d, y, z, c) if c == 0 else (x, y, z + d, c)


def swap_core(x, y, z, c):
    return (x, y, z, 1 - c)


def swap_zlo(x, y, z, c):
    return (x, y, z + 1 - 2 * (z % 2), c)


def send(v, fn):
    return lax.ppermute(v, AXES, moves(fn))


def spread(v, axis_fn):
    return [v] + [send(v, axis_fn(-d)) for d in SHIFTS[1:]]


def turn(v, start):
    size = v.shape[0]
    return lax.dynamic_slice_in_dim(jnp.concatenate([v, v], axis=0), start, size, axis=0)


ORDER = (0, 3, 1, 2)
BACK = (0, 2, 3, 1)


def add_up(parts):
    total = parts[0].astype(F32)
    for g in parts[1:]:
        total = total + g.astype(F32)
    return total


def after(v, *done):
    return lax.optimization_barrier((v,) + done)[0]


def shards(features, cotangent, dw_kernel, norm_gain, w_expand, grn_gamma, grn_beta, w_reduce):
    rep = lax.axis_index("rep")
    shard = lax.axis_index("shard")
    c = rep % 2
    zl = (rep // 2) % 2
    x = shard // 2
    z = (shard % 2) * 2 + zl
    hid = grn_gamma.shape[0]
    piece = hid // 32
    n = 4 * piece
    img = features[0]
    cot = cotangent[0]

    first = c * (2 * piece) + zl * piece
    own = jnp.concatenate([lax.dynamic_slice_in_dim(w, first, piece, axis=0) for w in (w_expand, w_reduce)], axis=1)
    filt = stem_first(img, dw_kernel)
    row = jnp.concatenate(spread(own, minor), axis=0)
    ws = spread(row, major)

    def to_own(v):
        v = lax.dynamic_index_in_dim(v.reshape(4, 2, 2, 2, piece), c, axis=2, keepdims=False).reshape(4, 4, piece)
        v = turn(v, x).transpose(1, 0, 2)
        v = turn(v, z)
        v = jnp.where(c == 0, v.transpose(1, 0, 2), v)
        v = jnp.stack([v[k] for k in ORDER])
        v = jnp.stack([v[:, k] for k in ORDER], axis=1)
        return jnp.pad(v.reshape(1, 4, n), ((0, 0), (0, 0), (0, SLOT - n)))

    def to_all(v):
        v = v[:, :n].reshape(4, 4, piece)
        v = jnp.stack([v[k] for k in BACK])
        v = jnp.stack([v[:, k] for k in BACK], axis=1)
        v = jnp.where(c == 0, v, v.transpose(1, 0, 2))
        v = turn(v, (4 - x) % 4).transpose(1, 0, 2)
        v = turn(v, (4 - z) % 4).transpose(1, 0, 2).reshape(4, 2, 1, 2, piece)
        zero = jnp.zeros_like(v)
        both = jnp.where(c == 0, jnp.concatenate([v, zero], axis=2), jnp.concatenate([zero, v], axis=2))
        return both.reshape(4, hid // 4)

    gamma = to_own(grn_gamma)
    beta = to_own(grn_beta)
    valid = (jnp.arange(SLOT) < n).astype(F32)

    c0 = widen(cot)
    c1 = send(c0, swap_core)
    n0, xhat, rstd = stem(after(img, row, c1), dw_kernel, norm_gain, filt)
    n1 = send(n0, swap_core)
    h = ()
    for j in range(4):
        h = hidden(n0, n1, c0, c1, ws[j], j, h)
    gamma3, beta3 = gamma.reshape(4, 1, SLOT), beta.reshape(4, 1, SLOT)
    mine = tally(h[3], gamma3, valid)
    vecs, back = vectors(h[3], gamma3, beta3, mine, send(mine, swap_core), hid)
    back_gamma = to_all(back[:, 0])
    back_beta = to_all(back[:, 1])
    t3, t1, *part = mix(h, n0, n1, c0, c1, ws[3], ws[1], vecs, 3, n, ())
    sent = [None, send(t1, major(SHIFTS[1])), None, send(t3, major(SHIFTS[3]))]
    t2, t0, br0, br1, bn0, bn1 = mix(h, n0, n1, c0, c1, ws[2], ws[0], vecs, 2, n, part)
    bn1_in = send(bn1, swap_core)
    sent[0], sent[2] = t0, send(t2, major(SHIFTS[2]))
    br1_in = send(br1, swap_core)
    d, gain_rows = unnorm(bn0, bn1_in, xhat, rstd, norm_gain)
    grad_taps = taps(img, d)

    small = jnp.concatenate([grad_taps, jnp.sum(gain_rows, axis=0, keepdims=True), back_gamma, back_beta], axis=0)
    small = jnp.pad(small, ((0, 6), (0, 0))).astype(BF16)
    small = jnp.concatenate([small[:32], small[32:]], axis=1)
    half = lax.dynamic_slice_in_dim(small, c * 16, 16, axis=0)
    give = lax.dynamic_slice_in_dim(small, 16 - c * 16, 16, axis=0)
    small = add_up([half, send(give, swap_core)]).astype(BF16)
    grad_features = unstem(d, dw_kernel, cot, None, 0)
    part = add_up([sent[0]] + [after(s, grad_taps) for s in sent[1:]]).astype(BF16)
    part = [part[k * piece : (k + 1) * piece] for k in range(4)]
    part = [part[0]] + [send(part[k], minor(SHIFTS[k])) for k in (1, 2, 3)]
    small = add_up([small] + [send(small, major(s)) for s in SHIFTS[1:]]).astype(BF16)
    small = [small] + [send(small, minor(s)) for s in SHIFTS[1:]]
    part = add_up([part[0]] + [after(s, grad_features) for s in part[1:]])
    grad_features = unstem(d, dw_kernel, cot, grad_features, HALF)
    block_out = finish(img, br0, br1_in)
    small = add_up([small[0]] + [after(s, grad_features) for s in small[1:]])
    merged = jnp.concatenate([part, small], axis=0).astype(BF16)
    total = add_up([merged] + [send(merged, along_y(s)) for s in SHIFTS[1:]])
    inverse = 1.0 / (features.shape[0] * lax.axis_size("rep") * lax.axis_size("shard"))
    total = (total * inverse).astype(BF16)
    small = total[piece:]
    total = total[:piece]
    other = send(total, swap_zlo)
    total = jnp.where(zl == 0, jnp.concatenate([total, other], axis=0), jnp.concatenate([other, total], axis=0))
    total = jnp.concatenate([total, small], axis=0)
    other = send(total, swap_core)
    lo = jnp.where(c == 0, total, other)
    hi = jnp.where(c == 0, other, total)
    rows = 2 * piece
    total = jnp.concatenate([lo[:rows], hi[:rows]], axis=0).astype(F32)
    small = jnp.concatenate([lo[rows:], hi[rows:]], axis=0).astype(F32)
    small = jnp.concatenate([small[:, :C], small[:, C:]], axis=0)
    return (
        block_out[None],
        grad_features[None],
        small[:49],
        small[49],
        total[:, :C],
        small[50:54].reshape(hid),
        small[54:58].reshape(hid),
        total[:, C:],
    )


def solution(mesh):
    data = P(AXES, None, None, None)
    rows = P("shard", None)
    return jax.shard_map(
        shards,
        mesh=mesh,
        in_specs=(data, data, P(), P(), rows, P(), P(), rows),
        out_specs=(data, data, P(), P(), rows, P(), P(), rows),
        check_vma=False,
    )
```

```python
import jax
import jax.numpy as jnp
from jax import lax
from jax.sharding import PartitionSpec as P
from jax.experimental import pallas as pl
from jax.experimental.pallas import tpu as pltpu

S, W, C = 28, 32, 704
T = S * W
CB = 128
NCB = 6
HEAD = 8
CP = NCB * CB
HALF = NCB // 2
SLOT = 384
F32, BF16 = jnp.float32, jnp.bfloat16


def params(mib=48, n=1):
    return pltpu.CompilerParams(vmem_limit_bytes=mib * 1024 * 1024, dimension_semantics=("arbitrary",) * n)


def cost(flops, nbytes):
    return pl.CostEstimate(flops=int(flops), bytes_accessed=int(nbytes), transcendentals=0)


def conv_taps(src, k_ref, dst, flip):
    def cols(jv, carry):
        base = jv * 8
        acc = [None] * S
        for b in range(7):
            taps = []
            for a in range(7):
                at = (6 - a) * 7 + (6 - b) if flip else a * 7 + b
                taps.append(jnp.broadcast_to(k_ref[pl.ds(at, 1), :], (8, CB)))
            for r in range(S):
                v = src[pl.ds(r * W + HEAD + b - 3 + base, 8), :]
                for a in range(7):
                    i = r + 3 - a
                    if 0 <= i < S:
                        t = taps[a] * v
                        acc[i] = t if acc[i] is None else acc[i] + t
        for i in range(S):
            dst[pl.ds(i * W + base, 8), :] = acc[i]
        return carry

    lax.fori_loop(0, W // 8, cols, 0)


def load_map(x_ref, pad):
    for i in range(S):
        pad[pl.ds(HEAD + i * W, S), :] = x_ref[i].astype(F32)


def conv_kernel(x_ref, k_ref, filt_ref, pad):
    @pl.when(pl.program_id(0) == 0)
    def _():
        pad[...] = jnp.zeros_like(pad)

    load_map(x_ref, pad)
    conv_taps(pad, k_ref, filt_ref.at[0], False)


def conv(x, k, at, count):
    return pl.pallas_call(
        conv_kernel,
        name="conv",
        grid=(count,),
        in_specs=[pl.BlockSpec((S, S, CB), lambda c: (0, 0, c + at)), pl.BlockSpec((49, CB), lambda c: (0, c + at))],
        out_specs=pl.BlockSpec((1, T, CB), lambda c: (c, 0, 0)),
        out_shape=jax.ShapeDtypeStruct((count, T, CB), F32),
        scratch_shapes=[pltpu.VMEM((T + 2 * HEAD, CB), F32)],
        compiler_params=params(60),
        cost_estimate=cost(T * C, T * C),
    )(x, k)


NORM = 224


def norm_kernel(one_ref, two_ref, gain_ref, normed_ref, xhat_ref, rstd_ref):
    lane = lax.broadcasted_iota(jnp.int32, (W, CB), 1)
    row = lax.broadcasted_iota(jnp.int32, (W, CB), 0)
    last = lane < C - (NCB - 1) * CB
    inside = row < S
    for i in range(NORM // W):
        at = slice(i * W, (i + 1) * W)
        v = [r[c, at, :] for r in (one_ref, two_ref) for c in range(r.shape[0])]
        v[-1] = jnp.where(last, v[-1], 0.0)
        total = v[0]
        for c in range(1, NCB):
            total = total + v[c]
        mean = jnp.sum(total, axis=1, keepdims=True) * (1.0 / C)
        d = [u - mean for u in v]
        d[-1] = jnp.where(last, d[-1], 0.0)
        total = d[0] * d[0]
        for c in range(1, NCB):
            total = total + d[c] * d[c]
        spread = jnp.sum(total, axis=1, keepdims=True) * (1.0 / C)
        rstd = jnp.broadcast_to(lax.rsqrt(spread + 1e-06), (W, CB))
        rstd_ref[at, :] = rstd
        for c in range(NCB):
            n = min(CB, C - c * CB)
            xh = jnp.where(inside, d[c] * rstd, 0.0)
            xhat_ref[at, c * CB : c * CB + n] = xh[:, :n]
            g = jnp.broadcast_to(gain_ref[0:1, c * CB : (c + 1) * CB], (W, CB))
            normed_ref[at, c * CB : (c + 1) * CB] = (xh * g).astype(BF16)


def norm(one, two, gain):
    return pl.pallas_call(
        norm_kernel,
        name="norm",
        grid=(T // NORM,),
        in_specs=[
            pl.BlockSpec((one.shape[0], NORM, CB), lambda r: (0, r, 0)),
            pl.BlockSpec((two.shape[0], NORM, CB), lambda r: (0, r, 0)),
            pl.BlockSpec((1, CP), lambda r: (0, 0)),
        ],
        out_specs=[
            pl.BlockSpec((NORM, CP), lambda r: (r, 0)),
            pl.BlockSpec((NORM, C), lambda r: (r, 0)),
            pl.BlockSpec((NORM, CB), lambda r: (r, 0)),
        ],
        out_shape=[
            jax.ShapeDtypeStruct((T, CP), BF16),
            jax.ShapeDtypeStruct((T, C), F32),
            jax.ShapeDtypeStruct((T, CB), F32),
        ],
        compiler_params=params(60),
        cost_estimate=cost(T * C, T * C),
    )(one, two, jnp.pad(gain, (0, CP - C)).reshape(1, CP))


def widen_kernel(x_ref, y_ref):
    zero = jnp.zeros((W - S, C), F32)
    y_ref[:, C:] = jnp.zeros((T, CP - C), BF16)
    for i in range(S):
        y_ref[pl.ds(i * W, W), :C] = jnp.concatenate([x_ref[i].astype(F32), zero], axis=0).astype(BF16)


def widen(x):
    return pl.pallas_call(
        widen_kernel,
        name="widen",
        out_shape=jax.ShapeDtypeStruct((T, CP), BF16),
        compiler_params=pltpu.CompilerParams(vmem_limit_bytes=60 * 1024 * 1024),
        cost_estimate=cost(T * C, T * C),
    )(x)


def gelu_pair(x):
    mag = jnp.abs(x)
    e = jnp.exp(-0.5 * (x * x))
    t = 1.0 / (1.0 + (0.3275911 * 0.7071067811865476) * mag)
    poly = (((1.061405429 * t - 1.453152027) * t + 1.421413741) * t - 0.284496736) * t + 0.254829592
    tail = (0.5 * poly) * (t * e)
    cdf = jnp.where(x < 0.0, tail, 1.0 - tail)
    return x * cdf, cdf + (0.3989422804014327 * x) * e


def split_rows(w):
    zero = jnp.zeros((SLOT - w.shape[0], C), BF16)
    return jnp.concatenate([w[:, :C], zero], axis=0), jnp.concatenate([w[:, C:], zero], axis=0)


ROWS = 448
STEPS = T // ROWS


def hidden_kernel(n0, n1, c0, c1, *refs, count):
    ws = refs[:count]
    act_ref, slope_ref, back_ref, stat_ref = refs[-4:]
    g = pl.program_id(0)
    nt = (((1,), (1,)), ((), ()))

    def body(n_ref, c_ref):
        for k in range(count):
            we, wr = split_rows(ws[k][...])
            pre = lax.dot_general(n_ref[:, :C], we, nt, preferred_element_type=F32)
            dm = lax.dot_general(c_ref[:, :C], wr, nt, preferred_element_type=F32)
            act, slope = gelu_pair(pre)
            act_ref[k] = act.astype(BF16)
            slope_ref[k] = slope.astype(BF16)
            back_ref[k] = dm.astype(BF16)
            e2 = jnp.sum(act * act, axis=0, keepdims=True)
            s1 = jnp.sum(dm * act, axis=0, keepdims=True)
            s0 = jnp.sum(dm, axis=0, keepdims=True)
            stat_ref[k, 0] += jnp.concatenate([e2, s1, s0, jnp.zeros((5, SLOT), F32)], axis=0)

    @pl.when(g % STEPS == 0)
    def _():
        stat_ref[...] = jnp.zeros_like(stat_ref)

    @pl.when(g < STEPS)
    def _():
        body(n0, c0)

    @pl.when(g >= STEPS)
    def _():
        body(n1, c1)


def hidden(n0, n1, c0, c1, ws):
    count = len(ws)
    wide = pl.BlockSpec((count, ROWS, SLOT), lambda g: (0, g, 0))
    one = pl.BlockSpec((ROWS, CP), lambda g: (jnp.minimum(g, STEPS - 1), 0))
    two = pl.BlockSpec((ROWS, CP), lambda g: (jnp.maximum(g - STEPS, 0), 0))
    return pl.pallas_call(
        lambda *refs: hidden_kernel(*refs, count=count),
        name="hidden",
        grid=(2 * STEPS,),
        in_specs=[one, two, one, two] + [pl.BlockSpec(ws[0].shape, lambda g: (0, 0))] * count,
        out_specs=[wide, wide, wide, pl.BlockSpec((count, 1, 8, SLOT), lambda g: (0, g // STEPS, 0, 0))],
        out_shape=[jax.ShapeDtypeStruct((count, 2 * T, SLOT), BF16)] * 3
        + [jax.ShapeDtypeStruct((count, 2, 8, SLOT), F32)],
        compiler_params=params(60),
        cost_estimate=cost(T * C, T * C),
    )(n0, n1, c0, c1, *ws)


def full_sum(v):
    return jnp.sum(jnp.sum(jnp.sum(v, axis=0), axis=0, keepdims=True), axis=1, keepdims=True)


def tally_kernel(stat_ref, gamma_ref, valid_ref, o_ref):
    rows = []
    for im in range(2):
        energy = jnp.sqrt(stat_ref[:, im, 0:1, :] + 1e-06)
        rows.append(jnp.broadcast_to(full_sum(energy * valid_ref[...]), (1, CB)))
        rows.append(jnp.broadcast_to(full_sum(gamma_ref[...] * stat_ref[:, im, 1:2, :] * energy), (1, CB)))
    o_ref[...] = jnp.concatenate(rows + [jnp.zeros((4, CB), F32)], axis=0)


def tally(stat, gamma, valid):
    return pl.pallas_call(
        tally_kernel,
        name="tally",
        out_shape=jax.ShapeDtypeStruct((8, CB), F32),
        compiler_params=pltpu.CompilerParams(vmem_limit_bytes=60 * 1024 * 1024),
        cost_estimate=cost(T * C, T * C),
    )(stat, gamma, valid)


def vectors_kernel(stat_ref, gamma_ref, beta_ref, mine, theirs, v_ref, g_ref, *, hid):
    gamma = gamma_ref[...]
    back_gamma = back_beta = 0.0
    for im in range(2):
        far = 2 * (1 - im)
        e_all = (mine[2 * im : 2 * im + 1, 0:1] + theirs[far : far + 1, 0:1]).reshape(1, 1, 1)
        d_all = (mine[2 * im + 1 : 2 * im + 2, 0:1] + theirs[far + 1 : far + 2, 0:1]).reshape(1, 1, 1)
        energy = jnp.sqrt(stat_ref[:, im, 0:1, :] + 1e-06)
        s1 = stat_ref[:, im, 1:2, :]
        inv = 1.0 / (e_all * (1.0 / hid) + 1e-06)
        ratio = energy * inv
        pull = (gamma * s1 * inv - d_all * (1.0 / hid) * inv * inv) / energy
        v_ref[:, im, 0:1, :] = 1.0 + gamma * ratio
        v_ref[:, im, 1:2, :] = pull
        v_ref[:, im, 2:3, :] = beta_ref[...]
        v_ref[:, im, 3:8, :] = jnp.zeros((4, 5, SLOT), F32)
        back_gamma = back_gamma + ratio * s1
        back_beta = back_beta + stat_ref[:, im, 2:3, :]
    g_ref[:, 0:1, :] = back_gamma
    g_ref[:, 1:2, :] = back_beta
    g_ref[:, 2:8, :] = jnp.zeros((4, 6, SLOT), F32)


def vectors(stat, gamma, beta, mine, theirs, hid):
    return pl.pallas_call(
        lambda *refs: vectors_kernel(*refs, hid=hid),
        name="vectors",
        out_shape=[jax.ShapeDtypeStruct((4, 2, 8, SLOT), F32), jax.ShapeDtypeStruct((4, 8, SLOT), F32)],
        compiler_params=pltpu.CompilerParams(vmem_limit_bytes=60 * 1024 * 1024),
        cost_estimate=cost(T * C, T * C),
    )(stat, gamma, beta, mine, theirs)


def mix_kernel(*refs, count, fresh):
    acts, slopes, backs = refs[:count], refs[count : 2 * count], refs[2 * count : 3 * count]
    n0, n1, c0, c1, wa, wb, v_ref = refs[3 * count : 3 * count + 7]
    rest = refs[3 * count + 7 :]
    old, rest = ([], rest) if fresh else (rest[:2], rest[2:])
    ta, tb, *outs, te, tr, we, wr = rest
    im = pl.program_id(0)
    tn = (((0,), (0,)), ((), ()))

    @pl.when(im == 0)
    def _():
        for k, w in enumerate((wa, wb)):
            we[k * SLOT : (k + 1) * SLOT, :], wr[k * SLOT : (k + 1) * SLOT, :] = split_rows(w[...])

    def pick(rs, k):
        return rs[0][k] if count == 1 else rs[k][0]

    def body(n_ref, c_ref):
        mapped, bp = [], []
        for k in range(2):
            v = v_ref[k, 0]
            p, q, beta = v[0:1], v[1:2], v[2:3]
            a = pick(acts, k).astype(F32)
            mapped.append((a * p + beta).astype(BF16))
            bp.append(((pick(backs, k).astype(F32) * p + a * q) * pick(slopes, k).astype(F32)).astype(BF16))
        mapped = jnp.concatenate(mapped, axis=1)
        bp = jnp.concatenate(bp, axis=1)
        br = lax.dot(mapped, wr[...], preferred_element_type=F32)
        bn = lax.dot(bp, we[...], preferred_element_type=F32)
        e = lax.dot_general(bp, n_ref[:, :C], tn, preferred_element_type=F32)
        r = lax.dot_general(mapped, c_ref[:, :C], tn, preferred_element_type=F32)
        return br, bn, e, r

    def put(br, bn, k):
        if fresh:
            outs[0][0] = br.astype(BF16)
            outs[1][0] = bn.astype(BF16)
        else:
            for o, v, w in ((outs[k], br, old[0]), (outs[2 + k], bn, old[1])):
                o[:, :C] = (v + w[0].astype(F32)).astype(BF16)
                o[:, C:] = jnp.zeros((T, CP - C), BF16)

    @pl.when(im == 0)
    def _():
        br, bn, te[...], tr[...] = body(n0, c0)
        put(br, bn, 0)

    @pl.when(im == 1)
    def _():
        br, bn, e, r = body(n1, c1)
        put(br, bn, 1)
        e = te[...] + e
        r = tr[...] + r
        n = ta.shape[0]
        for k, t in enumerate((ta, tb)):
            t[:, :C] = e[k * SLOT : k * SLOT + n].astype(BF16)
            t[:, C:] = r[k * SLOT : k * SLOT + n].astype(BF16)


def mix(sets, n0, n1, c0, c1, wa, wb, vecs, n, old):
    once = pl.Buffered(1)
    if len(sets) == 1:
        h, at = sets[0]
        acts = [(h[i], pl.BlockSpec((2, T, SLOT), lambda g: (at // 2, g, 0))) for i in range(3)]
    else:
        acts = [
            (h[i], pl.BlockSpec((1, T, SLOT), lambda g, at=at: (at, g, 0))) for i in range(3) for h, at in sets
        ]
    full = pl.BlockSpec((T, CP), lambda g: (0, 0), pipeline_mode=once)
    rows = pl.BlockSpec((n, 2 * C), lambda g: (0, 0), pipeline_mode=once)
    part = pl.BlockSpec((1, T, C), lambda g: (g, 0, 0))
    terms = jax.ShapeDtypeStruct((n, 2 * C), BF16)
    if old:
        outs, shapes = [full] * 4, [jax.ShapeDtypeStruct((T, CP), BF16)] * 4
    else:
        outs, shapes = [part] * 2, [jax.ShapeDtypeStruct((2, T, C), BF16)] * 2
    return pl.pallas_call(
        lambda *refs: mix_kernel(*refs, count=len(sets), fresh=not old),
        name="mix",
        grid=(2,),
        in_specs=[spec for _, spec in acts]
        + [full] * 4
        + [rows, rows, pl.BlockSpec((2, 1, 8, SLOT), lambda g: (0, g, 0, 0))]
        + [part] * len(old),
        out_specs=[rows, rows] + outs,
        out_shape=[terms, terms] + shapes,
        scratch_shapes=[pltpu.VMEM((2 * SLOT, C), F32)] * 2 + [pltpu.VMEM((2 * SLOT, C), BF16)] * 2,
        compiler_params=params(62),
        cost_estimate=cost(T * C, T * C),
    )(*[v for v, _ in acts], n0, n1, c0, c1, wa, wb, vecs, *old)


def unnorm_kernel(b0, b1, xhat, rstd, gain, d_ref, gg_ref, *, step):
    @pl.when(pl.program_id(0) == 0)
    def _():
        gg_ref[...] = jnp.zeros_like(gg_ref)

    def rows(i, carry):
        at = pl.ds(pl.multiple_of(i * W, W), W)
        bn = b0[at, :C].astype(F32) + b1[at, :C].astype(F32)
        xh = xhat[at, :]
        g = bn * gain[0:1, :]
        m1 = jnp.sum(g, axis=1, keepdims=True) * (1.0 / C)
        m2 = jnp.sum(g * xh, axis=1, keepdims=True) * (1.0 / C)
        r = rstd[at, 0:1]
        d_ref[at, :] = r * (g - m1 - xh * m2)
        gg_ref[...] += jnp.sum((bn * xh).reshape(W // 8, 8, C), axis=0)
        return carry

    lax.fori_loop(0, step // W, rows, 0, unroll=True)


def unnorm(b0, b1, xhat, rstd, gain):
    step = T // 4
    full = pl.BlockSpec((step, C), lambda r: (r, 0))
    wide = pl.BlockSpec((step, CP), lambda r: (r, 0))
    return pl.pallas_call(
        lambda *refs: unnorm_kernel(*refs, step=step),
        name="unnorm",
        grid=(T // step,),
        in_specs=[wide, wide, full, pl.BlockSpec((step, CB), lambda r: (r, 0)), pl.BlockSpec((1, C), lambda r: (0, 0))],
        out_specs=[full, pl.BlockSpec((8, C), lambda r: (0, 0))],
        out_shape=[jax.ShapeDtypeStruct((T, C), F32), jax.ShapeDtypeStruct((8, C), F32)],
        compiler_params=params(60),
        cost_estimate=cost(T * C, T * C),
    )(b0, b1, xhat, rstd, gain.reshape(1, C))


def taps_kernel(x_ref, d_ref, g_ref, pad):
    @pl.when(pl.program_id(0) == 0)
    def _():
        pad[...] = jnp.zeros_like(pad)

    for i in range(S):
        pad[pl.ds(HEAD + i * W, S), :] = x_ref[i].astype(F32)

    for b in range(7):
        def cols(jv, acc):
            base = jv * 8
            acc = list(acc)
            d = {}
            for r in range(S):
                if r == 0:
                    for i in range(4):
                        d[i] = d_ref[pl.ds(i * W + base, 8), :]
                elif r + 3 < S:
                    d[r + 3] = d_ref[pl.ds((r + 3) * W + base, 8), :]
                v = pad[pl.ds(r * W + HEAD + b - 3 + base, 8), :]
                for a in range(7):
                    i = r + 3 - a
                    if 0 <= i < S:
                        acc[a] = acc[a] + d[i] * v
            return tuple(acc)

        acc = lax.fori_loop(0, W // 8, cols, (jnp.zeros((8, CB), F32),) * 7)
        for a in range(7):
            g_ref[pl.ds(a * 7 + b, 1), :] = jnp.sum(acc[a], axis=0, keepdims=True)


def taps(x, d, at):
    return pl.pallas_call(
        taps_kernel,
        name="taps",
        grid=(HALF,),
        in_specs=[pl.BlockSpec((S, S, CB), lambda c: (0, 0, c + at)), pl.BlockSpec((T, CB), lambda c: (0, c + at))],
        out_specs=pl.BlockSpec((49, CB), lambda c: (0, c)),
        out_shape=jax.ShapeDtypeStruct((49, HALF * CB), F32),
        scratch_shapes=[pltpu.VMEM((T + 2 * HEAD, CB), F32)],
        compiler_params=params(60),
        cost_estimate=cost(T * C, T * C),
    )(x, d)


def unstem_kernel(d_ref, k_ref, c_ref, old_ref, o_ref, pad, res):
    @pl.when(pl.program_id(0) == 0)
    def _():
        pad[...] = jnp.zeros_like(pad)

    pad[pl.ds(HEAD, T), :] = d_ref[...]
    conv_taps(pad, k_ref, res, True)
    for i in range(S):
        o_ref[i] = (c_ref[i].astype(F32) + res[pl.ds(i * W, S), :]).astype(BF16)


def unstem(d, k, cot, old, at):
    return pl.pallas_call(
        unstem_kernel if old is not None else (lambda d, k, c, *r: unstem_kernel(d, k, c, None, *r)),
        name="unstem",
        grid=(2,),
        in_specs=[
            pl.BlockSpec((T, CB), lambda c: (0, c + at)),
            pl.BlockSpec((49, CB), lambda c: (0, c + at)),
            pl.BlockSpec((S, S, CB), lambda c: (0, 0, c + at)),
        ]
        + ([pl.BlockSpec(memory_space=pl.ANY)] if old is not None else []),
        out_specs=pl.BlockSpec((S, S, CB), lambda c: (0, 0, c + at)),
        out_shape=jax.ShapeDtypeStruct((S, S, C), BF16),
        scratch_shapes=[pltpu.VMEM((T + 2 * HEAD, CB), F32), pltpu.VMEM((T, CB), F32)],
        input_output_aliases={3: 0} if old is not None else {},
        compiler_params=params(60),
        cost_estimate=cost(T * C, T * C),
    )(d, k, cot, *([old] if old is not None else []))


def finish_kernel(x_ref, b0, b1, o_ref):
    for i in range(S):
        at = pl.ds(i * W, W)
        t = b0[at, :].astype(F32) + b1[at, :].astype(F32)
        o_ref[i] = (x_ref[i].astype(F32) + t[:S, :C]).astype(BF16)


def finish(x, b0, b1):
    return pl.pallas_call(
        finish_kernel,
        name="finish",
        out_shape=jax.ShapeDtypeStruct((S, S, C), BF16),
        compiler_params=pltpu.CompilerParams(vmem_limit_bytes=60 * 1024 * 1024),
        cost_estimate=cost(T * C, T * C),
    )(x, b0, b1)


SHIFTS = (0, -1, 1, 2)
AXES = ("rep", "shard")


def place(x, y, z, c):
    return ((y * 2 + z % 2) * 2 + c) * 8 + x * 2 + z // 2


def moves(fn):
    pairs = []
    for x in range(4):
        for y in range(4):
            for z in range(4):
                for c in range(2):
                    nx, ny, nz, nc = fn(x, y, z, c)
                    pairs.append((place(x, y, z, c), place(nx % 4, ny % 4, nz % 4, nc)))
    return pairs


def along_x(d):
    return lambda x, y, z, c: (x + d, y, z, c)


def along_y(d):
    return lambda x, y, z, c: (x, y + d, z, c)


def minor(d):
    return lambda x, y, z, c: (x, y, z + d, c) if c == 0 else (x + d, y, z, c)


def major(d):
    return lambda x, y, z, c: (x + d, y, z, c) if c == 0 else (x, y, z + d, c)


def swap_core(x, y, z, c):
    return (x, y, z, 1 - c)


def swap_zlo(x, y, z, c):
    return (x, y, z + 1 - 2 * (z % 2), c)


def send(v, fn):
    return lax.ppermute(v, AXES, moves(fn))


def spread(v, axis_fn):
    return [v] + [send(v, axis_fn(-d)) for d in SHIFTS[1:]]


def turn(v, start):
    size = v.shape[0]
    return lax.dynamic_slice_in_dim(jnp.concatenate([v, v], axis=0), start, size, axis=0)


ORDER = (0, 3, 1, 2)
BACK = (0, 2, 3, 1)
SLOTS = (3, 1, 2, 0)


def add_up(parts):
    total = parts[0].astype(F32)
    for g in parts[1:]:
        total = total + g.astype(F32)
    return total


def after(v, *done):
    return lax.optimization_barrier((v,) + done)[0]


def shards(features, cotangent, dw_kernel, norm_gain, w_expand, grn_gamma, grn_beta, w_reduce):
    rep = lax.axis_index("rep")
    shard = lax.axis_index("shard")
    c = rep % 2
    zl = (rep // 2) % 2
    x = shard // 2
    z = (shard % 2) * 2 + zl
    hid = grn_gamma.shape[0]
    piece = hid // 32
    n = 4 * piece
    img = features[0]
    cot = cotangent[0]

    first = c * (2 * piece) + zl * piece
    own = jnp.concatenate([lax.dynamic_slice_in_dim(w, first, piece, axis=0) for w in (w_expand, w_reduce)], axis=1)
    filt = conv(img, dw_kernel, 0, 2)
    row = jnp.concatenate(spread(own, minor), axis=0)
    ws = spread(row, major)

    def to_own(v):
        v = lax.dynamic_index_in_dim(v.reshape(4, 2, 2, 2, piece), c, axis=2, keepdims=False).reshape(4, 4, piece)
        v = turn(v, x).transpose(1, 0, 2)
        v = turn(v, z)
        v = jnp.where(c == 0, v.transpose(1, 0, 2), v)
        v = jnp.stack([v[ORDER[k]] for k in SLOTS])
        v = jnp.stack([v[:, k] for k in ORDER], axis=1)
        return jnp.pad(v.reshape(1, 4, n), ((0, 0), (0, 0), (0, SLOT - n)))

    def to_all(v):
        v = v[:, :n].reshape(4, 4, piece)
        v = jnp.stack([v[SLOTS.index(k)] for k in BACK])
        v = jnp.stack([v[:, k] for k in BACK], axis=1)
        v = jnp.where(c == 0, v, v.transpose(1, 0, 2))
        v = turn(v, (4 - x) % 4).transpose(1, 0, 2)
        v = turn(v, (4 - z) % 4).transpose(1, 0, 2).reshape(4, 2, 1, 2, piece)
        zero = jnp.zeros_like(v)
        both = jnp.where(c == 0, jnp.concatenate([v, zero], axis=2), jnp.concatenate([zero, v], axis=2))
        return both.reshape(4, hid // 4)

    gamma = to_own(grn_gamma)
    beta = to_own(grn_beta)
    valid = (jnp.arange(SLOT) < n).astype(F32)

    c0 = widen(cot)
    c1 = send(c0, swap_core)
    rest = conv(after(img, row, c1), dw_kernel, 2, NCB - 2)
    n0, xhat, rstd = norm(filt, after(rest, ws[1], ws[2]), norm_gain)
    n1 = send(n0, swap_core)
    h0 = hidden(n0, n1, c0, c1, [row])
    h3 = hidden(after(n0, h0[3]), n1, c0, c1, [ws[3], ws[1], ws[2]])
    stat = jnp.concatenate([h3[3], h0[3]], axis=0)
    gamma3, beta3 = gamma.reshape(4, 1, SLOT), beta.reshape(4, 1, SLOT)
    mine = tally(stat, gamma3, valid)
    vecs, back = vectors(stat, gamma3, beta3, mine, send(mine, swap_core), hid)
    back_gamma = to_all(back[:, 0])
    back_beta = to_all(back[:, 1])
    t3, t1, *part = mix([(h3, 0)], n0, n1, c0, c1, ws[3], ws[1], vecs[:2], n, ())
    s3, s1 = send(t3, major(SHIFTS[3])), send(t1, major(SHIFTS[1]))
    t2, t0, br0, br1, bn0, bn1 = mix([(h3, 2), (h0, 0)], n0, n1, c0, c1, ws[2], ws[0], vecs[2:], n, part)
    bn1_in = send(after(bn1, s1, s3), swap_core)
    s2 = send(t2, major(SHIFTS[2]))
    br1_in = send(br1, swap_core)
    d, gain_rows = unnorm(bn0, bn1_in, xhat, rstd, norm_gain)
    taps_a = taps(img, d, 0)
    part = add_up([after(t0, taps_a), s1, s2, s3]).astype(BF16)
    part = [part[k * piece : (k + 1) * piece] for k in range(4)]
    part = [part[0]] + [send(part[k], minor(SHIFTS[k])) for k in (1, 2, 3)]
    taps_b = taps(after(img, part[0]), d, HALF)[:, : C - HALF * CB]
    part = add_up([after(part[0], taps_b)] + part[1:]).astype(BF16)
    grad_taps = jnp.concatenate([taps_a, taps_b], axis=1)
    small = jnp.concatenate([grad_taps, jnp.sum(gain_rows, axis=0, keepdims=True), back_gamma, back_beta], axis=0)
    small = jnp.pad(small, ((0, 6), (0, 0))).astype(BF16)
    merged = jnp.concatenate([part, jnp.concatenate([small[:32], small[32:]], axis=1)], axis=0)
    merged = [merged] + [send(merged, along_y(s)) for s in SHIFTS[1:]]
    inverse = 1.0 / (features.shape[0] * lax.axis_size("rep") * lax.axis_size("shard"))
    grad_features = unstem(after(d, merged[0]), dw_kernel, cot, None, 0)
    merged = add_up([after(merged[0], grad_features)] + merged[1:])
    total = (merged[:piece] * inverse).astype(BF16)
    small = merged[piece:].astype(BF16)
    other = send(total, swap_zlo)
    small = [small] + [send(small, minor(s)) for s in SHIFTS[1:]]
    grad_features = unstem(after(d, small[0], total), dw_kernel, cot, grad_features, 2)
    total = after(total, grad_features)
    total = jnp.where(zl == 0, jnp.concatenate([total, other], axis=0), jnp.concatenate([other, total], axis=0))
    other = send(total, swap_core)
    small = add_up([after(small[0], grad_features)] + small[1:]).astype(BF16)
    small = [small] + [send(small, major(s)) for s in SHIFTS[1:]]
    grad_features = unstem(after(d, small[0], total), dw_kernel, cot, grad_features, 4)
    small = add_up([after(small[0], grad_features)] + small[1:]).astype(BF16)
    far = send(small, swap_core)
    block_out = finish(after(img, small), br0, br1_in)
    total = after(total, block_out)
    lo = jnp.where(c == 0, total, other)
    hi = jnp.where(c == 0, other, total)
    total = jnp.concatenate([lo, hi], axis=0).astype(F32)
    small = (after(small, total).astype(F32) + far.astype(F32)) * inverse
    small = jnp.concatenate([small[:, :C], small[:, C:]], axis=0)
    return (
        block_out[None],
        grad_features[None],
        small[:49],
        small[49],
        total[:, :C],
        small[50:54].reshape(hid),
        small[54:58].reshape(hid),
        total[:, C:],
    )


def solution(mesh):
    data = P(AXES, None, None, None)
    rows = P("shard", None)
    return jax.shard_map(
        shards,
        mesh=mesh,
        in_specs=(data, data, P(), P(), rows, P(), P(), rows),
        out_specs=(data, data, P(), P(), rows, P(), P(), rows),
        check_vma=False,
    )
```

```python
import jax
import jax.numpy as jnp
from jax import lax
from jax.sharding import PartitionSpec as P
from jax.experimental import pallas as pl
from jax.experimental.pallas import tpu as pltpu

S, W, C = 28, 32, 704
T = S * W
CB = 128
NCB = 6
HEAD = 8
CP = NCB * CB
HALF = NCB // 2
SLOT = 384
F32, BF16 = jnp.float32, jnp.bfloat16


def params(mib=48, n=1):
    return pltpu.CompilerParams(vmem_limit_bytes=mib * 1024 * 1024, dimension_semantics=("arbitrary",) * n)


def cost(flops, nbytes):
    return pl.CostEstimate(flops=int(flops), bytes_accessed=int(nbytes), transcendentals=0)


def conv_taps(src, k_ref, dst, flip):
    def cols(jv, carry):
        base = jv * 8
        acc = [None] * S
        for b in range(7):
            taps = []
            for a in range(7):
                at = (6 - a) * 7 + (6 - b) if flip else a * 7 + b
                taps.append(jnp.broadcast_to(k_ref[pl.ds(at, 1), :], (8, CB)))
            for r in range(S):
                v = src[pl.ds(r * W + HEAD + b - 3 + base, 8), :]
                for a in range(7):
                    i = r + 3 - a
                    if 0 <= i < S:
                        t = taps[a] * v
                        acc[i] = t if acc[i] is None else acc[i] + t
        for i in range(S):
            dst[pl.ds(i * W + base, 8), :] = acc[i]
        return carry

    for jv in range(W // 8):
        cols(jv, 0)


def load_map(x_ref, pad):
    for i in range(S):
        pad[pl.ds(HEAD + i * W, S), :] = x_ref[i].astype(F32)


def conv_kernel(x_ref, k_ref, filt_ref, pad):
    @pl.when(pl.program_id(0) == 0)
    def _():
        pad[...] = jnp.zeros_like(pad)

    load_map(x_ref, pad)
    conv_taps(pad, k_ref, filt_ref.at[0], False)


def conv(x, k, at, count):
    return pl.pallas_call(
        conv_kernel,
        name="conv",
        grid=(count,),
        in_specs=[pl.BlockSpec((S, S, CB), lambda c: (0, 0, c + at)), pl.BlockSpec((49, CB), lambda c: (0, c + at))],
        out_specs=pl.BlockSpec((1, T, CB), lambda c: (c, 0, 0)),
        out_shape=jax.ShapeDtypeStruct((count, T, CB), F32),
        scratch_shapes=[pltpu.VMEM((T + 2 * HEAD, CB), F32)],
        compiler_params=params(60),
        cost_estimate=cost(T * C, T * C),
    )(x, k)


NORM = 224


def norm_kernel(one_ref, two_ref, gain_ref, normed_ref, xhat_ref, rstd_ref):
    lane = lax.broadcasted_iota(jnp.int32, (W, CB), 1)
    row = lax.broadcasted_iota(jnp.int32, (W, CB), 0)
    last = lane < C - (NCB - 1) * CB
    inside = row < S
    for i in range(NORM // W):
        at = slice(i * W, (i + 1) * W)
        v = [r[c, at, :] for r in (one_ref, two_ref) for c in range(r.shape[0])]
        v[-1] = jnp.where(last, v[-1], 0.0)
        total = v[0]
        for c in range(1, NCB):
            total = total + v[c]
        mean = jnp.sum(total, axis=1, keepdims=True) * (1.0 / C)
        d = [u - mean for u in v]
        d[-1] = jnp.where(last, d[-1], 0.0)
        total = d[0] * d[0]
        for c in range(1, NCB):
            total = total + d[c] * d[c]
        spread = jnp.sum(total, axis=1, keepdims=True) * (1.0 / C)
        rstd = jnp.broadcast_to(lax.rsqrt(spread + 1e-06), (W, CB))
        rstd_ref[at, :] = rstd
        for c in range(NCB):
            n = min(CB, C - c * CB)
            xh = jnp.where(inside, d[c] * rstd, 0.0)
            xhat_ref[at, c * CB : c * CB + n] = xh[:, :n]
            g = jnp.broadcast_to(gain_ref[0:1, c * CB : (c + 1) * CB], (W, CB))
            normed_ref[at, c * CB : (c + 1) * CB] = (xh * g).astype(BF16)


def norm(one, two, gain):
    return pl.pallas_call(
        norm_kernel,
        name="norm",
        grid=(T // NORM,),
        in_specs=[
            pl.BlockSpec((one.shape[0], NORM, CB), lambda r: (0, r, 0)),
            pl.BlockSpec((two.shape[0], NORM, CB), lambda r: (0, r, 0)),
            pl.BlockSpec((1, CP), lambda r: (0, 0)),
        ],
        out_specs=[
            pl.BlockSpec((NORM, CP), lambda r: (r, 0)),
            pl.BlockSpec((NORM, C), lambda r: (r, 0)),
            pl.BlockSpec((NORM, CB), lambda r: (r, 0)),
        ],
        out_shape=[
            jax.ShapeDtypeStruct((T, CP), BF16),
            jax.ShapeDtypeStruct((T, C), F32),
            jax.ShapeDtypeStruct((T, CB), F32),
        ],
        compiler_params=params(60),
        cost_estimate=cost(T * C, T * C),
    )(one, two, jnp.pad(gain, (0, CP - C)).reshape(1, CP))


def widen_kernel(x_ref, y_ref):
    zero = jnp.zeros((W - S, C), F32)
    y_ref[:, C:] = jnp.zeros((T, CP - C), BF16)
    for i in range(S):
        y_ref[pl.ds(i * W, W), :C] = jnp.concatenate([x_ref[i].astype(F32), zero], axis=0).astype(BF16)


def widen(x):
    return pl.pallas_call(
        widen_kernel,
        name="widen",
        out_shape=jax.ShapeDtypeStruct((T, CP), BF16),
        compiler_params=pltpu.CompilerParams(vmem_limit_bytes=60 * 1024 * 1024),
        cost_estimate=cost(T * C, T * C),
    )(x)


def gelu_pair(x):
    mag = jnp.abs(x)
    e = jnp.exp2((x * x) * -0.7213475204444817)
    t = 1.0 / (1.0 + (0.3275911 * 0.7071067811865476) * mag)
    poly = (((0.5307027145 * t - 0.7265760135) * t + 0.7107068705) * t - 0.142248368) * t + 0.127414796
    tail = poly * (t * e)
    cdf = jnp.where(x < 0.0, tail, 1.0 - tail)
    return x * cdf, cdf + (0.3989422804014327 * x) * e


def split_rows(w):
    zero = jnp.zeros((SLOT - w.shape[0], C), BF16)
    return jnp.concatenate([w[:, :C], zero], axis=0), jnp.concatenate([w[:, C:], zero], axis=0)


ROWS = 448
STEPS = T // ROWS


def hidden_kernel(n0, n1, c0, c1, *refs, count):
    ws = refs[:count]
    act_ref, slope_ref, back_ref, stat_ref = refs[-4:]
    g = pl.program_id(0)
    nt = (((1,), (1,)), ((), ()))

    def body(n_ref, c_ref):
        for k in range(count):
            we, wr = split_rows(ws[k][...])
            pre = lax.dot_general(n_ref[:, :C], we, nt, preferred_element_type=F32)
            dm = lax.dot_general(c_ref[:, :C], wr, nt, preferred_element_type=F32)
            act, slope = gelu_pair(pre)
            act_ref[k] = act.astype(BF16)
            slope_ref[k] = slope.astype(BF16)
            back_ref[k] = dm.astype(BF16)
            e2 = jnp.sum(act * act, axis=0, keepdims=True)
            s1 = jnp.sum(dm * act, axis=0, keepdims=True)
            s0 = jnp.sum(dm, axis=0, keepdims=True)
            stat_ref[k, 0] += jnp.concatenate([e2, s1, s0, jnp.zeros((5, SLOT), F32)], axis=0)

    @pl.when(g % STEPS == 0)
    def _():
        stat_ref[...] = jnp.zeros_like(stat_ref)

    @pl.when(g < STEPS)
    def _():
        body(n0, c0)

    @pl.when(g >= STEPS)
    def _():
        body(n1, c1)


def hidden(n0, n1, c0, c1, ws):
    count = len(ws)
    wide = pl.BlockSpec((count, ROWS, SLOT), lambda g: (0, g, 0))
    one = pl.BlockSpec((ROWS, CP), lambda g: (jnp.minimum(g, STEPS - 1), 0))
    two = pl.BlockSpec((ROWS, CP), lambda g: (jnp.maximum(g - STEPS, 0), 0))
    return pl.pallas_call(
        lambda *refs: hidden_kernel(*refs, count=count),
        name="hidden",
        grid=(2 * STEPS,),
        in_specs=[one, two, one, two] + [pl.BlockSpec(ws[0].shape, lambda g: (0, 0))] * count,
        out_specs=[wide, wide, wide, pl.BlockSpec((count, 1, 8, SLOT), lambda g: (0, g // STEPS, 0, 0))],
        out_shape=[jax.ShapeDtypeStruct((count, 2 * T, SLOT), BF16)] * 3
        + [jax.ShapeDtypeStruct((count, 2, 8, SLOT), F32)],
        compiler_params=params(60),
        cost_estimate=cost(T * C, T * C),
    )(n0, n1, c0, c1, *ws)


def full_sum(v):
    return jnp.sum(jnp.sum(jnp.sum(v, axis=0), axis=0, keepdims=True), axis=1, keepdims=True)


def stat_row(refs, im, at):
    return jnp.concatenate([r[:, im, at : at + 1, :] for r in refs], axis=0)


def tally_kernel(one, two, gamma_ref, valid_ref, o_ref):
    rows = []
    for im in range(2):
        energy = jnp.sqrt(stat_row((one, two), im, 0) + 1e-06)
        rows.append(jnp.broadcast_to(full_sum(energy * valid_ref[...]), (1, CB)))
        rows.append(jnp.broadcast_to(full_sum(gamma_ref[...] * stat_row((one, two), im, 1) * energy), (1, CB)))
    o_ref[...] = jnp.concatenate(rows + [jnp.zeros((4, CB), F32)], axis=0)


def tally(one, two, gamma, valid):
    return pl.pallas_call(
        tally_kernel,
        name="tally",
        out_shape=jax.ShapeDtypeStruct((8, CB), F32),
        compiler_params=pltpu.CompilerParams(vmem_limit_bytes=60 * 1024 * 1024),
        cost_estimate=cost(T * C, T * C),
    )(one, two, gamma, valid)


def vectors_kernel(one, two, gamma_ref, beta_ref, mine, theirs, va_ref, vb_ref, g_ref, *, hid):
    gamma = gamma_ref[...]
    back_gamma = back_beta = 0.0
    for im in range(2):
        far = 2 * (1 - im)
        e_all = (mine[2 * im : 2 * im + 1, 0:1] + theirs[far : far + 1, 0:1]).reshape(1, 1, 1)
        d_all = (mine[2 * im + 1 : 2 * im + 2, 0:1] + theirs[far + 1 : far + 2, 0:1]).reshape(1, 1, 1)
        energy = jnp.sqrt(stat_row((one, two), im, 0) + 1e-06)
        s1 = stat_row((one, two), im, 1)
        inv = 1.0 / (e_all * (1.0 / hid) + 1e-06)
        ratio = energy * inv
        pull = (gamma * s1 * inv - d_all * (1.0 / hid) * inv * inv) / energy
        for at, row in enumerate((1.0 + gamma * ratio, pull, beta_ref[...])):
            va_ref[:, im, at : at + 1, :] = row[:2]
            vb_ref[:, im, at : at + 1, :] = row[2:]
        va_ref[:, im, 3:8, :] = jnp.zeros((2, 5, SLOT), F32)
        vb_ref[:, im, 3:8, :] = jnp.zeros((2, 5, SLOT), F32)
        back_gamma = back_gamma + ratio * s1
        back_beta = back_beta + stat_row((one, two), im, 2)
    g_ref[:, 0:1, :] = back_gamma
    g_ref[:, 1:2, :] = back_beta
    g_ref[:, 2:8, :] = jnp.zeros((4, 6, SLOT), F32)


def vectors(one, two, gamma, beta, mine, theirs, hid):
    return pl.pallas_call(
        lambda *refs: vectors_kernel(*refs, hid=hid),
        name="vectors",
        out_shape=[jax.ShapeDtypeStruct((2, 2, 8, SLOT), F32)] * 2 + [jax.ShapeDtypeStruct((4, 8, SLOT), F32)],
        compiler_params=pltpu.CompilerParams(vmem_limit_bytes=60 * 1024 * 1024),
        cost_estimate=cost(T * C, T * C),
    )(one, two, gamma, beta, mine, theirs)


def mix_kernel(*refs, count, fresh):
    acts, slopes, backs = refs[:count], refs[count : 2 * count], refs[2 * count : 3 * count]
    n0, n1, c0, c1, wa, wb, v_ref = refs[3 * count : 3 * count + 7]
    rest = refs[3 * count + 7 :]
    old, rest = ([], rest) if fresh else (rest[:2], rest[2:])
    ta, tb, *outs, te, tr, we, wr = rest
    g = pl.program_id(0)
    tn = (((0,), (0,)), ((), ()))

    @pl.when(g == 0)
    def _():
        for k, w in enumerate((wa, wb)):
            we[k * SLOT : (k + 1) * SLOT, :], wr[k * SLOT : (k + 1) * SLOT, :] = split_rows(w[...])
        te[...] = jnp.zeros_like(te)
        tr[...] = jnp.zeros_like(tr)

    def pick(rs, k):
        return rs[0][k] if count == 1 else rs[k][0]

    def body(n_ref, c_ref):
        mapped, bp = [], []
        for k in range(2):
            v = v_ref[k, 0]
            p, q, beta = v[0:1], v[1:2], v[2:3]
            a = pick(acts, k).astype(F32)
            mapped.append((a * p + beta).astype(BF16))
            bp.append(((pick(backs, k).astype(F32) * p + a * q) * pick(slopes, k).astype(F32)).astype(BF16))
        mapped = jnp.concatenate(mapped, axis=1)
        bp = jnp.concatenate(bp, axis=1)
        br = lax.dot(mapped, wr[...], preferred_element_type=F32)
        bn = lax.dot(bp, we[...], preferred_element_type=F32)
        te[...] += lax.dot_general(bp, n_ref[:, :C], tn, preferred_element_type=F32)
        tr[...] += lax.dot_general(mapped, c_ref[:, :C], tn, preferred_element_type=F32)
        return br, bn

    def put(br, bn, k):
        if fresh:
            outs[0][0] = br.astype(BF16)
            outs[1][0] = bn.astype(BF16)
        else:
            for o, v, w in ((outs[k], br, old[0]), (outs[2 + k], bn, old[1])):
                o[:, :C] = (v + w[0].astype(F32)).astype(BF16)
                o[:, C:] = jnp.zeros((ROWS, CP - C), BF16)

    @pl.when(g < STEPS)
    def _():
        put(*body(n0, c0), 0)

    @pl.when(g >= STEPS)
    def _():
        put(*body(n1, c1), 1)

    @pl.when(g == 2 * STEPS - 1)
    def _():
        n = ta.shape[0]
        for k, t in enumerate((ta, tb)):
            t[:, :C] = te[k * SLOT : k * SLOT + n, :].astype(BF16)
            t[:, C:] = tr[k * SLOT : k * SLOT + n, :].astype(BF16)


def mix(sets, n0, n1, c0, c1, wa, wb, vecs, n, old):
    once = pl.Buffered(1)
    if len(sets) == 1:
        h, at = sets[0]
        acts = [(h[i], pl.BlockSpec((2, ROWS, SLOT), lambda g: (at // 2, g, 0))) for i in range(3)]
    else:
        acts = [
            (h[i], pl.BlockSpec((1, ROWS, SLOT), lambda g, at=at: (at, g, 0))) for i in range(3) for h, at in sets
        ]
    one = pl.BlockSpec((ROWS, CP), lambda g: (jnp.minimum(g, STEPS - 1), 0))
    two = pl.BlockSpec((ROWS, CP), lambda g: (jnp.maximum(g - STEPS, 0), 0))
    rows = pl.BlockSpec((n, 2 * C), lambda g: (0, 0), pipeline_mode=once)
    part = pl.BlockSpec((1, ROWS, C), lambda g: (g // STEPS, g % STEPS, 0))
    terms = jax.ShapeDtypeStruct((n, 2 * C), BF16)
    if old:
        outs, shapes = [one, two, one, two], [jax.ShapeDtypeStruct((T, CP), BF16)] * 4
    else:
        outs, shapes = [part] * 2, [jax.ShapeDtypeStruct((2, T, C), BF16)] * 2
    return pl.pallas_call(
        lambda *refs: mix_kernel(*refs, count=len(sets), fresh=not old),
        name="mix",
        grid=(2 * STEPS,),
        in_specs=[spec for _, spec in acts]
        + [one, two, one, two]
        + [rows, rows, pl.BlockSpec((2, 1, 8, SLOT), lambda g: (0, g // STEPS, 0, 0))]
        + [part] * len(old),
        out_specs=[rows, rows] + outs,
        out_shape=[terms, terms] + shapes,
        scratch_shapes=[pltpu.VMEM((2 * SLOT, C), F32)] * 2 + [pltpu.VMEM((2 * SLOT, C), BF16)] * 2,
        compiler_params=params(62),
        cost_estimate=cost(T * C, T * C),
    )(*[v for v, _ in acts], n0, n1, c0, c1, wa, wb, vecs, *old)


def unnorm_kernel(b0, b1, xhat, rstd, gain, d_ref, gg_ref, *, step):
    @pl.when(pl.program_id(0) == 0)
    def _():
        gg_ref[...] = jnp.zeros_like(gg_ref)

    def rows(i, carry):
        at = pl.ds(pl.multiple_of(i * W, W), W)
        bn = b0[at, :C].astype(F32) + b1[at, :C].astype(F32)
        xh = xhat[at, :]
        g = bn * gain[0:1, :]
        m1 = jnp.sum(g, axis=1, keepdims=True) * (1.0 / C)
        m2 = jnp.sum(g * xh, axis=1, keepdims=True) * (1.0 / C)
        r = rstd[at, 0:1]
        d_ref[at, :] = r * (g - m1 - xh * m2)
        gg_ref[...] += jnp.sum((bn * xh).reshape(W // 8, 8, C), axis=0)
        return carry

    lax.fori_loop(0, step // W, rows, 0, unroll=True)


def unnorm(b0, b1, xhat, rstd, gain):
    step = T // 4
    full = pl.BlockSpec((step, C), lambda r: (r, 0))
    wide = pl.BlockSpec((step, CP), lambda r: (r, 0))
    return pl.pallas_call(
        lambda *refs: unnorm_kernel(*refs, step=step),
        name="unnorm",
        grid=(T // step,),
        in_specs=[wide, wide, full, pl.BlockSpec((step, CB), lambda r: (r, 0)), pl.BlockSpec((1, C), lambda r: (0, 0))],
        out_specs=[full, pl.BlockSpec((8, C), lambda r: (0, 0))],
        out_shape=[jax.ShapeDtypeStruct((T, C), F32), jax.ShapeDtypeStruct((8, C), F32)],
        compiler_params=params(60),
        cost_estimate=cost(T * C, T * C),
    )(b0, b1, xhat, rstd, gain.reshape(1, C))


def taps_kernel(x_ref, d_ref, g_ref, pad):
    @pl.when(pl.program_id(0) == 0)
    def _():
        pad[...] = jnp.zeros_like(pad)

    for i in range(S):
        pad[pl.ds(HEAD + i * W, S), :] = x_ref[i].astype(F32)

    for b in range(7):
        def cols(jv, acc):
            base = jv * 8
            acc = list(acc)
            d = {}
            for r in range(S):
                if r == 0:
                    for i in range(4):
                        d[i] = d_ref[pl.ds(i * W + base, 8), :]
                elif r + 3 < S:
                    d[r + 3] = d_ref[pl.ds((r + 3) * W + base, 8), :]
                v = pad[pl.ds(r * W + HEAD + b - 3 + base, 8), :]
                for a in range(7):
                    i = r + 3 - a
                    if 0 <= i < S:
                        acc[a] = acc[a] + d[i] * v
            return tuple(acc)

        acc = (jnp.zeros((8, CB), F32),) * 7
        for jv in range(W // 8):
            acc = cols(jv, acc)
        for a in range(7):
            g_ref[pl.ds(a * 7 + b, 1), :] = jnp.sum(acc[a], axis=0, keepdims=True)


def taps(x, d, at):
    return pl.pallas_call(
        taps_kernel,
        name="taps",
        grid=(HALF,),
        in_specs=[pl.BlockSpec((S, S, CB), lambda c: (0, 0, c + at)), pl.BlockSpec((T, CB), lambda c: (0, c + at))],
        out_specs=pl.BlockSpec((49, CB), lambda c: (0, c)),
        out_shape=jax.ShapeDtypeStruct((49, HALF * CB), F32),
        scratch_shapes=[pltpu.VMEM((T + 2 * HEAD, CB), F32)],
        compiler_params=params(60),
        cost_estimate=cost(T * C, T * C),
    )(x, d)


def unstem_kernel(d_ref, k_ref, c_ref, old_ref, o_ref, pad, res):
    @pl.when(pl.program_id(0) == 0)
    def _():
        pad[...] = jnp.zeros_like(pad)

    pad[pl.ds(HEAD, T), :] = d_ref[...]
    conv_taps(pad, k_ref, res, True)
    for i in range(S):
        o_ref[i] = (c_ref[i].astype(F32) + res[pl.ds(i * W, S), :]).astype(BF16)


def unstem(d, k, cot, old, at, count):
    return pl.pallas_call(
        unstem_kernel if old is not None else (lambda d, k, c, *r: unstem_kernel(d, k, c, None, *r)),
        name="unstem",
        grid=(count,),
        in_specs=[
            pl.BlockSpec((T, CB), lambda c: (0, c + at)),
            pl.BlockSpec((49, CB), lambda c: (0, c + at)),
            pl.BlockSpec((S, S, CB), lambda c: (0, 0, c + at)),
        ]
        + ([pl.BlockSpec(memory_space=pl.ANY)] if old is not None else []),
        out_specs=pl.BlockSpec((S, S, CB), lambda c: (0, 0, c + at)),
        out_shape=jax.ShapeDtypeStruct((S, S, C), BF16),
        scratch_shapes=[pltpu.VMEM((T + 2 * HEAD, CB), F32), pltpu.VMEM((T, CB), F32)],
        input_output_aliases={3: 0} if old is not None else {},
        compiler_params=params(60),
        cost_estimate=cost(T * C, T * C),
    )(d, k, cot, *([old] if old is not None else []))


PART = 7


def finish_kernel(x_ref, b0, b1, o_ref):
    for i in range(PART):
        at = slice(i * W, (i + 1) * W)
        t = b0[at, :].astype(F32) + b1[at, :].astype(F32)
        o_ref[i] = (x_ref[i].astype(F32) + t[:S, :C]).astype(BF16)


def finish(x, b0, b1):
    maps = pl.BlockSpec((PART, S, C), lambda r: (r, 0, 0))
    rows = pl.BlockSpec((PART * W, CP), lambda r: (r, 0))
    return pl.pallas_call(
        finish_kernel,
        name="finish",
        grid=(S // PART,),
        in_specs=[maps, rows, rows],
        out_specs=maps,
        out_shape=jax.ShapeDtypeStruct((S, S, C), BF16),
        compiler_params=params(60),
        cost_estimate=cost(T * C, T * C),
    )(x, b0, b1)


SHIFTS = (0, -1, 1, 2)
AXES = ("rep", "shard")


def place(x, y, z, c):
    return ((y * 2 + z % 2) * 2 + c) * 8 + x * 2 + z // 2


def moves(fn):
    pairs = []
    for x in range(4):
        for y in range(4):
            for z in range(4):
                for c in range(2):
                    nx, ny, nz, nc = fn(x, y, z, c)
                    pairs.append((place(x, y, z, c), place(nx % 4, ny % 4, nz % 4, nc)))
    return pairs


def along_x(d):
    return lambda x, y, z, c: (x + d, y, z, c)


def along_y(d):
    return lambda x, y, z, c: (x, y + d, z, c)


def minor(d):
    return lambda x, y, z, c: (x, y, z + d, c) if c == 0 else (x + d, y, z, c)


def major(d):
    return lambda x, y, z, c: (x + d, y, z, c) if c == 0 else (x, y, z + d, c)


def swap_core(x, y, z, c):
    return (x, y, z, 1 - c)


def swap_zlo(x, y, z, c):
    return (x, y, z + 1 - 2 * (z % 2), c)


def send(v, fn):
    return lax.ppermute(v, AXES, moves(fn))


def spread(v, axis_fn):
    return [v] + [send(v, axis_fn(-d)) for d in SHIFTS[1:]]


def turn(v, start):
    size = v.shape[0]
    return lax.dynamic_slice_in_dim(jnp.concatenate([v, v], axis=0), start, size, axis=0)


ORDER = (0, 3, 1, 2)
BACK = (0, 2, 3, 1)
SLOTS = (3, 1, 2, 0)


def add_up(parts):
    total = parts[0].astype(F32)
    for g in parts[1:]:
        total = total + g.astype(F32)
    return total


def after(v, *done):
    return lax.optimization_barrier((v,) + done)[0]


def shards(features, cotangent, dw_kernel, norm_gain, w_expand, grn_gamma, grn_beta, w_reduce):
    rep = lax.axis_index("rep")
    shard = lax.axis_index("shard")
    c = rep % 2
    zl = (rep // 2) % 2
    x = shard // 2
    z = (shard % 2) * 2 + zl
    hid = grn_gamma.shape[0]
    piece = hid // 32
    n = 4 * piece
    img = features[0]
    cot = cotangent[0]

    first = c * (2 * piece) + zl * piece
    own = jnp.concatenate([lax.dynamic_slice_in_dim(w, first, piece, axis=0) for w in (w_expand, w_reduce)], axis=1)
    filt = conv(img, dw_kernel, 0, 2)
    row = jnp.concatenate(spread(own, minor), axis=0)
    ws = spread(row, major)

    def to_own(v):
        v = lax.dynamic_index_in_dim(v.reshape(4, 2, 2, 2, piece), c, axis=2, keepdims=False).reshape(4, 4, piece)
        v = turn(v, x).transpose(1, 0, 2)
        v = turn(v, z)
        v = jnp.where(c == 0, v.transpose(1, 0, 2), v)
        v = jnp.stack([v[ORDER[k]] for k in SLOTS])
        v = jnp.stack([v[:, k] for k in ORDER], axis=1)
        return jnp.pad(v.reshape(1, 4, n), ((0, 0), (0, 0), (0, SLOT - n)))

    def to_all(v):
        v = v[:, :n].reshape(4, 4, piece)
        v = jnp.stack([v[SLOTS.index(k)] for k in BACK])
        v = jnp.stack([v[:, k] for k in BACK], axis=1)
        v = jnp.where(c == 0, v, v.transpose(1, 0, 2))
        v = turn(v, (4 - x) % 4).transpose(1, 0, 2)
        v = turn(v, (4 - z) % 4).transpose(1, 0, 2).reshape(4, 2, 1, 2, piece)
        zero = jnp.zeros_like(v)
        both = jnp.where(c == 0, jnp.concatenate([v, zero], axis=2), jnp.concatenate([zero, v], axis=2))
        return both.reshape(4, hid // 4)

    gamma = to_own(grn_gamma)
    beta = to_own(grn_beta)
    valid = (jnp.arange(SLOT) < n).astype(F32)

    c0 = widen(cot)
    c1 = send(c0, swap_core)
    rest = conv(after(img, row, c1), dw_kernel, 2, NCB - 2)
    n0, xhat, rstd = norm(filt, after(rest, ws[1], ws[2]), norm_gain)
    n1 = send(n0, swap_core)
    h0 = hidden(n0, n1, c0, c1, [row])
    h3 = hidden(after(n0, h0[3]), n1, c0, c1, [ws[3], ws[1], ws[2]])
    gamma3, beta3 = gamma.reshape(4, 1, SLOT), beta.reshape(4, 1, SLOT)
    mine = tally(h3[3], h0[3], gamma3, valid)
    vec_a, vec_b, back = vectors(h3[3], h0[3], gamma3, beta3, mine, send(mine, swap_core), hid)
    back_gamma = to_all(back[:, 0])
    back_beta = to_all(back[:, 1])
    t3, t1, *part = mix([(h3, 0)], n0, n1, c0, c1, ws[3], ws[1], vec_a, n, ())
    s3, s1 = send(t3, major(SHIFTS[3])), send(t1, major(SHIFTS[1]))
    t2, t0, br0, br1, bn0, bn1 = mix([(h3, 2), (h0, 0)], n0, n1, c0, c1, ws[2], ws[0], vec_b, n, part)
    bn1_in = send(after(bn1, s1, s3), swap_core)
    s2 = send(t2, major(SHIFTS[2]))
    br1_in = send(br1, swap_core)
    d, gain_rows = unnorm(bn0, bn1_in, xhat, rstd, norm_gain)
    taps_a = taps(img, d, 0)
    part = add_up([after(t0, taps_a), s1, s2, s3]).astype(BF16)
    part = [part[k * piece : (k + 1) * piece] for k in range(4)]
    part = [part[0]] + [send(part[k], minor(SHIFTS[k])) for k in (1, 2, 3)]
    taps_b = taps(after(img, part[0]), d, HALF)[:, : C - HALF * CB]
    part = add_up([after(part[0], taps_b)] + part[1:]).astype(BF16)
    grad_taps = jnp.concatenate([taps_a, taps_b], axis=1)
    small = jnp.concatenate([grad_taps, jnp.sum(gain_rows, axis=0, keepdims=True), back_gamma, back_beta], axis=0)
    small = jnp.pad(small, ((0, 6), (0, 0))).astype(BF16)
    merged = jnp.concatenate([part, jnp.concatenate([small[:32], small[32:]], axis=1)], axis=0)
    merged = [merged] + [send(merged, along_y(s)) for s in SHIFTS[1:]]
    inverse = 1.0 / (features.shape[0] * lax.axis_size("rep") * lax.axis_size("shard"))
    grad_features = unstem(after(d, merged[0]), dw_kernel, cot, None, 0, 3)
    block_out = finish(after(img, grad_features), br0, br1_in)
    merged = add_up([after(merged[0], block_out)] + merged[1:])
    total = (merged[:piece] * inverse).astype(BF16)
    small = merged[piece:].astype(BF16)
    other = send(total, swap_zlo)
    small = [small] + [send(small, minor(s)) for s in SHIFTS[1:]]
    grad_features = unstem(after(d, small[0], total), dw_kernel, cot, grad_features, 3, 1)
    total = after(total, grad_features)
    total = jnp.where(zl == 0, jnp.concatenate([total, other], axis=0), jnp.concatenate([other, total], axis=0))
    other = send(total, swap_core)
    small = add_up([after(small[0], grad_features)] + small[1:]).astype(BF16)
    small = [small] + [send(small, major(s)) for s in SHIFTS[1:]]
    grad_features = unstem(after(d, small[0], total), dw_kernel, cot, grad_features, 4, 2)
    small = add_up([after(small[0], grad_features)] + small[1:]).astype(BF16)
    far = send(small, swap_core)
    total = after(total, small)
    lo = jnp.where(c == 0, total, other)
    hi = jnp.where(c == 0, other, total)
    total = jnp.concatenate([lo, hi], axis=0).astype(F32)
    small = (after(small, total).astype(F32) + far.astype(F32)) * inverse
    small = jnp.concatenate([small[:, :C], small[:, C:]], axis=0)
    return (
        block_out[None],
        grad_features[None],
        small[:49],
        small[49],
        total[:, :C],
        small[50:54].reshape(hid),
        small[54:58].reshape(hid),
        total[:, C:],
    )


def solution(mesh):
    data = P(AXES, None, None, None)
    rows = P("shard", None)
    return jax.shard_map(
        shards,
        mesh=mesh,
        in_specs=(data, data, P(), P(), rows, P(), P(), rows),
        out_specs=(data, data, P(), P(), rows, P(), P(), rows),
        check_vma=False,
    )
```

```python
import jax
import jax.numpy as jnp
from jax import lax
from jax.sharding import PartitionSpec as P
from jax.experimental import pallas as pl
from jax.experimental.pallas import tpu as pltpu

S, W, C = 28, 32, 704
T = S * W
CB = 128
NCB = 6
HEAD = 8
CP = NCB * CB
HALF = NCB // 2
SLOT = 384
F32, BF16 = jnp.float32, jnp.bfloat16


def params(mib=48, n=1):
    return pltpu.CompilerParams(vmem_limit_bytes=mib * 1024 * 1024, dimension_semantics=("arbitrary",) * n)


def cost(flops, nbytes):
    return pl.CostEstimate(flops=int(flops), bytes_accessed=int(nbytes), transcendentals=0)


def conv_taps(src, k_ref, dst, flip):
    def cols(jv, carry):
        base = jv * 8
        acc = [None] * S
        for b in range(7):
            taps = []
            for a in range(7):
                at = (6 - a) * 7 + (6 - b) if flip else a * 7 + b
                taps.append(jnp.broadcast_to(k_ref[pl.ds(at, 1), :], (8, CB)))
            for r in range(S):
                v = src[pl.ds(r * W + HEAD + b - 3 + base, 8), :]
                for a in range(7):
                    i = r + 3 - a
                    if 0 <= i < S:
                        t = taps[a] * v
                        acc[i] = t if acc[i] is None else acc[i] + t
        for i in range(S):
            dst[pl.ds(i * W + base, 8), :] = acc[i]
        return carry

    for jv in range(W // 8):
        cols(jv, 0)


def load_map(x_ref, pad):
    for i in range(S):
        pad[pl.ds(HEAD + i * W, S), :] = x_ref[i].astype(F32)


def conv_kernel(x_ref, k_ref, filt_ref, pad):
    @pl.when(pl.program_id(0) == 0)
    def _():
        pad[...] = jnp.zeros_like(pad)

    load_map(x_ref, pad)
    conv_taps(pad, k_ref, filt_ref.at[0], False)


def conv(x, k, at, count):
    return pl.pallas_call(
        conv_kernel,
        name="conv",
        grid=(count,),
        in_specs=[pl.BlockSpec((S, S, CB), lambda c: (0, 0, c + at)), pl.BlockSpec((49, CB), lambda c: (0, c + at))],
        out_specs=pl.BlockSpec((1, T, CB), lambda c: (c, 0, 0)),
        out_shape=jax.ShapeDtypeStruct((count, T, CB), F32),
        scratch_shapes=[pltpu.VMEM((T + 2 * HEAD, CB), F32)],
        compiler_params=params(60),
        cost_estimate=cost(T * C, T * C),
    )(x, k)


NORM = 224


def norm_kernel(one_ref, two_ref, gain_ref, normed_ref, xhat_ref, rstd_ref):
    lane = lax.broadcasted_iota(jnp.int32, (W, CB), 1)
    row = lax.broadcasted_iota(jnp.int32, (W, CB), 0)
    last = lane < C - (NCB - 1) * CB
    inside = row < S
    for i in range(NORM // W):
        at = slice(i * W, (i + 1) * W)
        v = [r[c, at, :] for r in (one_ref, two_ref) for c in range(r.shape[0])]
        v[-1] = jnp.where(last, v[-1], 0.0)
        total = v[0]
        for c in range(1, NCB):
            total = total + v[c]
        mean = jnp.sum(total, axis=1, keepdims=True) * (1.0 / C)
        d = [u - mean for u in v]
        d[-1] = jnp.where(last, d[-1], 0.0)
        total = d[0] * d[0]
        for c in range(1, NCB):
            total = total + d[c] * d[c]
        spread = jnp.sum(total, axis=1, keepdims=True) * (1.0 / C)
        rstd = jnp.broadcast_to(lax.rsqrt(spread + 1e-06), (W, CB))
        rstd_ref[at, :] = rstd
        for c in range(NCB):
            n = min(CB, C - c * CB)
            xh = jnp.where(inside, d[c] * rstd, 0.0)
            xhat_ref[at, c * CB : c * CB + n] = xh[:, :n]
            g = jnp.broadcast_to(gain_ref[0:1, c * CB : (c + 1) * CB], (W, CB))
            normed_ref[at, c * CB : (c + 1) * CB] = (xh * g).astype(BF16)


def norm(one, two, gain):
    return pl.pallas_call(
        norm_kernel,
        name="norm",
        grid=(T // NORM,),
        in_specs=[
            pl.BlockSpec((one.shape[0], NORM, CB), lambda r: (0, r, 0)),
            pl.BlockSpec((two.shape[0], NORM, CB), lambda r: (0, r, 0)),
            pl.BlockSpec((1, CP), lambda r: (0, 0)),
        ],
        out_specs=[
            pl.BlockSpec((NORM, CP), lambda r: (r, 0)),
            pl.BlockSpec((NORM, C), lambda r: (r, 0)),
            pl.BlockSpec((NORM, CB), lambda r: (r, 0)),
        ],
        out_shape=[
            jax.ShapeDtypeStruct((T, CP), BF16),
            jax.ShapeDtypeStruct((T, C), F32),
            jax.ShapeDtypeStruct((T, CB), F32),
        ],
        compiler_params=params(60),
        cost_estimate=cost(T * C, T * C),
    )(one, two, jnp.pad(gain, (0, CP - C)).reshape(1, CP))


def widen_kernel(x_ref, y_ref):
    zero = jnp.zeros((W - S, C), F32)
    y_ref[:, C:] = jnp.zeros((T, CP - C), BF16)
    for i in range(S):
        y_ref[pl.ds(i * W, W), :C] = jnp.concatenate([x_ref[i].astype(F32), zero], axis=0).astype(BF16)


def widen(x):
    return pl.pallas_call(
        widen_kernel,
        name="widen",
        out_shape=jax.ShapeDtypeStruct((T, CP), BF16),
        compiler_params=pltpu.CompilerParams(vmem_limit_bytes=60 * 1024 * 1024),
        cost_estimate=cost(T * C, T * C),
    )(x)


def gelu_pair(x):
    mag = jnp.abs(x)
    e = jnp.exp2((x * x) * -0.7213475204444817)
    t = 1.0 / (1.0 + (0.3275911 * 0.7071067811865476) * mag)
    poly = (((0.5307027145 * t - 0.7265760135) * t + 0.7107068705) * t - 0.142248368) * t + 0.127414796
    tail = poly * (t * e)
    cdf = jnp.where(x < 0.0, tail, 1.0 - tail)
    return x * cdf, cdf + (0.3989422804014327 * x) * e


def split_rows(w):
    zero = jnp.zeros((SLOT - w.shape[0], C), BF16)
    return jnp.concatenate([w[:, :C], zero], axis=0), jnp.concatenate([w[:, C:], zero], axis=0)


ROWS = 448
STEPS = T // ROWS


def hidden_kernel(n0, n1, c0, c1, *refs, count):
    ws = refs[:count]
    act_ref, slope_ref, back_ref, stat_ref = refs[-4:]
    g = pl.program_id(0)
    nt = (((1,), (1,)), ((), ()))

    def body(n_ref, c_ref):
        for k in range(count):
            we, wr = split_rows(ws[k][...])
            pre = lax.dot_general(n_ref[:, :C], we, nt, preferred_element_type=F32)
            dm = lax.dot_general(c_ref[:, :C], wr, nt, preferred_element_type=F32)
            act, slope = gelu_pair(pre)
            act_ref[k] = act.astype(BF16)
            slope_ref[k] = slope.astype(BF16)
            back_ref[k] = dm.astype(BF16)
            e2 = jnp.sum(act * act, axis=0, keepdims=True)
            s1 = jnp.sum(dm * act, axis=0, keepdims=True)
            s0 = jnp.sum(dm, axis=0, keepdims=True)
            stat_ref[k, 0] += jnp.concatenate([e2, s1, s0, jnp.zeros((5, SLOT), F32)], axis=0)

    @pl.when(g % STEPS == 0)
    def _():
        stat_ref[...] = jnp.zeros_like(stat_ref)

    @pl.when(g < STEPS)
    def _():
        body(n0, c0)

    @pl.when(g >= STEPS)
    def _():
        body(n1, c1)


def hidden(n0, n1, c0, c1, ws):
    count = len(ws)
    wide = pl.BlockSpec((count, ROWS, SLOT), lambda g: (0, g, 0))
    one = pl.BlockSpec((ROWS, CP), lambda g: (jnp.minimum(g, STEPS - 1), 0))
    two = pl.BlockSpec((ROWS, CP), lambda g: (jnp.maximum(g - STEPS, 0), 0))
    return pl.pallas_call(
        lambda *refs: hidden_kernel(*refs, count=count),
        name="hidden",
        grid=(2 * STEPS,),
        in_specs=[one, two, one, two] + [pl.BlockSpec(ws[0].shape, lambda g: (0, 0))] * count,
        out_specs=[wide, wide, wide, pl.BlockSpec((count, 1, 8, SLOT), lambda g: (0, g // STEPS, 0, 0))],
        out_shape=[jax.ShapeDtypeStruct((count, 2 * T, SLOT), BF16)] * 3
        + [jax.ShapeDtypeStruct((count, 2, 8, SLOT), F32)],
        compiler_params=params(60),
        cost_estimate=cost(T * C, T * C),
    )(n0, n1, c0, c1, *ws)


def full_sum(v):
    return jnp.sum(jnp.sum(jnp.sum(v, axis=0), axis=0, keepdims=True), axis=1, keepdims=True)


def stat_row(refs, im, at):
    return jnp.concatenate([r[:, im, at : at + 1, :] for r in refs], axis=0)


def tally_kernel(one, two, gamma_ref, valid_ref, o_ref):
    rows = []
    for im in range(2):
        energy = jnp.sqrt(stat_row((one, two), im, 0) + 1e-06)
        rows.append(jnp.broadcast_to(full_sum(energy * valid_ref[...]), (1, CB)))
        rows.append(jnp.broadcast_to(full_sum(gamma_ref[...] * stat_row((one, two), im, 1) * energy), (1, CB)))
    o_ref[...] = jnp.concatenate(rows + [jnp.zeros((4, CB), F32)], axis=0)


def tally(one, two, gamma, valid):
    return pl.pallas_call(
        tally_kernel,
        name="tally",
        out_shape=jax.ShapeDtypeStruct((8, CB), F32),
        compiler_params=pltpu.CompilerParams(vmem_limit_bytes=60 * 1024 * 1024),
        cost_estimate=cost(T * C, T * C),
    )(one, two, gamma, valid)


def vectors_kernel(one, two, gamma_ref, beta_ref, mine, theirs, va_ref, vb_ref, g_ref, *, hid):
    gamma = gamma_ref[...]
    back_gamma = back_beta = 0.0
    for im in range(2):
        far = 2 * (1 - im)
        e_all = (mine[2 * im : 2 * im + 1, 0:1] + theirs[far : far + 1, 0:1]).reshape(1, 1, 1)
        d_all = (mine[2 * im + 1 : 2 * im + 2, 0:1] + theirs[far + 1 : far + 2, 0:1]).reshape(1, 1, 1)
        energy = jnp.sqrt(stat_row((one, two), im, 0) + 1e-06)
        s1 = stat_row((one, two), im, 1)
        inv = 1.0 / (e_all * (1.0 / hid) + 1e-06)
        ratio = energy * inv
        pull = (gamma * s1 * inv - d_all * (1.0 / hid) * inv * inv) / energy
        for at, row in enumerate((1.0 + gamma * ratio, pull, beta_ref[...])):
            va_ref[:, im, at : at + 1, :] = row[:2]
            vb_ref[:, im, at : at + 1, :] = row[2:]
        va_ref[:, im, 3:8, :] = jnp.zeros((2, 5, SLOT), F32)
        vb_ref[:, im, 3:8, :] = jnp.zeros((2, 5, SLOT), F32)
        back_gamma = back_gamma + ratio * s1
        back_beta = back_beta + stat_row((one, two), im, 2)
    g_ref[:, 0:1, :] = back_gamma
    g_ref[:, 1:2, :] = back_beta
    g_ref[:, 2:8, :] = jnp.zeros((4, 6, SLOT), F32)


def vectors(one, two, gamma, beta, mine, theirs, hid):
    return pl.pallas_call(
        lambda *refs: vectors_kernel(*refs, hid=hid),
        name="vectors",
        out_shape=[jax.ShapeDtypeStruct((2, 2, 8, SLOT), F32)] * 2 + [jax.ShapeDtypeStruct((4, 8, SLOT), F32)],
        compiler_params=pltpu.CompilerParams(vmem_limit_bytes=60 * 1024 * 1024),
        cost_estimate=cost(T * C, T * C),
    )(one, two, gamma, beta, mine, theirs)


def mix_kernel(*refs, count, fresh):
    acts, slopes, backs = refs[:count], refs[count : 2 * count], refs[2 * count : 3 * count]
    n0, n1, c0, c1, wa, wb, v_ref = refs[3 * count : 3 * count + 7]
    rest = refs[3 * count + 7 :]
    old, rest = ([], rest) if fresh else (rest[:2], rest[2:])
    ta, tb, *outs, te, tr, we, wr = rest
    g = pl.program_id(0)
    tn = (((0,), (0,)), ((), ()))

    @pl.when(g == 0)
    def _():
        for k, w in enumerate((wa, wb)):
            we[k * SLOT : (k + 1) * SLOT, :], wr[k * SLOT : (k + 1) * SLOT, :] = split_rows(w[...])
        te[...] = jnp.zeros_like(te)
        tr[...] = jnp.zeros_like(tr)

    def pick(rs, k):
        return rs[0][k] if count == 1 else rs[k][0]

    def body(n_ref, c_ref):
        mapped, bp = [], []
        for k in range(2):
            v = v_ref[k, 0]
            p, q, beta = v[0:1], v[1:2], v[2:3]
            a = pick(acts, k).astype(F32)
            mapped.append((a * p + beta).astype(BF16))
            bp.append(((pick(backs, k).astype(F32) * p + a * q) * pick(slopes, k).astype(F32)).astype(BF16))
        mapped = jnp.concatenate(mapped, axis=1)
        bp = jnp.concatenate(bp, axis=1)
        br = lax.dot(mapped, wr[...], preferred_element_type=F32)
        bn = lax.dot(bp, we[...], preferred_element_type=F32)
        te[...] += lax.dot_general(bp, n_ref[:, :C], tn, preferred_element_type=F32)
        tr[...] += lax.dot_general(mapped, c_ref[:, :C], tn, preferred_element_type=F32)
        return br, bn

    def put(br, bn, k):
        if fresh:
            outs[0][0] = br.astype(BF16)
            outs[1][0] = bn.astype(BF16)
        else:
            for o, v, w in ((outs[k], br, old[0]), (outs[2 + k], bn, old[1])):
                o[:, :C] = (v + w[0].astype(F32)).astype(BF16)
                o[:, C:] = jnp.zeros((ROWS, CP - C), BF16)

    @pl.when(g < STEPS)
    def _():
        put(*body(n0, c0), 0)

    @pl.when(g >= STEPS)
    def _():
        put(*body(n1, c1), 1)

    @pl.when(g == 2 * STEPS - 1)
    def _():
        n = ta.shape[0]
        for k, t in enumerate((ta, tb)):
            t[:, :C] = te[k * SLOT : k * SLOT + n, :].astype(BF16)
            t[:, C:] = tr[k * SLOT : k * SLOT + n, :].astype(BF16)


def mix(sets, n0, n1, c0, c1, wa, wb, vecs, n, old):
    once = pl.Buffered(1)
    if len(sets) == 1:
        h, at = sets[0]
        acts = [(h[i], pl.BlockSpec((2, ROWS, SLOT), lambda g: (at // 2, g, 0))) for i in range(3)]
    else:
        acts = [
            (h[i], pl.BlockSpec((1, ROWS, SLOT), lambda g, at=at: (at, g, 0))) for i in range(3) for h, at in sets
        ]
    one = pl.BlockSpec((ROWS, CP), lambda g: (jnp.minimum(g, STEPS - 1), 0))
    two = pl.BlockSpec((ROWS, CP), lambda g: (jnp.maximum(g - STEPS, 0), 0))
    rows = pl.BlockSpec((n, 2 * C), lambda g: (0, 0), pipeline_mode=once)
    part = pl.BlockSpec((1, ROWS, C), lambda g: (g // STEPS, g % STEPS, 0))
    terms = jax.ShapeDtypeStruct((n, 2 * C), BF16)
    if old:
        outs, shapes = [one, two, one, two], [jax.ShapeDtypeStruct((T, CP), BF16)] * 4
    else:
        outs, shapes = [part] * 2, [jax.ShapeDtypeStruct((2, T, C), BF16)] * 2
    return pl.pallas_call(
        lambda *refs: mix_kernel(*refs, count=len(sets), fresh=not old),
        name="mix",
        grid=(2 * STEPS,),
        in_specs=[spec for _, spec in acts]
        + [one, two, one, two]
        + [rows, rows, pl.BlockSpec((2, 1, 8, SLOT), lambda g: (0, g // STEPS, 0, 0))]
        + [part] * len(old),
        out_specs=[rows, rows] + outs,
        out_shape=[terms, terms] + shapes,
        scratch_shapes=[pltpu.VMEM((2 * SLOT, C), F32)] * 2 + [pltpu.VMEM((2 * SLOT, C), BF16)] * 2,
        compiler_params=params(62),
        cost_estimate=cost(T * C, T * C),
    )(*[v for v, _ in acts], n0, n1, c0, c1, wa, wb, vecs, *old)


def image_kernel(*refs, count, last):
    acts, slopes, backs = refs[:count], refs[count : 2 * count], refs[2 * count : 3 * count]
    n_ref, c_ref, wa, wb, v_ref, old_br, old_bn = refs[3 * count : 3 * count + 7]
    rest = refs[3 * count + 7 :]
    carry, rest = (rest[:2], rest[2:]) if last else ([], rest)
    ta, tb, br, bn, te, tr, we, wr = rest
    g = pl.program_id(0)
    tn = (((0,), (0,)), ((), ()))

    @pl.when(g == 0)
    def _():
        for k, w in enumerate((wa, wb)):
            we[k * SLOT : (k + 1) * SLOT, :], wr[k * SLOT : (k + 1) * SLOT, :] = split_rows(w[...])
        te[...] = carry[0][...] if last else jnp.zeros_like(te)
        tr[...] = carry[1][...] if last else jnp.zeros_like(tr)

    mapped, bp = [], []
    for k in range(2):
        v = v_ref[k, 0]
        p, q, beta = v[0:1], v[1:2], v[2:3]
        a = acts[k][0].astype(F32)
        mapped.append((a * p + beta).astype(BF16))
        bp.append(((backs[k][0].astype(F32) * p + a * q) * slopes[k][0].astype(F32)).astype(BF16))
    mapped = jnp.concatenate(mapped, axis=1)
    bp = jnp.concatenate(bp, axis=1)
    for o, m, w, old in ((br, mapped, wr, old_br), (bn, bp, we, old_bn)):
        v = lax.dot(m, w[...], preferred_element_type=F32) + old[0].astype(F32)
        o[:, :C] = v.astype(BF16)
        o[:, C:] = jnp.zeros((ROWS, CP - C), BF16)
    te[...] += lax.dot_general(bp, n_ref[:, :C], tn, preferred_element_type=F32)
    tr[...] += lax.dot_general(mapped, c_ref[:, :C], tn, preferred_element_type=F32)

    @pl.when(g == STEPS - 1)
    def _():
        if last:
            n = ta.shape[0]
            for k, t in enumerate((ta, tb)):
                t[:, :C] = te[k * SLOT : k * SLOT + n, :].astype(BF16)
                t[:, C:] = tr[k * SLOT : k * SLOT + n, :].astype(BF16)
        else:
            ta[...] = te[...]
            tb[...] = tr[...]


def mix_image(sets, n_own, c_own, wa, wb, vecs, n, old, im, carry):
    once = pl.Buffered(1)
    last = bool(carry)
    acts = [
        (h[i], pl.BlockSpec((1, ROWS, SLOT), lambda g, at=at: (at, g + im * STEPS, 0))) for i in range(3) for h, at in sets
    ]
    one = pl.BlockSpec((ROWS, CP), lambda g: (g, 0))
    rows = pl.BlockSpec((n, 2 * C), lambda g: (0, 0), pipeline_mode=once)
    sums = pl.BlockSpec((2 * SLOT, C), lambda g: (0, 0), pipeline_mode=once)
    part = pl.BlockSpec((1, ROWS, C), lambda g: (im, g, 0))
    if last:
        outs, shapes = [rows] * 2, [jax.ShapeDtypeStruct((n, 2 * C), BF16)] * 2
    else:
        outs, shapes = [sums] * 2, [jax.ShapeDtypeStruct((2 * SLOT, C), F32)] * 2
    return pl.pallas_call(
        lambda *refs: image_kernel(*refs, count=len(sets), last=last),
        name="mix_image",
        grid=(STEPS,),
        in_specs=[spec for _, spec in acts]
        + [one, one, rows, rows, pl.BlockSpec((2, 1, 8, SLOT), lambda g: (0, im, 0, 0)), part, part]
        + [sums] * len(carry),
        out_specs=outs + [one, one],
        out_shape=shapes + [jax.ShapeDtypeStruct((T, CP), BF16)] * 2,
        scratch_shapes=[pltpu.VMEM((2 * SLOT, C), F32)] * 2 + [pltpu.VMEM((2 * SLOT, C), BF16)] * 2,
        compiler_params=params(62),
        cost_estimate=cost(T * C, T * C),
    )(*[v for v, _ in acts], n_own, c_own, wa, wb, vecs, *old, *carry)


def unnorm_kernel(b0, b1, xhat, rstd, gain, d_ref, gg_ref, *, step):
    @pl.when(pl.program_id(0) == 0)
    def _():
        gg_ref[...] = jnp.zeros_like(gg_ref)

    def rows(i, carry):
        at = pl.ds(pl.multiple_of(i * W, W), W)
        bn = b0[at, :C].astype(F32) + b1[at, :C].astype(F32)
        xh = xhat[at, :]
        g = bn * gain[0:1, :]
        m1 = jnp.sum(g, axis=1, keepdims=True) * (1.0 / C)
        m2 = jnp.sum(g * xh, axis=1, keepdims=True) * (1.0 / C)
        r = rstd[at, 0:1]
        d_ref[at, :] = r * (g - m1 - xh * m2)
        gg_ref[...] += jnp.sum((bn * xh).reshape(W // 8, 8, C), axis=0)
        return carry

    lax.fori_loop(0, step // W, rows, 0, unroll=True)


def unnorm(b0, b1, xhat, rstd, gain):
    step = T // 4
    full = pl.BlockSpec((step, C), lambda r: (r, 0))
    wide = pl.BlockSpec((step, CP), lambda r: (r, 0))
    return pl.pallas_call(
        lambda *refs: unnorm_kernel(*refs, step=step),
        name="unnorm",
        grid=(T // step,),
        in_specs=[wide, wide, full, pl.BlockSpec((step, CB), lambda r: (r, 0)), pl.BlockSpec((1, C), lambda r: (0, 0))],
        out_specs=[full, pl.BlockSpec((8, C), lambda r: (0, 0))],
        out_shape=[jax.ShapeDtypeStruct((T, C), F32), jax.ShapeDtypeStruct((8, C), F32)],
        compiler_params=params(60),
        cost_estimate=cost(T * C, T * C),
    )(b0, b1, xhat, rstd, gain.reshape(1, C))


def taps_kernel(x_ref, d_ref, g_ref, pad):
    @pl.when(pl.program_id(0) == 0)
    def _():
        pad[...] = jnp.zeros_like(pad)

    for i in range(S):
        pad[pl.ds(HEAD + i * W, S), :] = x_ref[i].astype(F32)

    for b in range(7):
        def cols(jv, acc):
            base = jv * 8
            acc = list(acc)
            d = {}
            for r in range(S):
                if r == 0:
                    for i in range(4):
                        d[i] = d_ref[pl.ds(i * W + base, 8), :]
                elif r + 3 < S:
                    d[r + 3] = d_ref[pl.ds((r + 3) * W + base, 8), :]
                v = pad[pl.ds(r * W + HEAD + b - 3 + base, 8), :]
                for a in range(7):
                    i = r + 3 - a
                    if 0 <= i < S:
                        acc[a] = acc[a] + d[i] * v
            return tuple(acc)

        acc = (jnp.zeros((8, CB), F32),) * 7
        for jv in range(W // 8):
            acc = cols(jv, acc)
        for a in range(7):
            g_ref[pl.ds(a * 7 + b, 1), :] = jnp.sum(acc[a], axis=0, keepdims=True)


def taps(x, d, at):
    return pl.pallas_call(
        taps_kernel,
        name="taps",
        grid=(HALF,),
        in_specs=[pl.BlockSpec((S, S, CB), lambda c: (0, 0, c + at)), pl.BlockSpec((T, CB), lambda c: (0, c + at))],
        out_specs=pl.BlockSpec((49, CB), lambda c: (0, c)),
        out_shape=jax.ShapeDtypeStruct((49, HALF * CB), F32),
        scratch_shapes=[pltpu.VMEM((T + 2 * HEAD, CB), F32)],
        compiler_params=params(60),
        cost_estimate=cost(T * C, T * C),
    )(x, d)


def unstem_kernel(d_ref, k_ref, c_ref, old_ref, o_ref, pad, res):
    @pl.when(pl.program_id(0) == 0)
    def _():
        pad[...] = jnp.zeros_like(pad)

    pad[pl.ds(HEAD, T), :] = d_ref[...]
    conv_taps(pad, k_ref, res, True)
    for i in range(S):
        o_ref[i] = (c_ref[i].astype(F32) + res[pl.ds(i * W, S), :]).astype(BF16)


def unstem(d, k, cot, old, at, count):
    return pl.pallas_call(
        unstem_kernel if old is not None else (lambda d, k, c, *r: unstem_kernel(d, k, c, None, *r)),
        name="unstem",
        grid=(count,),
        in_specs=[
            pl.BlockSpec((T, CB), lambda c: (0, c + at)),
            pl.BlockSpec((49, CB), lambda c: (0, c + at)),
            pl.BlockSpec((S, S, CB), lambda c: (0, 0, c + at)),
        ]
        + ([pl.BlockSpec(memory_space=pl.ANY)] if old is not None else []),
        out_specs=pl.BlockSpec((S, S, CB), lambda c: (0, 0, c + at)),
        out_shape=jax.ShapeDtypeStruct((S, S, C), BF16),
        scratch_shapes=[pltpu.VMEM((T + 2 * HEAD, CB), F32), pltpu.VMEM((T, CB), F32)],
        input_output_aliases={3: 0} if old is not None else {},
        compiler_params=params(60),
        cost_estimate=cost(T * C, T * C),
    )(d, k, cot, *([old] if old is not None else []))


PART = 7


def finish_kernel(x_ref, b0, b1, o_ref):
    for i in range(PART):
        at = slice(i * W, (i + 1) * W)
        t = b0[at, :].astype(F32) + b1[at, :].astype(F32)
        o_ref[i] = (x_ref[i].astype(F32) + t[:S, :C]).astype(BF16)


def finish(x, b0, b1):
    maps = pl.BlockSpec((PART, S, C), lambda r: (r, 0, 0))
    rows = pl.BlockSpec((PART * W, CP), lambda r: (r, 0))
    return pl.pallas_call(
        finish_kernel,
        name="finish",
        grid=(S // PART,),
        in_specs=[maps, rows, rows],
        out_specs=maps,
        out_shape=jax.ShapeDtypeStruct((S, S, C), BF16),
        compiler_params=params(60),
        cost_estimate=cost(T * C, T * C),
    )(x, b0, b1)


SHIFTS = (0, -1, 1, 2)
AXES = ("rep", "shard")


def place(x, y, z, c):
    return ((y * 2 + z % 2) * 2 + c) * 8 + x * 2 + z // 2


def moves(fn):
    pairs = []
    for x in range(4):
        for y in range(4):
            for z in range(4):
                for c in range(2):
                    nx, ny, nz, nc = fn(x, y, z, c)
                    pairs.append((place(x, y, z, c), place(nx % 4, ny % 4, nz % 4, nc)))
    return pairs


def along_x(d):
    return lambda x, y, z, c: (x + d, y, z, c)


def along_y(d):
    return lambda x, y, z, c: (x, y + d, z, c)


def minor(d):
    return lambda x, y, z, c: (x, y, z + d, c) if c == 0 else (x + d, y, z, c)


def major(d):
    return lambda x, y, z, c: (x + d, y, z, c) if c == 0 else (x, y, z + d, c)


def swap_core(x, y, z, c):
    return (x, y, z, 1 - c)


def swap_zlo(x, y, z, c):
    return (x, y, z + 1 - 2 * (z % 2), c)


def send(v, fn):
    return lax.ppermute(v, AXES, moves(fn))


def spread(v, axis_fn):
    return [v] + [send(v, axis_fn(-d)) for d in SHIFTS[1:]]


def turn(v, start):
    size = v.shape[0]
    return lax.dynamic_slice_in_dim(jnp.concatenate([v, v], axis=0), start, size, axis=0)


ORDER = (0, 3, 1, 2)
BACK = (0, 2, 3, 1)
SLOTS = (3, 1, 2, 0)


def add_up(parts):
    total = parts[0].astype(F32)
    for g in parts[1:]:
        total = total + g.astype(F32)
    return total


def after(v, *done):
    return lax.optimization_barrier((v,) + done)[0]


def shards(features, cotangent, dw_kernel, norm_gain, w_expand, grn_gamma, grn_beta, w_reduce):
    rep = lax.axis_index("rep")
    shard = lax.axis_index("shard")
    c = rep % 2
    zl = (rep // 2) % 2
    x = shard // 2
    z = (shard % 2) * 2 + zl
    hid = grn_gamma.shape[0]
    piece = hid // 32
    n = 4 * piece
    img = features[0]
    cot = cotangent[0]

    first = c * (2 * piece) + zl * piece
    own = jnp.concatenate([lax.dynamic_slice_in_dim(w, first, piece, axis=0) for w in (w_expand, w_reduce)], axis=1)
    filt = conv(img, dw_kernel, 0, 2)
    row = jnp.concatenate(spread(own, minor), axis=0)
    ws = spread(row, major)

    def to_own(v):
        v = lax.dynamic_index_in_dim(v.reshape(4, 2, 2, 2, piece), c, axis=2, keepdims=False).reshape(4, 4, piece)
        v = turn(v, x).transpose(1, 0, 2)
        v = turn(v, z)
        v = jnp.where(c == 0, v.transpose(1, 0, 2), v)
        v = jnp.stack([v[ORDER[k]] for k in SLOTS])
        v = jnp.stack([v[:, k] for k in ORDER], axis=1)
        return jnp.pad(v.reshape(1, 4, n), ((0, 0), (0, 0), (0, SLOT - n)))

    def to_all(v):
        v = v[:, :n].reshape(4, 4, piece)
        v = jnp.stack([v[SLOTS.index(k)] for k in BACK])
        v = jnp.stack([v[:, k] for k in BACK], axis=1)
        v = jnp.where(c == 0, v, v.transpose(1, 0, 2))
        v = turn(v, (4 - x) % 4).transpose(1, 0, 2)
        v = turn(v, (4 - z) % 4).transpose(1, 0, 2).reshape(4, 2, 1, 2, piece)
        zero = jnp.zeros_like(v)
        both = jnp.where(c == 0, jnp.concatenate([v, zero], axis=2), jnp.concatenate([zero, v], axis=2))
        return both.reshape(4, hid // 4)

    gamma = to_own(grn_gamma)
    beta = to_own(grn_beta)
    valid = (jnp.arange(SLOT) < n).astype(F32)

    c0 = widen(cot)
    c1 = send(c0, swap_core)
    rest = conv(after(img, row, c1), dw_kernel, 2, NCB - 2)
    n0, xhat, rstd = norm(filt, after(rest, ws[1], ws[2]), norm_gain)
    n1 = send(n0, swap_core)
    h0 = hidden(n0, n1, c0, c1, [row])
    h3 = hidden(after(n0, h0[3]), n1, c0, c1, [ws[3], ws[1], ws[2]])
    gamma3, beta3 = gamma.reshape(4, 1, SLOT), beta.reshape(4, 1, SLOT)
    mine = tally(h3[3], h0[3], gamma3, valid)
    vec_a, vec_b, back = vectors(h3[3], h0[3], gamma3, beta3, mine, send(mine, swap_core), hid)
    back_gamma = to_all(back[:, 0])
    back_beta = to_all(back[:, 1])
    t3, t1, *part = mix([(h3, 0)], n0, n1, c0, c1, ws[3], ws[1], vec_a, n, ())
    s3, s1 = send(t3, major(SHIFTS[3])), send(t1, major(SHIFTS[1]))
    sets = [(h3, 2), (h0, 0)]
    e1, r1, br1, bn1 = mix_image(sets, n1, c1, ws[2], ws[0], vec_b, n, part, 1, ())
    bn1_in = send(bn1, swap_core)
    t2, t0, br0, bn0 = mix_image(sets, n0, c0, ws[2], ws[0], vec_b, n, part, 0, (e1, r1))
    s2 = send(t2, major(SHIFTS[2]))
    br1_in = send(after(br1, bn1_in), swap_core)
    d, gain_rows = unnorm(bn0, bn1_in, xhat, rstd, norm_gain)
    taps_a = taps(img, d, 0)
    part = add_up([after(t0, taps_a), s1, s2, s3]).astype(BF16)
    part = [part[k * piece : (k + 1) * piece] for k in range(4)]
    part = [part[0]] + [send(part[k], minor(SHIFTS[k])) for k in (1, 2, 3)]
    taps_b = taps(after(img, part[0]), d, HALF)[:, : C - HALF * CB]
    part = add_up([after(part[0], taps_b)] + part[1:]).astype(BF16)
    grad_taps = jnp.concatenate([taps_a, taps_b], axis=1)
    small = jnp.concatenate([grad_taps, jnp.sum(gain_rows, axis=0, keepdims=True), back_gamma, back_beta], axis=0)
    small = jnp.pad(small, ((0, 6), (0, 0))).astype(BF16)
    merged = jnp.concatenate([part, jnp.concatenate([small[:32], small[32:]], axis=1)], axis=0)
    merged = [merged] + [send(merged, along_y(s)) for s in SHIFTS[1:]]
    inverse = 1.0 / (features.shape[0] * lax.axis_size("rep") * lax.axis_size("shard"))
    grad_features = unstem(after(d, merged[0]), dw_kernel, cot, None, 0, 3)
    block_out = finish(after(img, grad_features), br0, br1_in)
    merged = add_up([after(merged[0], block_out)] + merged[1:])
    total = (merged[:piece] * inverse).astype(BF16)
    small = merged[piece:].astype(BF16)
    other = send(total, swap_zlo)
    small = [small] + [send(small, minor(s)) for s in SHIFTS[1:]]
    grad_features = unstem(after(d, small[0], total), dw_kernel, cot, grad_features, 3, 1)
    total = after(total, grad_features)
    total = jnp.where(zl == 0, jnp.concatenate([total, other], axis=0), jnp.concatenate([other, total], axis=0))
    other = send(total, swap_core)
    small = add_up([after(small[0], grad_features)] + small[1:]).astype(BF16)
    small = [small] + [send(small, major(s)) for s in SHIFTS[1:]]
    grad_features = unstem(after(d, small[0], total), dw_kernel, cot, grad_features, 4, 2)
    small = add_up([after(small[0], grad_features)] + small[1:]).astype(BF16)
    far = send(small, swap_core)
    total = after(total, small)
    lo = jnp.where(c == 0, total, other)
    hi = jnp.where(c == 0, other, total)
    total = jnp.concatenate([lo, hi], axis=0).astype(F32)
    small = (after(small, total).astype(F32) + far.astype(F32)) * inverse
    small = jnp.concatenate([small[:, :C], small[:, C:]], axis=0)
    return (
        block_out[None],
        grad_features[None],
        small[:49],
        small[49],
        total[:, :C],
        small[50:54].reshape(hid),
        small[54:58].reshape(hid),
        total[:, C:],
    )


def solution(mesh):
    data = P(AXES, None, None, None)
    rows = P("shard", None)
    return jax.shard_map(
        shards,
        mesh=mesh,
        in_specs=(data, data, P(), P(), rows, P(), P(), rows),
        out_specs=(data, data, P(), P(), rows, P(), P(), rows),
        check_vma=False,
    )
```

```python
import jax
import jax.numpy as jnp
from jax import lax
from jax.sharding import PartitionSpec as P
from jax.experimental import pallas as pl
from jax.experimental.pallas import tpu as pltpu

S, W, C = 28, 32, 704
T = S * W
CB = 128
NCB = 6
HEAD = 8
CP = NCB * CB
HALF = NCB // 2
SLOT = 384
F32, BF16 = jnp.float32, jnp.bfloat16


def params(mib=63, n=1):
    return pltpu.CompilerParams(vmem_limit_bytes=mib * 1024 * 1024, dimension_semantics=("arbitrary",) * n)


def cost(flops, nbytes):
    return pl.CostEstimate(flops=int(flops), bytes_accessed=int(nbytes), transcendentals=0)


def conv_taps(src, k_ref, dst, flip):
    def cols(jv, carry):
        base = jv * 8
        acc = [None] * S
        for b in range(7):
            taps = []
            for a in range(7):
                at = (6 - a) * 7 + (6 - b) if flip else a * 7 + b
                taps.append(jnp.broadcast_to(k_ref[pl.ds(at, 1), :], (8, CB)))
            for r in range(S):
                v = src[pl.ds(r * W + HEAD + b - 3 + base, 8), :]
                for a in range(7):
                    i = r + 3 - a
                    if 0 <= i < S:
                        t = taps[a] * v
                        acc[i] = t if acc[i] is None else acc[i] + t
        for i in range(S):
            dst[pl.ds(i * W + base, 8), :] = acc[i]
        return carry

    for jv in range(W // 8):
        cols(jv, 0)


def load_map(x_ref, pad):
    for i in range(S):
        pad[pl.ds(HEAD + i * W, S), :] = x_ref[i].astype(F32)


def conv_kernel(x_ref, k_ref, filt_ref, pad):
    @pl.when(pl.program_id(0) == 0)
    def _():
        pad[...] = jnp.zeros_like(pad)

    load_map(x_ref, pad)
    conv_taps(pad, k_ref, filt_ref.at[0], False)


def conv(x, k, at, count):
    return pl.pallas_call(
        conv_kernel,
        name="conv",
        grid=(count,),
        in_specs=[pl.BlockSpec((S, S, CB), lambda c: (0, 0, c + at)), pl.BlockSpec((49, CB), lambda c: (0, c + at))],
        out_specs=pl.BlockSpec((1, T, CB), lambda c: (c, 0, 0)),
        out_shape=jax.ShapeDtypeStruct((count, T, CB), F32),
        scratch_shapes=[pltpu.VMEM((T + 2 * HEAD, CB), F32)],
        compiler_params=params(63),
        cost_estimate=cost(T * C, T * C),
    )(x, k)


NORM = 224


def norm_kernel(one_ref, two_ref, gain_ref, normed_ref, xhat_ref, rstd_ref):
    lane = lax.broadcasted_iota(jnp.int32, (W, CB), 1)
    row = lax.broadcasted_iota(jnp.int32, (W, CB), 0)
    last = lane < C - (NCB - 1) * CB
    inside = row < S
    for i in range(NORM // W):
        at = slice(i * W, (i + 1) * W)
        v = [r[c, at, :] for r in (one_ref, two_ref) for c in range(r.shape[0])]
        v[-1] = jnp.where(last, v[-1], 0.0)
        total = v[0]
        for c in range(1, NCB):
            total = total + v[c]
        mean = jnp.sum(total, axis=1, keepdims=True) * (1.0 / C)
        d = [u - mean for u in v]
        d[-1] = jnp.where(last, d[-1], 0.0)
        total = d[0] * d[0]
        for c in range(1, NCB):
            total = total + d[c] * d[c]
        spread = jnp.sum(total, axis=1, keepdims=True) * (1.0 / C)
        rstd = jnp.broadcast_to(lax.rsqrt(spread + 1e-06), (W, CB))
        rstd_ref[at, :] = rstd
        for c in range(NCB):
            n = min(CB, C - c * CB)
            xh = jnp.where(inside, d[c] * rstd, 0.0)
            xhat_ref[at, c * CB : c * CB + n] = xh[:, :n]
            g = jnp.broadcast_to(gain_ref[0:1, c * CB : (c + 1) * CB], (W, CB))
            normed_ref[at, c * CB : (c + 1) * CB] = (xh * g).astype(BF16)


def norm(one, two, gain):
    return pl.pallas_call(
        norm_kernel,
        name="norm",
        grid=(T // NORM,),
        in_specs=[
            pl.BlockSpec((one.shape[0], NORM, CB), lambda r: (0, r, 0)),
            pl.BlockSpec((two.shape[0], NORM, CB), lambda r: (0, r, 0)),
            pl.BlockSpec((1, CP), lambda r: (0, 0)),
        ],
        out_specs=[
            pl.BlockSpec((NORM, CP), lambda r: (r, 0)),
            pl.BlockSpec((NORM, C), lambda r: (r, 0)),
            pl.BlockSpec((NORM, CB), lambda r: (r, 0)),
        ],
        out_shape=[
            jax.ShapeDtypeStruct((T, CP), BF16),
            jax.ShapeDtypeStruct((T, C), F32),
            jax.ShapeDtypeStruct((T, CB), F32),
        ],
        compiler_params=params(63),
        cost_estimate=cost(T * C, T * C),
    )(one, two, jnp.pad(gain, (0, CP - C)).reshape(1, CP))


def widen_kernel(x_ref, y_ref):
    zero = jnp.zeros((W - S, C), F32)
    y_ref[:, C:] = jnp.zeros((T, CP - C), BF16)
    for i in range(S):
        y_ref[pl.ds(i * W, W), :C] = jnp.concatenate([x_ref[i].astype(F32), zero], axis=0).astype(BF16)


def widen(x):
    return pl.pallas_call(
        widen_kernel,
        name="widen",
        out_shape=jax.ShapeDtypeStruct((T, CP), BF16),
        compiler_params=pltpu.CompilerParams(vmem_limit_bytes=63 * 1024 * 1024),
        cost_estimate=cost(T * C, T * C),
    )(x)


def gelu_pair(x):
    mag = jnp.abs(x)
    e = jnp.exp2((x * x) * -0.7213475204444817)
    t = 1.0 / (1.0 + (0.3275911 * 0.7071067811865476) * mag)
    poly = (((0.5307027145 * t - 0.7265760135) * t + 0.7107068705) * t - 0.142248368) * t + 0.127414796
    tail = poly * (t * e)
    cdf = jnp.where(x < 0.0, tail, 1.0 - tail)
    return x * cdf, cdf + (0.3989422804014327 * x) * e


def split_rows(w):
    zero = jnp.zeros((SLOT - w.shape[0], C), BF16)
    return jnp.concatenate([w[:, :C], zero], axis=0), jnp.concatenate([w[:, C:], zero], axis=0)


ROWS = 448
STEPS = T // ROWS


def hidden_kernel(n0, n1, c0, c1, *refs, count):
    ws = refs[:count]
    act_ref, slope_ref, back_ref, stat_ref = refs[-4:]
    g = pl.program_id(0)
    nt = (((1,), (1,)), ((), ()))

    def body(n_ref, c_ref):
        for k in range(count):
            we, wr = split_rows(ws[k][...])
            pre = lax.dot_general(n_ref[:, :C], we, nt, preferred_element_type=F32)
            dm = lax.dot_general(c_ref[:, :C], wr, nt, preferred_element_type=F32)
            act, slope = gelu_pair(pre)
            act_ref[k] = act.astype(BF16)
            slope_ref[k] = slope.astype(BF16)
            back_ref[k] = dm.astype(BF16)
            e2 = jnp.sum(act * act, axis=0, keepdims=True)
            s1 = jnp.sum(dm * act, axis=0, keepdims=True)
            s0 = jnp.sum(dm, axis=0, keepdims=True)
            stat_ref[k, 0] += jnp.concatenate([e2, s1, s0, jnp.zeros((5, SLOT), F32)], axis=0)

    @pl.when(g % STEPS == 0)
    def _():
        stat_ref[...] = jnp.zeros_like(stat_ref)

    @pl.when(g < STEPS)
    def _():
        body(n0, c0)

    @pl.when(g >= STEPS)
    def _():
        body(n1, c1)


def hidden(n0, n1, c0, c1, ws):
    count = len(ws)
    wide = pl.BlockSpec((count, ROWS, SLOT), lambda g: (0, g, 0))
    one = pl.BlockSpec((ROWS, CP), lambda g: (jnp.minimum(g, STEPS - 1), 0))
    two = pl.BlockSpec((ROWS, CP), lambda g: (jnp.maximum(g - STEPS, 0), 0))
    return pl.pallas_call(
        lambda *refs: hidden_kernel(*refs, count=count),
        name="hidden",
        grid=(2 * STEPS,),
        in_specs=[one, two, one, two] + [pl.BlockSpec(ws[0].shape, lambda g: (0, 0))] * count,
        out_specs=[wide, wide, wide, pl.BlockSpec((count, 1, 8, SLOT), lambda g: (0, g // STEPS, 0, 0))],
        out_shape=[jax.ShapeDtypeStruct((count, 2 * T, SLOT), BF16)] * 3
        + [jax.ShapeDtypeStruct((count, 2, 8, SLOT), F32)],
        compiler_params=params(63),
        cost_estimate=cost(T * C, T * C),
    )(n0, n1, c0, c1, *ws)


def full_sum(v):
    return jnp.sum(jnp.sum(jnp.sum(v, axis=0), axis=0, keepdims=True), axis=1, keepdims=True)


def stat_row(refs, im, at):
    return jnp.concatenate([r[:, im, at : at + 1, :] for r in refs], axis=0)


def tally_kernel(one, two, gamma_ref, valid_ref, o_ref):
    rows = []
    for im in range(2):
        energy = jnp.sqrt(stat_row((one, two), im, 0) + 1e-06)
        rows.append(jnp.broadcast_to(full_sum(energy * valid_ref[...]), (1, CB)))
        rows.append(jnp.broadcast_to(full_sum(gamma_ref[...] * stat_row((one, two), im, 1) * energy), (1, CB)))
    o_ref[...] = jnp.concatenate(rows + [jnp.zeros((4, CB), F32)], axis=0)


def tally(one, two, gamma, valid):
    return pl.pallas_call(
        tally_kernel,
        name="tally",
        out_shape=jax.ShapeDtypeStruct((8, CB), F32),
        compiler_params=pltpu.CompilerParams(vmem_limit_bytes=63 * 1024 * 1024),
        cost_estimate=cost(T * C, T * C),
    )(one, two, gamma, valid)


def vectors_kernel(one, two, gamma_ref, beta_ref, mine, theirs, va_ref, vb_ref, g_ref, *, hid):
    gamma = gamma_ref[...]
    back_gamma = back_beta = 0.0
    for im in range(2):
        far = 2 * (1 - im)
        e_all = (mine[2 * im : 2 * im + 1, 0:1] + theirs[far : far + 1, 0:1]).reshape(1, 1, 1)
        d_all = (mine[2 * im + 1 : 2 * im + 2, 0:1] + theirs[far + 1 : far + 2, 0:1]).reshape(1, 1, 1)
        energy = jnp.sqrt(stat_row((one, two), im, 0) + 1e-06)
        s1 = stat_row((one, two), im, 1)
        inv = 1.0 / (e_all * (1.0 / hid) + 1e-06)
        ratio = energy * inv
        pull = (gamma * s1 * inv - d_all * (1.0 / hid) * inv * inv) / energy
        for at, row in enumerate((1.0 + gamma * ratio, pull, beta_ref[...])):
            va_ref[:, im, at : at + 1, :] = row[:2]
            vb_ref[:, im, at : at + 1, :] = row[2:]
        va_ref[:, im, 3:8, :] = jnp.zeros((2, 5, SLOT), F32)
        vb_ref[:, im, 3:8, :] = jnp.zeros((2, 5, SLOT), F32)
        back_gamma = back_gamma + ratio * s1
        back_beta = back_beta + stat_row((one, two), im, 2)
    g_ref[:, 0:1, :] = back_gamma
    g_ref[:, 1:2, :] = back_beta
    g_ref[:, 2:8, :] = jnp.zeros((4, 6, SLOT), F32)


def vectors(one, two, gamma, beta, mine, theirs, hid):
    return pl.pallas_call(
        lambda *refs: vectors_kernel(*refs, hid=hid),
        name="vectors",
        out_shape=[jax.ShapeDtypeStruct((2, 2, 8, SLOT), F32)] * 2 + [jax.ShapeDtypeStruct((4, 8, SLOT), F32)],
        compiler_params=pltpu.CompilerParams(vmem_limit_bytes=63 * 1024 * 1024),
        cost_estimate=cost(T * C, T * C),
    )(one, two, gamma, beta, mine, theirs)


def mix_kernel(*refs, count, fresh):
    acts, slopes, backs = refs[:count], refs[count : 2 * count], refs[2 * count : 3 * count]
    n0, n1, c0, c1, wa, wb, v_ref = refs[3 * count : 3 * count + 7]
    rest = refs[3 * count + 7 :]
    old, rest = ([], rest) if fresh else (rest[:2], rest[2:])
    ta, tb, *outs, te, tr, we, wr = rest
    g = pl.program_id(0)
    tn = (((0,), (0,)), ((), ()))

    @pl.when(g == 0)
    def _():
        for k, w in enumerate((wa, wb)):
            we[k * SLOT : (k + 1) * SLOT, :], wr[k * SLOT : (k + 1) * SLOT, :] = split_rows(w[...])
        te[...] = jnp.zeros_like(te)
        tr[...] = jnp.zeros_like(tr)

    def pick(rs, k):
        return rs[0][k] if count == 1 else rs[k][0]

    def body(n_ref, c_ref):
        mapped, bp = [], []
        for k in range(2):
            v = v_ref[k, 0]
            p, q, beta = v[0:1], v[1:2], v[2:3]
            a = pick(acts, k).astype(F32)
            mapped.append((a * p + beta).astype(BF16))
            bp.append(((pick(backs, k).astype(F32) * p + a * q) * pick(slopes, k).astype(F32)).astype(BF16))
        mapped = jnp.concatenate(mapped, axis=1)
        bp = jnp.concatenate(bp, axis=1)
        br = lax.dot(mapped, wr[...], preferred_element_type=F32)
        bn = lax.dot(bp, we[...], preferred_element_type=F32)
        te[...] += lax.dot_general(bp, n_ref[:, :C], tn, preferred_element_type=F32)
        tr[...] += lax.dot_general(mapped, c_ref[:, :C], tn, preferred_element_type=F32)
        return br, bn

    def put(br, bn, k):
        if fresh:
            outs[0][0] = br.astype(BF16)
            outs[1][0] = bn.astype(BF16)
        else:
            for o, v, w in ((outs[k], br, old[0]), (outs[2 + k], bn, old[1])):
                o[:, :C] = (v + w[0].astype(F32)).astype(BF16)
                o[:, C:] = jnp.zeros((ROWS, CP - C), BF16)

    @pl.when(g < STEPS)
    def _():
        put(*body(n0, c0), 0)

    @pl.when(g >= STEPS)
    def _():
        put(*body(n1, c1), 1)

    @pl.when(g == 2 * STEPS - 1)
    def _():
        n = ta.shape[0]
        for k, t in enumerate((ta, tb)):
            t[:, :C] = te[k * SLOT : k * SLOT + n, :].astype(BF16)
            t[:, C:] = tr[k * SLOT : k * SLOT + n, :].astype(BF16)


def mix(sets, n0, n1, c0, c1, wa, wb, vecs, n, old):
    once = pl.Buffered(1)
    if len(sets) == 1:
        h, at = sets[0]
        acts = [(h[i], pl.BlockSpec((2, ROWS, SLOT), lambda g: (at // 2, g, 0))) for i in range(3)]
    else:
        acts = [
            (h[i], pl.BlockSpec((1, ROWS, SLOT), lambda g, at=at: (at, g, 0))) for i in range(3) for h, at in sets
        ]
    one = pl.BlockSpec((ROWS, CP), lambda g: (jnp.minimum(g, STEPS - 1), 0))
    two = pl.BlockSpec((ROWS, CP), lambda g: (jnp.maximum(g - STEPS, 0), 0))
    rows = pl.BlockSpec((n, 2 * C), lambda g: (0, 0), pipeline_mode=once)
    part = pl.BlockSpec((1, ROWS, C), lambda g: (g // STEPS, g % STEPS, 0))
    terms = jax.ShapeDtypeStruct((n, 2 * C), BF16)
    if old:
        outs, shapes = [one, two, one, two], [jax.ShapeDtypeStruct((T, CP), BF16)] * 4
    else:
        outs, shapes = [part] * 2, [jax.ShapeDtypeStruct((2, T, C), BF16)] * 2
    return pl.pallas_call(
        lambda *refs: mix_kernel(*refs, count=len(sets), fresh=not old),
        name="mix",
        grid=(2 * STEPS,),
        in_specs=[spec for _, spec in acts]
        + [one, two, one, two]
        + [rows, rows, pl.BlockSpec((2, 1, 8, SLOT), lambda g: (0, g // STEPS, 0, 0))]
        + [part] * len(old),
        out_specs=[rows, rows] + outs,
        out_shape=[terms, terms] + shapes,
        scratch_shapes=[pltpu.VMEM((2 * SLOT, C), F32)] * 2 + [pltpu.VMEM((2 * SLOT, C), BF16)] * 2,
        compiler_params=params(63),
        cost_estimate=cost(T * C, T * C),
    )(*[v for v, _ in acts], n0, n1, c0, c1, wa, wb, vecs, *old)


def unnorm_kernel(b0, b1, xhat, rstd, gain, d_ref, gg_ref, *, step):
    @pl.when(pl.program_id(0) == 0)
    def _():
        gg_ref[...] = jnp.zeros_like(gg_ref)

    def rows(i, carry):
        at = pl.ds(pl.multiple_of(i * W, W), W)
        bn = b0[at, :C].astype(F32) + b1[at, :C].astype(F32)
        xh = xhat[at, :]
        g = bn * gain[0:1, :]
        m1 = jnp.sum(g, axis=1, keepdims=True) * (1.0 / C)
        m2 = jnp.sum(g * xh, axis=1, keepdims=True) * (1.0 / C)
        r = rstd[at, 0:1]
        d_ref[at, :] = r * (g - m1 - xh * m2)
        gg_ref[...] += jnp.sum((bn * xh).reshape(W // 8, 8, C), axis=0)
        return carry

    lax.fori_loop(0, step // W, rows, 0, unroll=True)


def unnorm(b0, b1, xhat, rstd, gain):
    step = T // 4
    full = pl.BlockSpec((step, C), lambda r: (r, 0))
    wide = pl.BlockSpec((step, CP), lambda r: (r, 0))
    return pl.pallas_call(
        lambda *refs: unnorm_kernel(*refs, step=step),
        name="unnorm",
        grid=(T // step,),
        in_specs=[wide, wide, full, pl.BlockSpec((step, CB), lambda r: (r, 0)), pl.BlockSpec((1, C), lambda r: (0, 0))],
        out_specs=[full, pl.BlockSpec((8, C), lambda r: (0, 0))],
        out_shape=[jax.ShapeDtypeStruct((T, C), F32), jax.ShapeDtypeStruct((8, C), F32)],
        compiler_params=params(63),
        cost_estimate=cost(T * C, T * C),
    )(b0, b1, xhat, rstd, gain.reshape(1, C))


def taps_kernel(x_ref, d_ref, g_ref, pad):
    @pl.when(pl.program_id(0) == 0)
    def _():
        pad[...] = jnp.zeros_like(pad)

    for i in range(S):
        pad[pl.ds(HEAD + i * W, S), :] = x_ref[i].astype(F32)

    for b in range(7):
        def cols(jv, acc):
            base = jv * 8
            acc = list(acc)
            d = {}
            for r in range(S):
                if r == 0:
                    for i in range(4):
                        d[i] = d_ref[pl.ds(i * W + base, 8), :]
                elif r + 3 < S:
                    d[r + 3] = d_ref[pl.ds((r + 3) * W + base, 8), :]
                v = pad[pl.ds(r * W + HEAD + b - 3 + base, 8), :]
                for a in range(7):
                    i = r + 3 - a
                    if 0 <= i < S:
                        acc[a] = acc[a] + d[i] * v
            return tuple(acc)

        acc = (jnp.zeros((8, CB), F32),) * 7
        for jv in range(W // 8):
            acc = cols(jv, acc)
        for a in range(7):
            g_ref[pl.ds(a * 7 + b, 1), :] = jnp.sum(acc[a], axis=0, keepdims=True)


def taps(x, d, at):
    return pl.pallas_call(
        taps_kernel,
        name="taps",
        grid=(HALF,),
        in_specs=[pl.BlockSpec((S, S, CB), lambda c: (0, 0, c + at)), pl.BlockSpec((T, CB), lambda c: (0, c + at))],
        out_specs=pl.BlockSpec((49, CB), lambda c: (0, c)),
        out_shape=jax.ShapeDtypeStruct((49, HALF * CB), F32),
        scratch_shapes=[pltpu.VMEM((T + 2 * HEAD, CB), F32)],
        compiler_params=params(63),
        cost_estimate=cost(T * C, T * C),
    )(x, d)


def unstem_kernel(d_ref, k_ref, c_ref, old_ref, o_ref, pad, res):
    @pl.when(pl.program_id(0) == 0)
    def _():
        pad[...] = jnp.zeros_like(pad)

    pad[pl.ds(HEAD, T), :] = d_ref[...]
    conv_taps(pad, k_ref, res, True)
    for i in range(S):
        o_ref[i] = (c_ref[i].astype(F32) + res[pl.ds(i * W, S), :]).astype(BF16)


def unstem(d, k, cot, old, at, count):
    return pl.pallas_call(
        unstem_kernel if old is not None else (lambda d, k, c, *r: unstem_kernel(d, k, c, None, *r)),
        name="unstem",
        grid=(count,),
        in_specs=[
            pl.BlockSpec((T, CB), lambda c: (0, c + at)),
            pl.BlockSpec((49, CB), lambda c: (0, c + at)),
            pl.BlockSpec((S, S, CB), lambda c: (0, 0, c + at)),
        ]
        + ([pl.BlockSpec(memory_space=pl.ANY)] if old is not None else []),
        out_specs=pl.BlockSpec((S, S, CB), lambda c: (0, 0, c + at)),
        out_shape=jax.ShapeDtypeStruct((S, S, C), BF16),
        scratch_shapes=[pltpu.VMEM((T + 2 * HEAD, CB), F32), pltpu.VMEM((T, CB), F32)],
        input_output_aliases={3: 0} if old is not None else {},
        compiler_params=params(63),
        cost_estimate=cost(T * C, T * C),
    )(d, k, cot, *([old] if old is not None else []))


PART = 7


def finish_kernel(x_ref, b0, b1, o_ref):
    for i in range(PART):
        at = slice(i * W, (i + 1) * W)
        t = b0[at, :].astype(F32) + b1[at, :].astype(F32)
        o_ref[i] = (x_ref[i].astype(F32) + t[:S, :C]).astype(BF16)


def finish(x, b0, b1):
    maps = pl.BlockSpec((PART, S, C), lambda r: (r, 0, 0))
    rows = pl.BlockSpec((PART * W, CP), lambda r: (r, 0))
    return pl.pallas_call(
        finish_kernel,
        name="finish",
        grid=(S // PART,),
        in_specs=[maps, rows, rows],
        out_specs=maps,
        out_shape=jax.ShapeDtypeStruct((S, S, C), BF16),
        compiler_params=params(63),
        cost_estimate=cost(T * C, T * C),
    )(x, b0, b1)


SHIFTS = (0, -1, 1, 2)
AXES = ("rep", "shard")


def place(x, y, z, c):
    return ((y * 2 + z % 2) * 2 + c) * 8 + x * 2 + z // 2


def moves(fn):
    pairs = []
    for x in range(4):
        for y in range(4):
            for z in range(4):
                for c in range(2):
                    nx, ny, nz, nc = fn(x, y, z, c)
                    pairs.append((place(x, y, z, c), place(nx % 4, ny % 4, nz % 4, nc)))
    return pairs


def along_x(d):
    return lambda x, y, z, c: (x + d, y, z, c)


def along_y(d):
    return lambda x, y, z, c: (x, y + d, z, c)


def minor(d):
    return lambda x, y, z, c: (x, y, z + d, c) if c == 0 else (x + d, y, z, c)


def major(d):
    return lambda x, y, z, c: (x + d, y, z, c) if c == 0 else (x, y, z + d, c)


def swap_core(x, y, z, c):
    return (x, y, z, 1 - c)


def swap_zlo(x, y, z, c):
    return (x, y, z + 1 - 2 * (z % 2), c)


def send(v, fn):
    return lax.ppermute(v, AXES, moves(fn))


def spread(v, axis_fn):
    return [v] + [send(v, axis_fn(-d)) for d in SHIFTS[1:]]


def turn(v, start):
    size = v.shape[0]
    return lax.dynamic_slice_in_dim(jnp.concatenate([v, v], axis=0), start, size, axis=0)


ORDER = (0, 3, 1, 2)
BACK = (0, 2, 3, 1)
SLOTS = (3, 1, 2, 0)


def add_up(parts):
    total = parts[0].astype(F32)
    for g in parts[1:]:
        total = total + g.astype(F32)
    return total


def after(v, *done):
    return lax.optimization_barrier((v,) + done)[0]


def shards(features, cotangent, dw_kernel, norm_gain, w_expand, grn_gamma, grn_beta, w_reduce):
    rep = lax.axis_index("rep")
    shard = lax.axis_index("shard")
    c = rep % 2
    zl = (rep // 2) % 2
    x = shard // 2
    z = (shard % 2) * 2 + zl
    hid = grn_gamma.shape[0]
    piece = hid // 32
    n = 4 * piece
    img = features[0]
    cot = cotangent[0]

    first = c * (2 * piece) + zl * piece
    own = jnp.concatenate([lax.dynamic_slice_in_dim(w, first, piece, axis=0) for w in (w_expand, w_reduce)], axis=1)
    filt = conv(img, dw_kernel, 0, 2)
    row = jnp.concatenate(spread(own, minor), axis=0)
    ws = spread(row, major)

    def to_own(v):
        v = lax.dynamic_index_in_dim(v.reshape(4, 2, 2, 2, piece), c, axis=2, keepdims=False).reshape(4, 4, piece)
        v = turn(v, x).transpose(1, 0, 2)
        v = turn(v, z)
        v = jnp.where(c == 0, v.transpose(1, 0, 2), v)
        v = jnp.stack([v[ORDER[k]] for k in SLOTS])
        v = jnp.stack([v[:, k] for k in ORDER], axis=1)
        return jnp.pad(v.reshape(1, 4, n), ((0, 0), (0, 0), (0, SLOT - n)))

    def to_all(v):
        v = v[:, :n].reshape(4, 4, piece)
        v = jnp.stack([v[SLOTS.index(k)] for k in BACK])
        v = jnp.stack([v[:, k] for k in BACK], axis=1)
        v = jnp.where(c == 0, v, v.transpose(1, 0, 2))
        v = turn(v, (4 - x) % 4).transpose(1, 0, 2)
        v = turn(v, (4 - z) % 4).transpose(1, 0, 2).reshape(4, 2, 1, 2, piece)
        zero = jnp.zeros_like(v)
        both = jnp.where(c == 0, jnp.concatenate([v, zero], axis=2), jnp.concatenate([zero, v], axis=2))
        return both.reshape(4, hid // 4)

    gamma = to_own(grn_gamma)
    beta = to_own(grn_beta)
    valid = (jnp.arange(SLOT) < n).astype(F32)

    c0 = widen(cot)
    c1 = send(c0, swap_core)
    rest = conv(after(img, row, c1), dw_kernel, 2, NCB - 2)
    n0, xhat, rstd = norm(filt, after(rest, ws[1], ws[2]), norm_gain)
    n1 = send(n0, swap_core)
    h0 = hidden(n0, n1, c0, c1, [row])
    h3 = hidden(after(n0, h0[3]), n1, c0, c1, [ws[3], ws[1], ws[2]])
    gamma3, beta3 = gamma.reshape(4, 1, SLOT), beta.reshape(4, 1, SLOT)
    mine = tally(h3[3], h0[3], gamma3, valid)
    vec_a, vec_b, back = vectors(h3[3], h0[3], gamma3, beta3, mine, send(mine, swap_core), hid)
    back_gamma = to_all(back[:, 0])
    back_beta = to_all(back[:, 1])
    t3, t1, *part = mix([(h3, 0)], n0, n1, c0, c1, ws[3], ws[1], vec_a, n, ())
    s3, s1 = send(t3, major(SHIFTS[3])), send(t1, major(SHIFTS[1]))
    t2, t0, br0, br1, bn0, bn1 = mix([(h3, 2), (h0, 0)], n0, n1, c0, c1, ws[2], ws[0], vec_b, n, part)
    bn1_in = send(after(bn1, s1, s3), swap_core)
    s2 = send(t2, major(SHIFTS[2]))
    br1_in = send(br1, swap_core)
    d, gain_rows = unnorm(bn0, bn1_in, xhat, rstd, norm_gain)
    taps_a = taps(img, d, 0)
    part = add_up([after(t0, taps_a), s1, s2, s3]).astype(BF16)
    part = [part[k * piece : (k + 1) * piece] for k in range(4)]
    part = [part[0]] + [send(part[k], minor(SHIFTS[k])) for k in (1, 2, 3)]
    taps_b = taps(after(img, part[0]), d, HALF)[:, : C - HALF * CB]
    part = add_up([after(part[0], taps_b)] + part[1:]).astype(BF16)
    grad_taps = jnp.concatenate([taps_a, taps_b], axis=1)
    small = jnp.concatenate([grad_taps, jnp.sum(gain_rows, axis=0, keepdims=True), back_gamma, back_beta], axis=0)
    small = jnp.pad(small, ((0, 6), (0, 0))).astype(BF16)
    merged = jnp.concatenate([part, jnp.concatenate([small[:32], small[32:]], axis=1)], axis=0)
    merged = [merged] + [send(merged, along_y(s)) for s in SHIFTS[1:]]
    inverse = 1.0 / (features.shape[0] * lax.axis_size("rep") * lax.axis_size("shard"))
    grad_features = unstem(after(d, merged[0]), dw_kernel, cot, None, 0, 3)
    block_out = finish(after(img, grad_features), br0, br1_in)
    merged = add_up([after(merged[0], block_out)] + merged[1:])
    total = (merged[:piece] * inverse).astype(BF16)
    small = merged[piece:].astype(BF16)
    other = send(total, swap_zlo)
    small = [small] + [send(small, minor(s)) for s in SHIFTS[1:]]
    grad_features = unstem(after(d, small[0], total), dw_kernel, cot, grad_features, 3, 1)
    total = after(total, grad_features)
    total = jnp.where(zl == 0, jnp.concatenate([total, other], axis=0), jnp.concatenate([other, total], axis=0))
    other = send(total, swap_core)
    small = add_up([after(small[0], grad_features)] + small[1:]).astype(BF16)
    small = [small] + [send(small, major(s)) for s in SHIFTS[1:]]
    grad_features = unstem(after(d, small[0], total), dw_kernel, cot, grad_features, 4, 2)
    small = add_up([after(small[0], grad_features)] + small[1:]).astype(BF16)
    far = send(small, swap_core)
    total = after(total, small)
    lo = jnp.where(c == 0, total, other)
    hi = jnp.where(c == 0, other, total)
    total = jnp.concatenate([lo, hi], axis=0).astype(F32)
    small = (after(small, total).astype(F32) + far.astype(F32)) * inverse
    small = jnp.concatenate([small[:, :C], small[:, C:]], axis=0)
    return (
        block_out[None],
        grad_features[None],
        small[:49],
        small[49],
        total[:, :C],
        small[50:54].reshape(hid),
        small[54:58].reshape(hid),
        total[:, C:],
    )


def solution(mesh):
    data = P(AXES, None, None, None)
    rows = P("shard", None)
    return jax.shard_map(
        shards,
        mesh=mesh,
        in_specs=(data, data, P(), P(), rows, P(), P(), rows),
        out_specs=(data, data, P(), P(), rows, P(), P(), rows),
        check_vma=False,
    )
```
